128 devices in a mesh: dp: 16 (over y_lo, x, core), tensor: 8 (over z, y_hi).
Axes of the slice: x: 4, y: 4 (y_hi: 2, y_lo: 2; y = y_hi * 2 + y_lo), z: 4, core: 2. Of those that a mesh axis runs over, the one named last changes fastest.
Arguments:
- x_in: bfloat16 [32768, 1536], P(('dp', 'tensor')), may hold values from -6 to 6
- cotangent: bfloat16 [32768, 1536], P(('dp', 'tensor')), may hold values from -6 to 6
- seq_lengths: int32 [16, 2], P('dp'), may hold values from 0 to 2048, as said below
- in_gain: float32 [1536], replicated, may hold values from 0.1 to 1.9
- w_z: bfloat16 [1536, 3072], P('dp', 'tensor'), may hold values from -0.15625 to 0.15625
- w_x: bfloat16 [1536, 3072], P('dp', 'tensor'), may hold values from -0.15625 to 0.15625
- w_dt: bfloat16 [1536, 48], P('dp', 'tensor'), may hold values from -0.15625 to 0.15625
- w_bc: bfloat16 [1536, 256], P('dp'), may hold values from -0.15625 to 0.15625
- conv_wx: float32 [4, 3072], P(None, 'tensor'), may hold values from -3 to 3
- conv_bx: float32 [3072], P('tensor'), may hold values from -3 to 3
- conv_wbc: float32 [4, 256], replicated, may hold values from -3 to 3
- conv_bbc: float32 [256], replicated, may hold values from -3 to 3
- dt_bias: float32 [48], P('tensor'), may hold values from -6 to -2
- a_log: float32 [48], P('tensor'), may hold values from 0 to 2.77
- d_skip: float32 [48], P('tensor'), may hold values from 0.5 to 1.5
- gnorm_gain: float32 [3072], P('tensor'), may hold values from 0.1 to 1.9
- w_out: bfloat16 [1536, 3072], P('dp', 'tensor'), may hold values from -0.109375 to 0.109375
Outputs:
- output: bfloat16 [32768, 1536], P(('dp', 'tensor'))
- x_grad: float32 [32768, 1536], P(('dp', 'tensor'))
- in_gain_grad: float32 [1536], P(('dp', 'tensor'))
- w_z_grad: float32 [1536, 3072], P('dp', 'tensor')
- w_x_grad: float32 [1536, 3072], P('dp', 'tensor')
- w_dt_grad: float32 [1536, 48], P('dp', 'tensor')
- w_bc_grad: float32 [1536, 256], P('dp')
- conv_wx_grad: float32 [4, 3072], P(None, 'tensor')
- conv_bx_grad: float32 [3072], P('tensor')
- conv_wbc_grad: float32 [4, 256], replicated
- conv_bbc_grad: float32 [256], replicated
- dt_bias_grad: float32 [48], P('tensor')
- a_log_grad: float32 [48], P('tensor')
- d_skip_grad: float32 [48], P('tensor')
- gnorm_gain_grad: float32 [3072], P('tensor')
- w_out_grad: float32 [1536, 3072], P('dp', 'tensor')
The draws below stay inside these ranges and needn't reach their ends.
Inputs may be any that keep to these rules, and one draw needn't show every extreme that they name: `seq_lengths`: row g lists the lengths of group g's sequences; a 0 is followed only by 0s, the first entry is positive, every positive length is 1024 or more, and the lengths rounded up to multiples of 256 sum to at most 2048. Some group holds one sequence of exactly 2048 tokens.
All inputs are finite; a program needn't handle non-finite values.
Results may differ from the reference program's by a relative error of at most 0.012.
Values may be sent and summed in bfloat16 or wider, within the bound.
No kernel may reach another device: no remote copies, remote signals or barrier semaphores. Data moves between devices by JAX's collectives and lax.ppermute only.
A program may use at most 192 MiB of HBM per device.

```python
import jax
import jax.numpy as jnp
from jax import lax

D = 1536
H = 48
NS = 128
KW = 4
CH = 256
DI = 3072
SEQ_MIN = 1024
GROUP = 2048
GROUPS = 16
TOKENS = 32768


def draw_seq_lengths(key, part):
    key = jax.random.fold_in(key, 11)
    keys = jax.random.split(key, 5)
    pad_least = (SEQ_MIN + CH - 1) // CH * CH
    single = jax.random.randint(keys[0], (GROUPS,), SEQ_MIN, GROUP + 1)
    fullest = jax.random.randint(keys[1], (), 0, GROUPS)
    if 2 * pad_least <= GROUP:
        paired = jax.random.randint(keys[2], (GROUPS,), 0, 2)
        first_two = jax.random.randint(keys[3], (GROUPS,), SEQ_MIN, pad_least + 1)
        second_two = jax.random.randint(keys[4], (GROUPS,), SEQ_MIN, GROUP - pad_least + 1)
        first_len = jnp.where(paired == 1, first_two, single)
        second_len = jnp.where(paired == 1, second_two, 0)
    else:
        first_len = single
        second_len = jnp.zeros((GROUPS,), jnp.int32)
    place = jnp.arange(GROUPS)
    first_len = jnp.where(place == fullest, GROUP, first_len)
    second_len = jnp.where(place == fullest, 0, second_len)
    return jnp.stack([first_len, second_len], axis=1).astype(jnp.int32)


def block_scale(key, extent, shards, least, largest):
    def one(dim, parts):
        steps = jax.random.uniform(jax.random.fold_in(jax.random.fold_in(key, 6), dim), (parts,), jnp.float32, least / len(shards), largest / len(shards))
        return jnp.repeat(jnp.exp(steps), extent[dim] // parts).reshape((-1,) + (1,) * (len(extent) - dim - 1))

    gain = one(*shards[0])
    for cut in shards[1:]:
        gain = gain * one(*cut)
    return gain


def noise(stream_key, dims, scale, most, cuts=(), kind=jnp.bfloat16):
    loudness = block_scale(stream_key, dims, cuts, -0.22, 0.18) if cuts else 1.0
    values = jax.random.normal(stream_key, dims, jnp.float32) * scale * loudness
    return jnp.minimum(jnp.maximum(values, -most), most).astype(kind)


def setup_inputs(seed: int = 0) -> dict:
    key_list = jax.random.split(jax.random.key(seed), 18)
    return {
        "x_in": noise(key_list[0], (TOKENS, D), 1.0, 6.0, ((0, 128),)),
        "cotangent": noise(key_list[1], (TOKENS, D), 1.0, 6.0, ((0, 128),)),
        "seq_lengths": draw_seq_lengths(jax.random.fold_in(key_list[17], 71), 0),
        "in_gain": jnp.clip(1.0 + 0.18 * jax.random.normal(key_list[3], (D,), jnp.float32), 0.1, 1.9),
        "w_z": noise(key_list[4], (D, DI), D ** -0.5, 0.15625, ((0, 16), (1, 8))),
        "w_x": noise(key_list[5], (D, DI), D ** -0.5, 0.15625, ((0, 16), (1, 8))),
        "w_dt": noise(key_list[6], (D, H), D ** -0.5, 0.15625, ((0, 16), (1, 8))),
        "w_bc": noise(key_list[7], (D, 2 * NS), D ** -0.5, 0.15625, ((0, 16),)),
        "conv_wx": noise(key_list[8], (KW, DI), 0.5, 3.0, ((1, 8),), jnp.float32),
        "conv_bx": noise(key_list[9], (DI,), 0.5, 3.0, ((0, 8),), jnp.float32),
        "conv_wbc": noise(key_list[10], (KW, 2 * NS), 0.5, 3.0, (), jnp.float32),
        "conv_bbc": noise(key_list[11], (2 * NS,), 0.5, 3.0, (), jnp.float32),
        "dt_bias": jnp.clip(-6.0 + 4.0 * jax.random.uniform(key_list[12], (H,), jnp.float32) ** block_scale(key_list[12], (H,), ((0, 8),), -0.2, 0.2), -6.0, -2.0),
        "a_log": jnp.clip(2.77 * jax.random.uniform(key_list[13], (H,), jnp.float32) ** block_scale(key_list[13], (H,), ((0, 8),), -0.2, 0.2), 0.0, 2.77),
        "d_skip": jnp.clip(0.5 + 1.0 * jax.random.uniform(key_list[14], (H,), jnp.float32) ** block_scale(key_list[14], (H,), ((0, 8),), -0.2, 0.2), 0.5, 1.5),
        "gnorm_gain": jnp.clip(1.0 + 0.18 * jax.random.normal(key_list[15], (DI,), jnp.float32), 0.1, 1.9),
        "w_out": noise(key_list[16], (D, DI), DI ** -0.5, 0.109375, ((0, 16), (1, 8))),
    }


EPS = 1e-05
HIGH = lax.Precision.HIGHEST

@jax.custom_vjp
def low(v):
    return lax.optimization_barrier(v.astype(jnp.bfloat16)).astype(jnp.float32)

@jax.custom_vjp
def low_back(v):
    return v

def low_keep(v):
    return (low(v), None)

def low_pass(kept, grad):
    return (grad,)

def back_keep(v):
    return (v, None)

def back_low(kept, grad):
    return (low(grad),)
low.defvjp(low_keep, low_pass)
low_back.defvjp(back_keep, back_low)

def exact_dot(left, right):
    return jnp.dot(left, right, precision=HIGH, preferred_element_type=jnp.float32)

def layout(lengths, group_len, stretch):
    lengths = lengths.astype(jnp.int32)
    stretch_count = (lengths + stretch - 1) // stretch
    padded_span = stretch_count * stretch
    offsets = jnp.cumsum(padded_span) - padded_span
    token_place = jnp.arange(group_len, dtype=jnp.int32)
    inside = (token_place[:, None] >= offsets[None, :]) & (token_place[:, None] < (offsets + padded_span)[None, :])
    position = lax.optimization_barrier(jnp.sum(jnp.where(inside, token_place[:, None] - offsets[None, :], 0), axis=1)).astype(jnp.int32)
    within = (token_place[:, None] >= offsets[None, :]) & (token_place[:, None] < (offsets + lengths)[None, :])
    live_mask = lax.optimization_barrier(jnp.sum(within.astype(jnp.float32), axis=1))
    keep_state = (position[::stretch] > 0).astype(jnp.float32)
    return (position, live_mask, keep_state)

def conv_silu(values, taps, offset, position):
    width = taps.shape[0]
    padded = jnp.pad(values, ((width - 1, 0), (0, 0)))
    running = offset + jnp.zeros_like(values)
    for j in range(width):
        shifted = padded[width - 1 - j:width - 1 - j + values.shape[0]]
        running = running + taps[width - 1 - j] * shifted * (position >= j)[:, None].astype(jnp.float32)
    return jax.nn.silu(running)

def state_space(inner, states, step_pre, dt_bias, a_log, d_skip, keep_state):
    group_len = inner.shape[0]
    heads = step_pre.shape[1]
    hsize = inner.shape[1] // heads
    nstate = states.shape[1] // 2
    count = group_len // CH
    step_size = jax.nn.softplus(step_pre + dt_bias)
    decay_rate = step_size * -jnp.exp(a_log)
    x_blocks = inner.reshape(count, CH, heads, hsize)
    b_blocks = states[:, :nstate].reshape(count, CH, nstate)
    c_blocks = states[:, nstate:].reshape(count, CH, nstate)
    s_blocks = step_size.reshape(count, CH, heads)
    r_blocks = decay_rate.reshape(count, CH, heads)
    lower = jnp.arange(CH)[:, None] >= jnp.arange(CH)[None, :]

    def advance(carried, pieces):
        xc, bc, cc, sc, rc, kc = pieces
        cumulate = jnp.cumsum(rc, axis=0)
        carried = carried * kc
        scores = exact_dot(cc, bc.T)
        diff = cumulate.T[:, :, None] - cumulate.T[:, None, :]
        decay_term = jnp.exp(jnp.where(lower[None], diff, -1e+30))
        mixing = scores[None] * decay_term * sc.T[:, None, :]
        diagonal = jnp.einsum('hij,jhp->ihp', mixing, xc, precision=HIGH)
        carried_part = jnp.einsum('in,hpn->ihp', cc, carried, precision=HIGH) * jnp.exp(cumulate)[:, :, None]
        weights = jnp.exp(cumulate[-1][None, :] - cumulate) * sc
        updated = carried * jnp.exp(cumulate[-1])[:, None, None] + jnp.einsum('jh,jn,jhp->hpn', weights, bc, xc, precision=HIGH)
        return (updated, diagonal + carried_part)
    start = jnp.zeros((heads, hsize, nstate), jnp.float32)
    _, blocks = lax.scan(jax.checkpoint(advance), start, (x_blocks, b_blocks, c_blocks, s_blocks, r_blocks, keep_state))
    return blocks.reshape(group_len, heads * hsize) + inner * jnp.repeat(d_skip, hsize)

def block_forward(resid, in_gain, w_z, w_x, w_dt, w_bc, conv_wx, conv_bx, conv_wbc, conv_bbc, dt_bias, a_log, d_skip, gnorm_gain, w_out, position, live_mask, keep_state):
    inverse = lax.rsqrt(lax.optimization_barrier(jnp.mean(resid * resid, axis=-1, keepdims=True)) + EPS)
    normed = low(resid * inverse * in_gain)
    gate = low_back(exact_dot(normed, w_z))
    inner_pre = low_back(exact_dot(normed, w_x))
    state_pre = low_back(exact_dot(normed, w_bc))
    step_pre = low_back(exact_dot(normed, w_dt))
    inner_act = low(conv_silu(inner_pre, conv_wx, conv_bx, position))
    state_act = low(conv_silu(state_pre, conv_wbc, conv_bbc, position))
    mixed = state_space(inner_act, state_act, step_pre, dt_bias, a_log, d_skip, keep_state)
    gated = mixed * jax.nn.silu(gate)
    scale = lax.rsqrt(lax.optimization_barrier(jnp.mean(gated * gated, axis=-1, keepdims=True)) + EPS)
    hidden = low(gated * scale * gnorm_gain)
    branch = low_back(exact_dot(hidden, w_out.T))
    return resid + live_mask[:, None] * branch

def widen(value):
    return value.astype(jnp.float32)

def reference(x_in, cotangent, seq_lengths, in_gain, w_z, w_x, w_dt, w_bc, conv_wx, conv_bx, conv_wbc, conv_bbc, dt_bias, a_log, d_skip, gnorm_gain, w_out):
    params = (in_gain, widen(w_z), widen(w_x), widen(w_dt), widen(w_bc), conv_wx, conv_bx, conv_wbc, conv_bbc, dt_bias, a_log, d_skip, gnorm_gain, widen(w_out))
    groups = seq_lengths.shape[0]
    x_groups = x_in.reshape(groups, GROUP, x_in.shape[1])
    c_groups = cotangent.reshape(groups, GROUP, x_in.shape[1])

    def visit(running, item):
        resid, cot, lengths = item
        position, live_mask, keep_state = layout(lengths, GROUP, CH)

        def forward(value, *weights):
            return block_forward(value, *weights, position, live_mask, keep_state)
        result, pullback = jax.vjp(forward, widen(resid), *params)
        grads = pullback(widen(cot))
        running = jax.tree.map(jnp.add, running, tuple(grads[1:]))
        return (running, (result.astype(jnp.bfloat16), grads[0]))
    zeros = tuple((jnp.zeros_like(value) for value in params))
    sums, (results, input_grads) = lax.scan(visit, zeros, (x_groups, c_groups, seq_lengths))
    return (results.reshape(x_in.shape), input_grads.reshape(x_in.shape).astype(jnp.float32), sums[0], sums[1], sums[2], sums[3], sums[4], sums[5], sums[6], sums[7], sums[8], sums[9], sums[10], sums[11], sums[12], sums[13])
```

```python
import functools

import jax
import jax.numpy as jnp
from jax import lax
from jax.experimental import pallas as pl
from jax.experimental.pallas import tpu as pltpu
from jax.sharding import PartitionSpec as P

Q = 256
HD = 64
NS = 128
EPS = 1e-05
F32 = jnp.float32
BF = jnp.bfloat16
VMEM_LIMIT = 56 * 1024 * 1024


def mm(a, b):
    return lax.dot_general(a, b, (((1,), (0,)), ((), ())), preferred_element_type=F32)


def mm_nt(a, b):
    return lax.dot_general(a, b, (((1,), (1,)), ((), ())), preferred_element_type=F32)


def mm_tn(a, b):
    return lax.dot_general(a, b, (((0,), (0,)), ((), ())), preferred_element_type=F32)


def split3(v):
    hi = v.astype(BF)
    rest = v - hi.astype(F32)
    mid = rest.astype(BF)
    low = (rest - mid.astype(F32)).astype(BF)
    return hi, mid, low


def split2(v):
    hi = v.astype(BF)
    return hi, (v - hi.astype(F32)).astype(BF)


def lanes(shape):
    return lax.broadcasted_iota(jnp.int32, shape, len(shape) - 1)


def lower_ones():
    rows = lax.broadcasted_iota(jnp.int32, (Q, Q), 0)
    return rows >= lanes((Q, Q))


def expander(heads):
    row = lax.broadcasted_iota(jnp.int32, (128, heads * HD), 0)
    head = lanes((128, heads * HD)) // HD
    return ((row == head) | (row == head + 8)).astype(BF)


def spread(v, ones):
    hi, low = split2(v)
    first = lanes(v.shape) < 8
    return mm(jnp.where(first, hi.astype(F32), low.astype(F32)).astype(BF), ones)


def gather_heads(v, ones):
    hi, low = split2(v)
    return mm_nt(hi, ones) + mm_nt(low, ones)


def softplus(z):
    return jnp.maximum(z, 0.0) + jnp.log1p(jnp.exp(-jnp.abs(z)))


def sigmoid(v):
    return 1.0 / (1.0 + jnp.exp(-v))


def running_sum(tri, v):
    hi, mid, low = split3(v)
    return mm(tri, hi) + mm(tri, mid) + mm(tri, low)


def suffix_sum(tri, v):
    hi, mid, low = split3(v)
    return mm_tn(tri, hi) + mm_tn(tri, mid) + mm_tn(tri, low)


def forward_kernel(
    keep_ref, tok_ref, w_ref, conv_ref, head_ref, chan_ref, ones_ref, tri_ref,
    gate_ref, pre_ref, act_ref, z_ref, cum_ref, mixed_ref, sin_ref,
    state, tail, buf, *, heads,
):
    c = pl.program_id(0)
    width = heads * HD
    conv = width + 2 * NS

    @pl.when(c == 0)
    def _():
        state[...] = jnp.zeros_like(state)
        tail[...] = jnp.zeros_like(tail)

    keep = keep_ref[c].astype(F32)
    proj = mm(tok_ref[...], w_ref[...])
    gate_ref[...] = proj[:, :width]
    pre = proj[:, width : width + conv]
    pre_ref[...] = pre
    buf[0:8, :] = tail[...] * keep
    buf[8 : 8 + Q, :] = pre
    tail[...] = pre[Q - 8 :, :]
    run = conv_ref[4:5, :] + conv_ref[3:4, :] * pre
    for j in range(1, 4):
        run = run + conv_ref[3 - j : 4 - j, :] * buf[8 - j : 8 - j + Q, :]
    act = (run * sigmoid(run)).astype(BF)
    act_ref[...] = act
    z = proj[:, width + conv :] + head_ref[0:1, :]
    z_ref[...] = z
    step = softplus(z)
    tri = tri_ref[...]
    cum = running_sum(tri, step * head_ref[1:2, :])
    cum_ref[...] = cum
    ones = ones_ref[...]
    step_x = spread(step, ones)
    grow_x = spread(jnp.exp(cum), ones)
    fade_x = spread(jnp.exp(cum[Q - 1 :, :] - cum), ones)
    x = act[:, :width].astype(F32)
    xs = x * step_x
    bmat = act[:, width : width + NS]
    cmat = act[:, width + NS :]
    scores = mm_nt(cmat, bmat)
    cum_row = cum.T
    lower = lower_ones()
    half = lanes((Q, 128)) < HD
    carried = state[...] * keep
    sin_ref[...] = carried
    through = mm(cmat, carried.astype(BF)) * grow_x
    for p in range(heads // 2):
        span = slice(128 * p, 128 * (p + 1))
        xp = xs[:, span]
        total = through[:, span] + chan_ref[0:1, span] * x[:, span]
        for k in range(2):
            h = 2 * p + k
            diff = cum[:, h : h + 1] - cum_row[h : h + 1, :]
            decay = jnp.exp(jnp.where(lower, diff, -1e30))
            mix = (scores * decay).astype(BF)
            mine = half if k == 0 else ~half
            total = total + mm(mix, jnp.where(mine, xp, 0.0).astype(BF))
        mixed_ref[:, span] = total
    state[...] = carried * grow_x[Q - 1 :, :] + mm_tn(bmat, (xs * fade_x).astype(BF))


def forward(keep, tokens, weights, conv, head, chan, ones, tri, heads):
    rows, d = tokens.shape
    n = rows // Q
    width = heads * HD
    cols = width + 2 * NS
    block = lambda w: pl.BlockSpec((Q, w), lambda c, keep: (c, 0))
    whole = lambda a: pl.BlockSpec(a.shape, lambda c, keep: (0,) * a.ndim)
    out = lambda w, dt: jax.ShapeDtypeStruct((rows, w), dt)
    return pl.pallas_call(
        functools.partial(forward_kernel, heads=heads),
        grid_spec=pltpu.PrefetchScalarGridSpec(
            num_scalar_prefetch=1,
            grid=(n,),
            in_specs=[
                block(d),
                pl.BlockSpec((d, width + cols + 128), lambda c, keep: (0, 0)),
                whole(conv), whole(head), whole(chan), whole(ones), whole(tri),
            ],
            out_specs=[
                block(width), block(cols), block(cols), block(128), block(128), block(width),
                pl.BlockSpec((NS, width), lambda c, keep: (c, 0)),
            ],
            scratch_shapes=[
                pltpu.VMEM((NS, width), F32),
                pltpu.VMEM((8, cols), F32),
                pltpu.VMEM((8 + Q, cols), F32),
            ],
        ),
        out_shape=[
            out(width, F32), out(cols, F32), out(cols, BF), out(128, F32), out(128, F32), out(width, F32),
            jax.ShapeDtypeStruct((n * NS, width), F32),
        ],
        compiler_params=pltpu.CompilerParams(
            dimension_semantics=("arbitrary",), vmem_limit_bytes=VMEM_LIMIT
        ),
        cost_estimate=pl.CostEstimate(flops=12 * 10**9, bytes_accessed=30 * 10**6, transcendentals=5 * 10**6),
        name="ssd_forward",
    )(keep, tokens, weights, conv, head, chan, ones, tri)


def grad_sums_kernel(live_ref, cot_ref, w_ref, mixed_ref, gate_ref, chan_ref, hg_ref, sums_ref):
    c = pl.program_id(0)
    width = mixed_ref.shape[1]
    row = lax.broadcasted_iota(jnp.int32, (Q, width), 0)
    hg = jnp.where(row < live_ref[c], mm(cot_ref[...], w_ref[...]), 0.0)
    hg_ref[...] = hg
    gate = gate_ref[...]
    gated = mixed_ref[...] * (gate * sigmoid(gate))
    one = jnp.ones((8, width), BF)
    square = sum(mm_nt(one, part) for part in split2(gated * gated))
    inner = sum(mm_nt(one, part) for part in split2(hg * chan_ref[1:2, :] * gated))
    first = lax.broadcasted_iota(jnp.int32, (8, Q), 0) == 0
    sums_ref[...] = jnp.where(first, square, inner)


def grad_sums(live, cot, weights, mixed, gate, chan, first_col):
    rows, d = cot.shape
    width = mixed.shape[1]
    block = lambda w: pl.BlockSpec((Q, w), lambda c, live: (c, 0))
    return pl.pallas_call(
        grad_sums_kernel,
        grid_spec=pltpu.PrefetchScalarGridSpec(
            num_scalar_prefetch=1,
            grid=(rows // Q,),
            in_specs=[
                block(d),
                pl.BlockSpec((d, width), lambda c, live: (0, first_col // width)),
                block(width), block(width),
                pl.BlockSpec(chan.shape, lambda c, live: (0, 0)),
            ],
            out_specs=[block(width), pl.BlockSpec((8, Q), lambda c, live: (0, c))],
        ),
        out_shape=[jax.ShapeDtypeStruct((rows, width), F32), jax.ShapeDtypeStruct((8, rows), F32)],
        compiler_params=pltpu.CompilerParams(
            dimension_semantics=("arbitrary",), vmem_limit_bytes=VMEM_LIMIT
        ),
        cost_estimate=pl.CostEstimate(flops=2 * rows * d * width, bytes_accessed=17 * 10**6, transcendentals=10**6),
        name="grad_sums",
    )(live, cot, weights, mixed, gate, chan)


def gate_back_kernel(live_ref, hg_ref, mixed_ref, gate_ref, sums_ref, chan_ref, hidden_ref, glow_ref, dy_ref, ngg_ref, *, inner):
    c = pl.program_id(0)
    width = mixed_ref.shape[1]

    @pl.when(c == 0)
    def _():
        ngg_ref[...] = jnp.zeros_like(ngg_ref)

    sums = sums_ref[...]
    scale_row = lax.rsqrt(sums[0:1, :] / inner + EPS)
    pull_row = scale_row * scale_row * scale_row * (sums[1:2, :] / inner)
    sub = lax.broadcasted_iota(jnp.int32, (128, Q), 0)
    cols = jnp.where(sub == 0, scale_row, jnp.where(sub == 1, pull_row, 0.0)).T
    scale = cols[:, 0:1]
    pull = cols[:, 1:2]
    hg = hg_ref[...]
    mixed = mixed_ref[...]
    gate = gate_ref[...]
    sg = sigmoid(gate)
    silu = gate * sg
    gated = mixed * silu
    normal = gated * scale
    gain = chan_ref[1:2, :]
    row = lax.broadcasted_iota(jnp.int32, (Q, width), 0)
    hidden_ref[...] = jnp.where(row < live_ref[c], normal * gain, 0.0).astype(BF)
    ngg_ref[0:1, :] += jnp.sum(hg * normal, axis=0, keepdims=True)
    gg = scale * gain * hg - gated * pull
    dy_ref[...] = gg * silu
    glow_ref[...] = (gg * mixed * sg * (1.0 + gate * (1.0 - sg))).astype(BF)


def gate_back(live, hg, mixed, gate, sums, chan, inner):
    rows, width = hg.shape
    block = lambda w: pl.BlockSpec((Q, w), lambda c, live: (c, 0))
    return pl.pallas_call(
        functools.partial(gate_back_kernel, inner=inner),
        grid_spec=pltpu.PrefetchScalarGridSpec(
            num_scalar_prefetch=1,
            grid=(rows // Q,),
            in_specs=[
                block(width), block(width), block(width),
                pl.BlockSpec((8, Q), lambda c, live: (0, c)),
                pl.BlockSpec(chan.shape, lambda c, live: (0, 0)),
            ],
            out_specs=[block(width), block(width), block(width), pl.BlockSpec((8, width), lambda c, live: (0, 0))],
        ),
        out_shape=[
            jax.ShapeDtypeStruct((rows, width), BF), jax.ShapeDtypeStruct((rows, width), BF),
            jax.ShapeDtypeStruct((rows, width), F32), jax.ShapeDtypeStruct((8, width), F32),
        ],
        compiler_params=pltpu.CompilerParams(
            dimension_semantics=("arbitrary",), vmem_limit_bytes=VMEM_LIMIT
        ),
        cost_estimate=pl.CostEstimate(flops=20 * rows * width, bytes_accessed=16 * 10**6, transcendentals=10**6),
        name="gate_back",
    )(live, hg, mixed, gate, sums, chan)


def backward_kernel(
    keep_ref, act_ref, pre_ref, before_ref, z_ref, cum_ref, sin_ref, dy_ref, conv_ref, head_ref, chan_ref, ones_ref, tri_ref,
    low_ref, convsum_ref, headsum_ref, skipsum_ref,
    dstate, halo, buf, *, heads, count,
):
    c = count - 1 - pl.program_id(0)
    width = heads * HD

    @pl.when(pl.program_id(0) == 0)
    def _():
        dstate[...] = jnp.zeros_like(dstate)
        halo[...] = jnp.zeros_like(halo)
        convsum_ref[...] = jnp.zeros_like(convsum_ref)
        headsum_ref[...] = jnp.zeros_like(headsum_ref)
        skipsum_ref[...] = jnp.zeros_like(skipsum_ref)

    keep = keep_ref[c].astype(F32)
    keep_next = keep_ref[c + 1].astype(F32)
    act = act_ref[...]
    x = act[:, :width].astype(F32)
    bmat = act[:, width : width + NS]
    cmat = act[:, width + NS :]
    z = z_ref[...]
    step = softplus(z)
    cum = cum_ref[...]
    ones = ones_ref[...]
    tri = tri_ref[...]
    step_x = spread(step, ones)
    grow_x = spread(jnp.exp(cum), ones)
    fade_x = spread(jnp.exp(cum[Q - 1 :, :] - cum), ones)
    xs = x * step_x
    xsb = xs.astype(BF)
    dy = dy_ref[...]
    scores = mm_nt(cmat, bmat)
    cum_row = cum.T
    lower = lower_ones()
    lane = lanes((Q, 128))
    half = lane < HD
    sub = lax.broadcasted_iota(jnp.int32, (128, Q), 0)
    dscores = jnp.zeros((Q, Q), F32)
    rowsum = jnp.zeros((Q, 128), F32)
    colsum = jnp.zeros((128, Q), F32)
    parts = []
    for p in range(heads // 2):
        span = slice(128 * p, 128 * (p + 1))
        dyp = dy[:, span]
        part = jnp.zeros((Q, 128), F32)
        for k in range(2):
            h = 2 * p + k
            diff = cum[:, h : h + 1] - cum_row[h : h + 1, :]
            decay = jnp.exp(jnp.where(lower, diff, -1e30))
            mix = (scores * decay).astype(BF)
            mine = half if k == 0 else ~half
            dym = jnp.where(mine, dyp, 0.0).astype(BF)
            grad = mm_nt(dym, xsb[:, span]) * decay
            dscores = dscores + grad
            grad = grad * scores
            rowsum = jnp.where(lane == h, jnp.sum(grad, axis=1, keepdims=True), rowsum)
            colsum = jnp.where(sub == h, jnp.sum(grad, axis=0, keepdims=True), colsum)
            part = part + mm_tn(mix, dym)
        parts.append(part)
    within = jnp.concatenate(parts, axis=1)
    carried = sin_ref[...]
    carried_low = carried.astype(BF)
    dstate_now = dstate[...]
    dstate_low = dstate_now.astype(BF)
    dyg = (dy * grow_x).astype(BF)
    dsl = dscores.astype(BF)
    dc = mm(dsl, bmat) + mm_nt(dyg, carried_low)
    xsf = (xs * fade_x).astype(BF)
    db = mm_tn(dsl, cmat) + mm_nt(xsf, dstate_low)
    through = mm(cmat, carried_low) * grow_x
    later = mm(bmat, dstate_low) * fade_x
    last_x = grow_x[Q - 1 :, :]
    q_through = gather_heads(dy * through, ones)
    q_later = gather_heads(x * later, ones)
    q_within = gather_heads(x * within, ones)
    hold = jnp.sum(dstate_now * carried, axis=0, keepdims=True) * last_x
    q_hold = gather_heads(jnp.broadcast_to(hold, (8, width)), ones)[0:1, :]
    dstate[...] = (mm_tn(cmat, dyg) + last_x * dstate_now) * keep
    dxs = within + later
    dx = step_x * dxs + chan_ref[0:1, :] * dy
    first = lane < 8
    net = jnp.where(first, q_through + rowsum - colsum.T, 0.0)
    push = step * q_later
    drate = suffix_sum(tri, net) + running_sum(tri, push) - push + q_hold
    rate_of = head_ref[1:2, :]
    dstep = q_within + q_later + drate * rate_of
    dz = jnp.where(lane < heads, dstep * sigmoid(z), 0.0)
    headsum_ref[0:1, :] += jnp.sum(dz, axis=0, keepdims=True)
    headsum_ref[1:2, :] += jnp.sum(drate * step * rate_of, axis=0, keepdims=True)
    skipsum_ref[0:1, :] += jnp.sum(dy * x, axis=0, keepdims=True)

    grad = jnp.concatenate([dx, db, dc], axis=1)
    buf[0:8, :] = before_ref[...] * keep
    buf[8 : 8 + Q, :] = pre_ref[...]
    run = conv_ref[4:5, :] + conv_ref[3:4, :] * buf[8 : 8 + Q, :]
    for j in range(1, 4):
        run = run + conv_ref[3 - j : 4 - j, :] * buf[8 - j : 8 - j + Q, :]
    sg = sigmoid(run)
    dact = grad * (sg * (1.0 + run * (1.0 - sg)))
    for j in range(4):
        convsum_ref[3 - j : 4 - j, :] += jnp.sum(dact * buf[8 - j : 8 - j + Q, :], axis=0, keepdims=True)
    convsum_ref[4:5, :] += jnp.sum(dact, axis=0, keepdims=True)
    buf[0:Q, :] = dact
    buf[Q : Q + 8, :] = halo[...] * keep_next
    halo[...] = dact[0:8, :]
    dpre = conv_ref[3:4, :] * dact
    for j in range(1, 4):
        dpre = dpre + conv_ref[3 - j : 4 - j, :] * buf[j : j + Q, :]
    low_ref[:, : width + 2 * NS] = dpre.astype(BF)
    low_ref[:, width + 2 * NS :] = dz.astype(BF)


def backward(keep, act, pre, z, cum, sin, dy, conv, head, chan, ones, tri, heads):
    rows, cols = act.shape
    n = rows // Q
    width = heads * HD
    at = lambda i: n - 1 - i
    block = lambda w: pl.BlockSpec((Q, w), lambda i, keep: (at(i), 0))
    whole = lambda a: pl.BlockSpec(a.shape, lambda i, keep: (0,) * a.ndim)
    still = lambda w: pl.BlockSpec((8, w), lambda i, keep: (0, 0))
    return pl.pallas_call(
        functools.partial(backward_kernel, heads=heads, count=n),
        grid_spec=pltpu.PrefetchScalarGridSpec(
            num_scalar_prefetch=1,
            grid=(n,),
            in_specs=[
                block(cols), block(cols),
                pl.BlockSpec((8, cols), lambda i, keep: (jnp.maximum(at(i) * (Q // 8) - 1, 0), 0)),
                block(128), block(128),
                pl.BlockSpec((NS, width), lambda i, keep: (at(i), 0)),
                block(width),
                whole(conv), whole(head), whole(chan), whole(ones), whole(tri),
            ],
            out_specs=[block(cols + 128), still(cols), still(128), still(width)],
            scratch_shapes=[
                pltpu.VMEM((NS, width), F32),
                pltpu.VMEM((8, cols), F32),
                pltpu.VMEM((8 + Q, cols), F32),
            ],
        ),
        out_shape=[
            jax.ShapeDtypeStruct((rows, cols + 128), BF),
            jax.ShapeDtypeStruct((8, cols), F32), jax.ShapeDtypeStruct((8, 128), F32), jax.ShapeDtypeStruct((8, width), F32),
        ],
        compiler_params=pltpu.CompilerParams(
            dimension_semantics=("arbitrary",), vmem_limit_bytes=VMEM_LIMIT
        ),
        cost_estimate=pl.CostEstimate(flops=30 * 10**9, bytes_accessed=25 * 10**6, transcendentals=6 * 10**6),
        name="ssd_backward",
    )(keep, act, pre, pre, z, cum, sin, dy, conv, head, chan, ones, tri)


def ring_maps(size, step):
    places = size // 2
    return [(t, ((t // 2 + step) % places) * 2 + t % 2) for t in range(size)]


ZR, ZL = ring_maps(8, 1), ring_maps(8, -1)
YS = [(t, t ^ 1) for t in range(8)]
ZN, ZF = [(t, t ^ 2) for t in range(8)], [(t, t ^ 4) for t in range(8)]
XR = [(d, d // 8 * 8 + (d % 8 // 2 + 1) % 4 * 2 + d % 2) for d in range(16)]
XL = [(d, d // 8 * 8 + (d % 8 // 2 + 3) % 4 * 2 + d % 2) for d in range(16)]
CS = [(d, d ^ 1) for d in range(16)]
XN, XF = [(d, d ^ 2) for d in range(16)], [(d, d ^ 4) for d in range(16)]
YL = [(d, d ^ 8) for d in range(16)]
FRONT = 160


def pick(array, index, axis):
    return lax.dynamic_index_in_dim(array, index, axis, keepdims=False)


def gather_tensor(x):
    t = lax.axis_index("tensor")
    z, y = t // 2, t % 2
    send = lambda v, to: lax.ppermute(v, "tensor", to)
    a, b = x[:FRONT], x[FRONT:]
    nb = b.shape[0] // 2
    out = jnp.zeros((8 * Q, x.shape[1]), x.dtype)

    def put(out, piece, dz, dy, row):
        at = (((z + dz) % 4) * 2 + (y + dy) % 2) * Q + row
        return lax.dynamic_update_slice_in_dim(out, piece, at, 0)

    b_right, b_left = send(b, ZR), send(b, ZL)
    a_y = send(a, YS)
    out = put(out, x, 0, 0, 0)
    b_far = jnp.concatenate([send(b_right[:nb], ZR), send(b_left[nb:], ZL)])
    a_right, a_left = send(a, ZR), send(a, ZL)
    ay_right, ay_left = send(a_y, ZR), send(a_y, ZL)
    far = send(a_right, ZR), send(ay_left, ZL)
    by = send(jnp.concatenate([b, b_right, b_left]), YS)
    by_far = send(b_far, YS)
    size = b.shape[0]
    out = put(out, a_y, 0, 1, 0)
    out = put(out, by[:size], 0, 1, FRONT)
    out = put(out, jnp.concatenate([a_right, b_right]), -1, 0, 0)
    out = put(out, jnp.concatenate([a_left, b_left]), 1, 0, 0)
    out = put(out, jnp.concatenate([ay_right, by[size : 2 * size]]), -1, 1, 0)
    out = put(out, jnp.concatenate([ay_left, by[2 * size :]]), 1, 1, 0)
    out = put(out, jnp.concatenate([far[0], b_far]), 2, 0, 0)
    out = put(out, jnp.concatenate([far[1], by_far]), 2, 1, 0)
    return out


def ring_sum(block, right, left, send):
    up = lambda v: v.astype(F32)
    far = block(2)
    from_left, from_right = send(far[0], right), send(far[1], left)
    ahead, behind = block(1), block(3)
    ahead = jnp.stack([(up(ahead[0]) + up(from_left)).astype(BF), ahead[1]])
    behind = jnp.stack([behind[0], (up(behind[1]) + up(from_right)).astype(BF)])
    return up(block(0)) + up(send(ahead, right)) + up(send(behind, left))


def scatter_tensor(part):
    t = lax.axis_index("tensor")
    z, y = t // 2, t % 2
    d = part.shape[1]
    send = lambda v, to: lax.ppermute(v, "tensor", to)
    stack = part.reshape(4, 2, Q, d)
    front, back = stack[:, :, :FRONT], stack[:, :, FRONT:]
    other = pick(back, 1 - y, 1)
    back = (pick(back, y, 1).astype(F32) + send(other, YS).astype(F32)).astype(BF)
    back = back.reshape(4, 2, (Q - FRONT) // 2, d)
    front = ring_sum(lambda k: pick(front, (z + k) % 4, 0), ZR, ZL, send)
    back = ring_sum(lambda k: pick(back, (z + k) % 4, 0), ZR, ZL, send)
    front = pick(front, y, 0) + send(pick(front, 1 - y, 0).astype(BF), YS).astype(F32)
    return jnp.concatenate([front, back.reshape(Q - FRONT, d)])


def scatter_dp(part):
    i = lax.axis_index("dp")
    yl, x, core = i // 8, i % 8 // 2, i % 2
    send = lambda v, to: lax.ppermute(v, "dp", to)
    rows, cols = part.shape
    stack = part.reshape(2, 4, 2, rows // 16, cols)
    both = (pick(stack, core, 2).astype(F32) + send(pick(stack, 1 - core, 2), CS).astype(F32)).astype(BF)
    own = ring_sum(lambda k: pick(both, (x + k) % 4, 1), XR, XL, send)
    return pick(own, yl, 0) + send(pick(own, 1 - yl, 0).astype(BF), YL).astype(F32)


def total(value, axis, maps):
    for to in maps:
        value = value + lax.ppermute(value, axis, to)
    return value


def local(
    x_in,
    cotangent,
    seq_lengths,
    in_gain,
    w_z,
    w_x,
    w_dt,
    w_bc,
    conv_wx,
    conv_bx,
    conv_wbc,
    conv_bbc,
    dt_bias,
    a_log,
    d_skip,
    gnorm_gain,
    w_out,
):
    rows, d = x_in.shape
    heads = dt_bias.shape[0]
    width = heads * HD
    cols = width + 2 * NS
    inner = width * 8
    own = w_z.shape[0]
    t = lax.axis_index("tensor")
    dp = lax.axis_index("dp")

    lengths = seq_lengths[0]
    spans = (lengths + Q - 1) // Q * Q
    starts = jnp.cumsum(spans) - spans
    place = jnp.arange(9, dtype=jnp.int32)[:, None] * Q
    inside = (place >= starts) & (place < starts + spans)
    keep = jnp.sum((inside & (place > starts)).astype(jnp.int32), axis=1)
    live = jnp.sum(jnp.where(inside, jnp.clip(starts + lengths - place, 0, Q), 0), axis=1)

    resid = x_in.astype(F32)
    inverse = lax.rsqrt(jnp.mean(resid * resid, axis=-1, keepdims=True) + EPS)
    normed = (resid * inverse * in_gain).astype(BF)
    tokens = gather_tensor(normed)

    blank = lambda k: jnp.zeros((own, k), BF)
    dt_cols = jnp.concatenate([w_dt, blank(8 - heads), w_dt, blank(120 - heads)], axis=1)
    own_in = jnp.concatenate([w_z, w_x, w_bc, dt_cols], axis=1)
    weights = lax.all_gather(jnp.concatenate([own_in, w_out], axis=1), "dp", axis=0, tiled=True)
    split = own_in.shape[1]

    def pad_rows(*values):
        stack = jnp.concatenate([v.reshape(-1, v.shape[-1]) for v in values])
        return jnp.pad(stack, ((0, 8 - stack.shape[0]), (0, 0)))

    def per_head(v):
        gap = jnp.zeros((8 - heads,), F32)
        return jnp.concatenate([v, gap, v, gap, jnp.zeros((112,), F32)])

    conv = pad_rows(jnp.concatenate([conv_wx, conv_wbc], axis=1), jnp.concatenate([conv_bx, conv_bbc]))
    head = pad_rows(per_head(dt_bias), per_head(-jnp.exp(a_log)))
    chan = pad_rows(jnp.repeat(d_skip, HD), gnorm_gain)
    ones = expander(heads)
    tri = lower_ones().astype(BF)

    gate, pre, act, z, cum, mixed, sin = forward(keep, tokens, weights, conv, head, chan, ones, tri, heads)
    late, _ = lax.optimization_barrier((cotangent, tokens[:8]))
    cot_all = gather_tensor(late)
    hg, sums = grad_sums(live, cot_all, weights, mixed, gate, chan, split)
    sums = total(sums, "tensor", (YS, ZN, ZF))
    hidden, gate_low, dy, gain_sum = gate_back(live, hg, mixed, gate, sums, chan, inner)
    full_in, full_out = weights[:, :split], weights[:, split:]
    branch = scatter_tensor(mm_nt(hidden, full_out).astype(BF))
    own_live = pick(live, t, 0)
    live_rows = jnp.arange(rows, dtype=jnp.int32)[:, None] < own_live
    output = (resid + jnp.where(live_rows, branch, 0.0)).astype(BF)

    early = jnp.concatenate([mm_tn(tokens, gate_low).astype(BF), mm_tn(cot_all, hidden).astype(BF)], axis=1)
    early = scatter_dp(early)
    low, conv_sum, head_sum, skip_sum = backward(
        keep, act, pre, z, cum, sin, dy, conv, head, chan, ones, tri, heads
    )
    lows = jnp.concatenate([gate_low, low], axis=1)
    normed_grad = scatter_tensor(mm_nt(lows, full_in).astype(BF))
    late_sums = scatter_dp(mm_tn(tokens, low).astype(BF))

    projected = jnp.sum(normed_grad * in_gain * resid, axis=-1, keepdims=True) / d
    x_grad = inverse * in_gain * normed_grad - resid * inverse**3 * projected + cotangent.astype(F32)

    w_z_grad, w_out_grad = early[:, :width], early[:, width:]
    w_x_grad, bc_part, dt_part = late_sums[:, :width], late_sums[:, width:cols], late_sums[:, cols:]
    dots = (
        jnp.sum(w_z.astype(F32) * w_z_grad, axis=1)
        + jnp.sum(w_x.astype(F32) * w_x_grad, axis=1)
        + jnp.sum(w_dt.astype(F32) * dt_part[:, :heads], axis=1)
    )
    pack = jnp.concatenate([bc_part, jnp.broadcast_to(dots[:, None], (own, 128))], axis=1)
    pack = total(pack, "tensor", (YS, ZN, ZF))
    w_bc_grad = pack[:, : 2 * NS]
    dots = pack[:, 2 * NS] + jnp.sum(w_bc.astype(F32) * w_bc_grad, axis=1)
    each = own // 8
    gain = lax.dynamic_slice_in_dim(in_gain, dp * own + t * each, each, 0)
    in_gain_grad = lax.dynamic_slice_in_dim(dots, t * each, each, 0) / gain

    small = jnp.concatenate(
        [
            conv_sum[:5],
            jnp.concatenate([gain_sum[:1], head_sum[:1], head_sum[1:2]], axis=1),
            jnp.pad(skip_sum[:1], ((0, 0), (0, 2 * NS))),
            jnp.zeros((1, cols), F32),
        ]
    )
    small = total(small, "dp", (CS, XN, XF, YL))
    bc_small = total(small[:, width:], "tensor", (YS, ZN, ZF))
    return (
        output,
        x_grad,
        in_gain_grad,
        w_z_grad,
        w_x_grad,
        dt_part[:, :heads],
        w_bc_grad,
        small[:4, :width],
        small[4, :width],
        bc_small[:4],
        bc_small[4],
        small[5, width : width + heads],
        small[5, width + 128 : width + 128 + heads],
        jnp.sum(small[6, :width].reshape(heads, HD), axis=1),
        small[5, :width],
        w_out_grad,
    )


def solution(mesh):
    placed = (
        P(("dp", "tensor"), None),
        P(("dp", "tensor"), None),
        P("dp", None),
        P(),
        P("dp", "tensor"),
        P("dp", "tensor"),
        P("dp", "tensor"),
        P("dp", None),
        P(None, "tensor"),
        P("tensor"),
        P(),
        P(),
        P("tensor"),
        P("tensor"),
        P("tensor"),
        P("tensor"),
        P("dp", "tensor"),
    )
    return jax.shard_map(
        local,
        mesh=mesh,
        in_specs=placed,
        out_specs=(
            P(("dp", "tensor"), None),
            P(("dp", "tensor"), None),
            P(("dp", "tensor")),
            P("dp", "tensor"),
            P("dp", "tensor"),
            P("dp", "tensor"),
            P("dp", None),
            P(None, "tensor"),
            P("tensor"),
            P(),
            P(),
            P("tensor"),
            P("tensor"),
            P("tensor"),
            P("tensor"),
            P("dp", "tensor"),
        ),
        check_vma=False,
    )
```

```python
import functools

import jax
import jax.numpy as jnp
from jax import lax
from jax.experimental import pallas as pl
from jax.experimental.pallas import tpu as pltpu
from jax.sharding import Mesh
from jax.sharding import PartitionSpec as P

Q = 256
HD = 64
NS = 128
EPS = 1e-05
F32 = jnp.float32
BF = jnp.bfloat16
VMEM_LIMIT = 56 * 1024 * 1024


def mm(a, b):
    return lax.dot_general(a, b, (((1,), (0,)), ((), ())), preferred_element_type=F32)


def mm_nt(a, b):
    return lax.dot_general(a, b, (((1,), (1,)), ((), ())), preferred_element_type=F32)


def mm_tn(a, b):
    return lax.dot_general(a, b, (((0,), (0,)), ((), ())), preferred_element_type=F32)


def split3(v):
    hi = v.astype(BF)
    rest = v - hi.astype(F32)
    mid = rest.astype(BF)
    low = (rest - mid.astype(F32)).astype(BF)
    return hi, mid, low


def split2(v):
    hi = v.astype(BF)
    return hi, (v - hi.astype(F32)).astype(BF)


def lanes(shape):
    return lax.broadcasted_iota(jnp.int32, shape, len(shape) - 1)


def lower_ones():
    rows = lax.broadcasted_iota(jnp.int32, (Q, Q), 0)
    return rows >= lanes((Q, Q))


def expander(heads):
    row = lax.broadcasted_iota(jnp.int32, (128, heads * HD), 0)
    head = lanes((128, heads * HD)) // HD
    return ((row == head) | (row == head + LOW)).astype(BF)


LOW = 16


def spread(v, ones):
    hi, low = split2(v)
    return mm(jnp.where(lanes(v.shape) < LOW, hi.astype(F32), low.astype(F32)).astype(BF), ones)


def gather_heads(v, ones):
    hi, low = split2(v)
    return mm_nt(hi, ones) + mm_nt(low, ones)


def softplus(z):
    return jnp.maximum(z, 0.0) + jnp.log1p(jnp.exp(-jnp.abs(z)))


def sigmoid(v):
    return 1.0 / (1.0 + jnp.exp(-v))


def running_sum(tri, v):
    hi, mid, low = split3(v)
    return mm(tri, hi) + mm(tri, mid) + mm(tri, low)


def suffix_sum(tri, v):
    hi, mid, low = split3(v)
    return mm_tn(tri, hi) + mm_tn(tri, mid) + mm_tn(tri, low)


KEEP = 0
SIDE = 9
LIVE = 10
PREV = 14
HALF = 18
ROWS = 34
STATE_ROWS = NS + 16


def call(kernel, name, grid, table, ins, outs, scratch=(), cost=(0, 0, 0)):
    def spec(block, index):
        if block is None:
            return pl.BlockSpec(memory_space=pl.ANY)
        return pl.BlockSpec(block, index)

    return pl.pallas_call(
        kernel,
        grid_spec=pltpu.PrefetchScalarGridSpec(
            num_scalar_prefetch=1,
            grid=(grid,),
            in_specs=[spec(block, index) for _, block, index in ins],
            out_specs=[spec(block, index) for _, _, block, index in outs],
            scratch_shapes=list(scratch),
        ),
        out_shape=[jax.ShapeDtypeStruct(shape, dtype) for shape, dtype, _, _ in outs],
        compiler_params=pltpu.CompilerParams(dimension_semantics=("arbitrary",), vmem_limit_bytes=VMEM_LIMIT),
        cost_estimate=pl.CostEstimate(flops=cost[0], bytes_accessed=cost[1], transcendentals=cost[2]),
        name=name,
    )(table, *[array for array, _, _ in ins])


def rows_of(array, size=Q):
    return array, (size, array.shape[1]), lambda k, table: (k, 0)


def all_of(array):
    return array, array.shape, lambda k, table: (0,) * array.ndim


def out_rows(count, width, dtype, size=Q):
    return (count * size, width), dtype, (size, width), lambda k, table: (k, 0)


def out_all(shape, dtype):
    return shape, dtype, shape, lambda k, table: (0,) * len(shape)


def decays(cum, ones):
    grow = spread(jnp.exp(cum), ones)
    fade = spread(jnp.exp(cum[Q - 1 :, :] - cum), ones)
    return grow, fade


def conv_run(conv_ref, buf):
    run = conv_ref[4:5, :] + conv_ref[3:4, :] * buf[8 : 8 + Q, :]
    for j in range(1, 4):
        run = run + conv_ref[3 - j : 4 - j, :] * buf[8 - j : 8 - j + Q, :]
    return run


def front_kernel(
    table, mine_ref, other_ref, tok_ref, tail_ref, conv_ref, head_ref, ones_ref, tri_ref,
    w_ref, pre_ref, before_ref, act_ref, z_ref, cum_ref, state_ref,
    ext, buf, sems,
):
    k = pl.program_id(0)
    part = tok_ref.shape[1] // 16
    width = ones_ref.shape[1]
    half = width // 2

    @pl.when(k == 0)
    def _():
        copies = []
        for c, ref in enumerate((mine_ref, other_ref)):
            for i in range(16):
                row = pl.multiple_of(table[ROWS + 16 * c + i], part)
                copies.append(
                    pltpu.make_async_copy(
                        ref.at[i], w_ref.at[table[HALF + i], pl.ds(row, part), :], sems.at[16 * c + i]
                    )
                )
        for copy in copies:
            copy.start()
        for copy in copies:
            copy.wait()

    keep = table[KEEP + 2 * k + table[SIDE]].astype(F32)
    ext[0:16, :] = tail_ref[...]
    ext[16:, :] = tok_ref[...]
    tok = ext[...]
    proj = mm(tok, w_ref[0]), mm(tok, w_ref[1])
    for i in range(2):
        for to, size, at in ((half * i, half, 0), (width + NS * i, NS, half)):
            buf[0:8, to : to + size] = proj[i][8:16, at : at + size] * keep
            buf[8:, to : to + size] = proj[i][16:, at : at + size]
    pre_ref[...] = buf[8:, :]
    before_ref[...] = buf[0:8, :]
    run = conv_run(conv_ref, buf)
    act = (run * sigmoid(run)).astype(BF)
    act_ref[...] = act
    z = proj[0][16:, half + NS :] + proj[1][16:, half + NS :] + head_ref[0:1, :]
    z_ref[...] = z
    step = softplus(z)
    cum = running_sum(tri_ref[...], step * head_ref[1:2, :])
    cum_ref[...] = cum
    ones = ones_ref[...]
    weigh = spread(step * jnp.exp(cum[Q - 1 :, :] - cum), ones)
    grown = (act[:, :width].astype(F32) * weigh).astype(BF)
    state_ref[0:NS, :] = mm_tn(act[:, width : width + NS], grown).astype(BF)
    last = spread(jnp.broadcast_to(jnp.exp(cum[Q - 1 :, :]), (16, 128)), ones)
    hi, low = split2(last)
    sub = lax.broadcasted_iota(jnp.int32, last.shape, 0)
    state_ref[NS:, :] = jnp.where(sub == 0, hi.astype(F32), low.astype(F32)).astype(BF)


def front(table, mine, other, tokens, tails, conv, head, ones, tri):
    d = tokens.shape[1]
    width = ones.shape[1]
    cols = width + 2 * NS
    half = width // 2 + NS + 128
    return call(
        front_kernel, "conv_and_states", 4, table,
        [
            (mine, None, None), (other, None, None), rows_of(tokens),
            (tails, (16, d), lambda k, table: (table[PREV + k], 0)),
            all_of(conv), all_of(head), all_of(ones), all_of(tri),
        ],
        [
            out_all((2, d, half), BF), out_rows(4, cols, F32), out_rows(4, cols, F32, 8), out_rows(4, cols, BF),
            out_rows(4, 128, F32), out_rows(4, 128, F32), out_rows(4, width, BF, STATE_ROWS),
        ],
        [pltpu.VMEM((16 + Q, d), BF), pltpu.VMEM((8 + Q, cols), F32), pltpu.SemaphoreType.DMA((32,))],
        (5 * 10**9, 16 * 10**6, 2 * 10**6),
    )


def within_kernel(table, act_ref, z_ref, cum_ref, chan_ref, ones_ref, mixed_ref):
    width = ones_ref.shape[1]
    act = act_ref[...]
    cum = cum_ref[...]
    x = act[:, :width].astype(F32)
    xs = x * spread(softplus(z_ref[...]), ones_ref[...])
    scores = mm_nt(act[:, width + NS :], act[:, width : width + NS])
    cum_row = cum.T
    lower = lower_ones()
    half = lanes((Q, 128)) < HD
    for p in range(width // 128):
        span = slice(128 * p, 128 * (p + 1))
        xp = xs[:, span]
        total = chan_ref[0:1, span] * x[:, span]
        for i in range(2):
            h = 2 * p + i
            diff = cum[:, h : h + 1] - cum_row[h : h + 1, :]
            mix = (scores * jnp.exp(jnp.where(lower, diff, -1e30))).astype(BF)
            total = total + mm(mix, jnp.where(half if i == 0 else ~half, xp, 0.0).astype(BF))
        mixed_ref[:, span] = total


def within(table, act, z, cum, chan, ones):
    return call(
        within_kernel, "ssd_within", 4, table,
        [rows_of(act), rows_of(z), rows_of(cum), all_of(chan), all_of(ones)],
        [out_rows(4, ones.shape[1], F32)],
        cost=(8 * 10**9, 6 * 10**6, 4 * 10**6),
    )[0]


def decay_of(state_ref):
    rows = state_ref[NS : NS + 8, :].astype(F32)
    return rows[0:1, :] + rows[1:2, :]


def through_kernel(
    table, tok_ref, cot_ref, w_ref, within_ref, act_ref, cum_ref, own_ref, pair_ref, chan_ref, ones_ref,
    gate_ref, mixed_ref, hg_ref, sin_ref, sums_ref,
    state,
):
    k = pl.program_id(0)
    width = ones_ref.shape[1]
    half = width // 2
    first = table[SIDE] == 0

    @pl.when(k == 0)
    def _():
        state[...] = jnp.zeros_like(state)

    own, pair = own_ref[0:NS, :].astype(F32), pair_ref[0:NS, :].astype(F32)
    own_decay, pair_decay = decay_of(own_ref), decay_of(pair_ref)
    at_a = table[KEEP + 2 * k].astype(F32) * state[...]
    after_a = jnp.where(first, own_decay, pair_decay) * at_a + jnp.where(first, own, pair)
    at_b = table[KEEP + 2 * k + 1].astype(F32) * after_a
    state[...] = jnp.where(first, pair_decay, own_decay) * at_b + jnp.where(first, pair, own)
    carried = jnp.where(first, at_a, at_b).astype(BF)
    sin_ref[...] = carried

    grow = spread(jnp.exp(cum_ref[...]), ones_ref[...])
    mixed = within_ref[...] + mm(act_ref[:, width + NS :], carried) * grow
    mixed_ref[...] = mixed
    tok = tok_ref[...]
    cot = cot_ref[...]
    row = lax.broadcasted_iota(jnp.int32, (Q, half), 0)
    live = row < table[LIVE + k]
    square = jnp.zeros((8, Q), F32)
    inner = jnp.zeros((8, Q), F32)
    one = jnp.ones((8, half), BF)
    for i in range(2):
        span = slice(half * i, half * (i + 1))
        gate = mm(tok, w_ref[i, :, :half])
        gate_ref[:, span] = gate
        hg = jnp.where(live, mm(cot, w_ref[i, :, half:]), 0.0)
        hg_ref[:, span] = hg
        gated = mixed[:, span] * (gate * sigmoid(gate))
        for part in split2(gated * gated):
            square = square + mm_nt(one, part)
        for part in split2(hg * chan_ref[1:2, span] * gated):
            inner = inner + mm_nt(one, part)
    sub = lax.broadcasted_iota(jnp.int32, (8, Q), 0)
    sums_ref[...] = jnp.where(sub == 0, square, inner)


def through(table, tokens, cot, w, mixed, act, cum, own, pair, chan, ones):
    width = ones.shape[1]
    return call(
        through_kernel, "ssd_through", 4, table,
        [
            rows_of(tokens), rows_of(cot), all_of(w), rows_of(mixed), rows_of(act), rows_of(cum),
            rows_of(own, STATE_ROWS), rows_of(pair, STATE_ROWS), all_of(chan), all_of(ones),
        ],
        [
            out_rows(4, width, F32), out_rows(4, width, F32), out_rows(4, width, F32), out_rows(4, width, BF, NS),
            ((8, 4 * Q), F32, (8, Q), lambda k, table: (0, k)),
        ],
        [pltpu.VMEM((NS, width), F32)],
        (6 * 10**9, 30 * 10**6, 2 * 10**6),
    )


def gate_back_kernel(
    table, hg_ref, mixed_ref, gate_ref, sums_ref, act_ref, cum_ref, chan_ref, ones_ref,
    hidden_ref, glow_ref, dy_ref, dstate_ref, ngg_ref, *, inner,
):
    k = pl.program_id(0)
    width = ones_ref.shape[1]

    @pl.when(k == 0)
    def _():
        ngg_ref[...] = jnp.zeros_like(ngg_ref)

    sums = sums_ref[...]
    scale_row = lax.rsqrt(sums[0:1, :] / inner + EPS)
    pull_row = scale_row * scale_row * scale_row * (sums[1:2, :] / inner)
    sub = lax.broadcasted_iota(jnp.int32, (128, Q), 0)
    cols = jnp.where(sub == 0, scale_row, jnp.where(sub == 1, pull_row, 0.0)).T
    scale = cols[:, 0:1]
    pull = cols[:, 1:2]
    hg = hg_ref[...]
    mixed = mixed_ref[...]
    gate = gate_ref[...]
    sg = sigmoid(gate)
    silu = gate * sg
    gated = mixed * silu
    normal = gated * scale
    gain = chan_ref[1:2, :]
    row = lax.broadcasted_iota(jnp.int32, (Q, width), 0)
    hidden_ref[...] = jnp.where(row < table[LIVE + k], normal * gain, 0.0).astype(BF)
    ngg_ref[0:1, :] += jnp.sum(hg * normal, axis=0, keepdims=True)
    gg = scale * gain * hg - gated * pull
    dy = gg * silu
    dy_ref[...] = dy
    glow_ref[...] = (gg * mixed * sg * (1.0 + gate * (1.0 - sg))).astype(BF)
    grow = spread(jnp.exp(cum_ref[...]), ones_ref[...])
    dstate_ref[...] = mm_tn(act_ref[:, width + NS :], (dy * grow).astype(BF)).astype(BF)


def gate_back(table, hg, mixed, gate, sums, act, cum, chan, ones, inner):
    width = ones.shape[1]
    return call(
        functools.partial(gate_back_kernel, inner=inner), "gate_back", 4, table,
        [
            rows_of(hg), rows_of(mixed), rows_of(gate), (sums, (8, Q), lambda k, table: (0, k)),
            rows_of(act), rows_of(cum), all_of(chan), all_of(ones),
        ],
        [
            out_rows(4, width, BF), out_rows(4, width, BF), out_rows(4, width, F32), out_rows(4, width, BF, NS),
            out_all((8, width), F32),
        ],
        cost=(2 * 10**9, 18 * 10**6, 10**6),
    )


def backward_kernel(
    table, act_ref, pre_ref, before_ref, z_ref, cum_ref, sin_ref, dy_ref, mine_ref, theirs_ref, decay_ref,
    conv_ref, head_ref, chan_ref, ones_ref, tri_ref,
    low_ref, tail_ref, first_ref, convsum_ref, headsum_ref, skipsum_ref,
    carry, buf, *, heads,
):
    k = 3 - pl.program_id(0)
    width = heads * HD
    cols = width + 2 * NS
    side = table[SIDE]

    @pl.when(pl.program_id(0) == 0)
    def _():
        carry[...] = jnp.zeros_like(carry)
        convsum_ref[...] = jnp.zeros_like(convsum_ref)
        headsum_ref[...] = jnp.zeros_like(headsum_ref)
        skipsum_ref[...] = jnp.zeros_like(skipsum_ref)

    act = act_ref[...]
    x = act[:, :width].astype(F32)
    bmat = act[:, width : width + NS]
    cmat = act[:, width + NS :]
    z = z_ref[...]
    step = softplus(z)
    cum = cum_ref[...]
    ones = ones_ref[...]
    tri = tri_ref[...]
    step_x = spread(step, ones)
    grow_x, fade_x = decays(cum, ones)
    last_x = grow_x[Q - 1 :, :]
    xs = x * step_x
    xsb = xs.astype(BF)
    dy = dy_ref[...]

    mine = mine_ref[...].astype(F32)
    theirs = theirs_ref[...].astype(F32)
    pair_decay = decay_of(decay_ref)
    keep_a = table[KEEP + 2 * k].astype(F32)
    keep_b = table[KEEP + 2 * k + 1].astype(F32)
    after_b = carry[...]
    first = side == 0
    after_a = keep_b * (jnp.where(first, pair_decay, last_x) * after_b + jnp.where(first, theirs, mine))
    carry[...] = keep_a * (jnp.where(first, last_x, pair_decay) * after_a + jnp.where(first, mine, theirs))
    dstate = jnp.where(first, after_a, after_b)
    dstate_low = dstate.astype(BF)

    scores = mm_nt(cmat, bmat)
    cum_row = cum.T
    lower = lower_ones()
    lane = lanes((Q, 128))
    half = lane < HD
    sub = lax.broadcasted_iota(jnp.int32, (128, Q), 0)
    dscores = jnp.zeros((Q, Q), F32)
    rowsum = jnp.zeros((Q, 128), F32)
    colsum = jnp.zeros((128, Q), F32)
    parts = []
    for p in range(heads // 2):
        span = slice(128 * p, 128 * (p + 1))
        dyp = dy[:, span]
        part = jnp.zeros((Q, 128), F32)
        for i in range(2):
            h = 2 * p + i
            diff = cum[:, h : h + 1] - cum_row[h : h + 1, :]
            decay = jnp.exp(jnp.where(lower, diff, -1e30))
            mix = (scores * decay).astype(BF)
            dym = jnp.where(half if i == 0 else ~half, dyp, 0.0).astype(BF)
            grad = mm_nt(dym, xsb[:, span]) * decay
            dscores = dscores + grad
            grad = grad * scores
            rowsum = jnp.where(lane == h, jnp.sum(grad, axis=1, keepdims=True), rowsum)
            colsum = jnp.where(sub == h, jnp.sum(grad, axis=0, keepdims=True), colsum)
            part = part + mm_tn(mix, dym)
        parts.append(part)
    inside = jnp.concatenate(parts, axis=1)
    carried = sin_ref[...]
    dyg = (dy * grow_x).astype(BF)
    dsl = dscores.astype(BF)
    dc = mm(dsl, bmat) + mm_nt(dyg, carried)
    db = mm_tn(dsl, cmat) + mm_nt((xs * fade_x).astype(BF), dstate_low)
    passed = mm(cmat, carried) * grow_x
    later = mm(bmat, dstate_low) * fade_x
    q_passed = gather_heads(dy * passed, ones)
    q_later = gather_heads(x * later, ones)
    q_inside = gather_heads(x * inside, ones)
    hold = jnp.sum(dstate * carried.astype(F32), axis=0, keepdims=True) * last_x
    q_hold = gather_heads(jnp.broadcast_to(hold, (8, width)), ones)[0:1, :]
    dx = step_x * (inside + later) + chan_ref[0:1, :] * dy
    net = jnp.where(lane < LOW, q_passed + rowsum - colsum.T, 0.0)
    push = step * q_later
    drate = suffix_sum(tri, net) + running_sum(tri, push) - push + q_hold
    rate_of = head_ref[1:2, :]
    dstep = q_inside + q_later + drate * rate_of
    dz = jnp.where(lane < heads, dstep * sigmoid(z), 0.0)
    headsum_ref[0:1, :] += jnp.sum(dz, axis=0, keepdims=True)
    headsum_ref[1:2, :] += jnp.sum(drate * step * rate_of, axis=0, keepdims=True)
    skipsum_ref[0:1, :] += jnp.sum(dy * x, axis=0, keepdims=True)

    grad = jnp.concatenate([dx, db, dc], axis=1)
    buf[0:8, :] = before_ref[...]
    buf[8 : 8 + Q, :] = pre_ref[...]
    run = conv_run(conv_ref, buf)
    sg = sigmoid(run)
    dact = grad * (sg * (1.0 + run * (1.0 - sg)))
    for j in range(4):
        convsum_ref[3 - j : 4 - j, :] += jnp.sum(dact * buf[8 - j : 8 - j + Q, :], axis=0, keepdims=True)
    convsum_ref[4:5, :] += jnp.sum(dact, axis=0, keepdims=True)
    first_ref[...] = dact[0:8, :]
    buf[0:Q, :] = dact
    buf[Q : Q + 8, :] = jnp.zeros((8, cols), F32)
    dpre = conv_ref[3:4, :] * dact
    for j in range(1, 4):
        dpre = dpre + conv_ref[3 - j : 4 - j, :] * buf[j : j + Q, :]
    tail_ref[...] = dpre[Q - 8 :, :]
    low_ref[:, :cols] = dpre.astype(BF)
    low_ref[:, cols:] = dz.astype(BF)


def backward(table, act, pre, before, z, cum, sin, dy, mine, theirs, pair, conv, head, chan, ones, tri, heads):
    cols = act.shape[1]
    width = heads * HD

    def back(array, size=Q):
        return array, (size, array.shape[1]), lambda i, table: (3 - i, 0)

    def out_back(w, dtype, size=Q):
        return (4 * size, w), dtype, (size, w), lambda i, table: (3 - i, 0)

    return call(
        functools.partial(backward_kernel, heads=heads), "ssd_backward", 4, table,
        [
            back(act), back(pre), back(before, 8), back(z), back(cum), back(sin, NS), back(dy),
            back(mine, NS), back(theirs, NS), back(pair, STATE_ROWS),
            all_of(conv), all_of(head), all_of(chan), all_of(ones), all_of(tri),
        ],
        [
            out_back(cols + 128, BF), out_back(cols, F32, 8), out_back(cols, F32, 8),
            out_all((8, cols), F32), out_all((8, 128), F32), out_all((8, width), F32),
        ],
        [pltpu.VMEM((NS, width), F32), pltpu.VMEM((8 + Q, cols), F32)],
        (30 * 10**9, 25 * 10**6, 6 * 10**6),
    )


def normed_kernel(table, order, glow_ref, low_ref, tok_ref, wzo_ref, wx_ref, out_ref, dots_ref):
    half = wzo_ref.shape[2] // 2
    width = 2 * half

    @pl.when(pl.program_id(0) == 0)
    def _():
        dots_ref[...] = jnp.zeros_like(dots_ref)

    low = low_ref[...]
    total = mm_nt(low[:, width + 2 * NS :], wx_ref[0, :, half + NS :] + wx_ref[1, :, half + NS :])
    for i in range(2):
        total = total + mm_nt(glow_ref[:, half * i : half * (i + 1)], wzo_ref[i, :, :half])
        total = total + mm_nt(low[:, half * i : half * (i + 1)], wx_ref[i, :, :half])
        total = total + mm_nt(low[:, width + NS * i : width + NS * (i + 1)], wx_ref[i, :, half : half + NS])
    out_ref[...] = total.astype(BF)
    dots_ref[0:1, :] += jnp.sum(total * tok_ref[...].astype(F32), axis=0, keepdims=True)


def normed_part(order, glow, low, tokens, wzo, wx):
    n = order.shape[0]
    d = tokens.shape[1]
    pick_rows = lambda a: pl.BlockSpec((Q, a.shape[1]), lambda i, order: (order[i], 0))
    whole = lambda a: pl.BlockSpec(a.shape, lambda i, order: (0, 0, 0))

    def kernel(order_ref, *refs):
        normed_kernel(None, order_ref, *refs)

    return pl.pallas_call(
        kernel,
        grid_spec=pltpu.PrefetchScalarGridSpec(
            num_scalar_prefetch=1,
            grid=(n,),
            in_specs=[pick_rows(glow), pick_rows(low), pick_rows(tokens), whole(wzo), whole(wx)],
            out_specs=[
                pl.BlockSpec((Q, d), lambda i, order: (i, 0)),
                pl.BlockSpec((8, d), lambda i, order: (0, 0)),
            ],
        ),
        out_shape=[jax.ShapeDtypeStruct((n * Q, d), BF), jax.ShapeDtypeStruct((8, d), F32)],
        compiler_params=pltpu.CompilerParams(dimension_semantics=("arbitrary",), vmem_limit_bytes=VMEM_LIMIT),
        cost_estimate=pl.CostEstimate(
            flops=2 * n * Q * d * 1920, bytes_accessed=9 * 10**6 + n * 2 * 10**6, transcendentals=0
        ),
        name="normed_grad",
    )(order, glow, low, tokens, wzo, wx)


DP = ("yl", "x", "core")
RIGHT = [(i, (i + 1) % 4) for i in range(4)]
LEFT = [(i, (i + 3) % 4) for i in range(4)]
NEAR = [(i, i ^ 1) for i in range(4)]
FAR = [(i, i ^ 2) for i in range(4)]
SWAP = [(0, 1), (1, 0)]


def around_y(step):
    place = lambda y: y % 2 * 2 + y // 2
    return [(place(y), place((y + step) % 4)) for y in range(4)]


def pick(array, index, axis):
    return lax.dynamic_index_in_dim(array, index, axis, keepdims=False)


def up(v):
    return v.astype(F32)


def ring_gather(x, axis, cut):
    back, on = lax.ppermute(x, axis, RIGHT), lax.ppermute(x, axis, LEFT)
    far = jnp.concatenate([lax.ppermute(back[:cut], axis, RIGHT), lax.ppermute(on[cut:], axis, LEFT)])
    return back, on, far


def ring_sum(far, ahead, behind, own, axis):
    from_left, from_right = lax.ppermute(far[0], axis, RIGHT), lax.ppermute(far[1], axis, LEFT)
    ahead = jnp.stack([(up(ahead[0]) + up(from_left)).astype(BF), ahead[1]])
    behind = jnp.stack([behind[0], (up(behind[1]) + up(from_right)).astype(BF)])
    return ahead, behind, lambda a, b: up(own) + up(lax.ppermute(a, axis, RIGHT)) + up(lax.ppermute(b, axis, LEFT))


def total(value, steps):
    for axis, to in steps:
        value = value + lax.ppermute(value, axis, to)
    return value


def gather_shards(own):
    send = lambda step: lax.ppermute(own, ("yl", "yh"), around_y(step))
    stack = jnp.stack([own, send(1), send(3), send(2)])
    back, on, far = ring_gather(stack, "x", 2)
    mine = jnp.concatenate([stack, back, on, far])
    return mine, lax.ppermute(mine, "core", SWAP)


def scatter_shards(part):
    yl, x, core, yh = (lax.axis_index(a) for a in ("yl", "x", "core", "yh"))
    _, d, cols = part.shape
    part = part.reshape(2, 2, 4, 2, d // 16, cols)
    swapped = lax.ppermute(pick(part, 1 - core, 3), "core", SWAP)
    both = (up(pick(part, core, 3)) + up(swapped)).astype(BF)
    block = lambda k: pick(both, (x + k) % 4, 2)
    ahead, behind, finish = ring_sum(block(2), block(1), block(3), block(0), "x")
    own = finish(ahead, behind).reshape(4, d // 16, cols)
    y = yh * 2 + yl
    out = pick(own, y, 0)
    for step in (2, 1, 3):
        out = out + up(lax.ppermute(pick(own, (y + step) % 4, 0).astype(BF), ("yl", "yh"), around_y(step)))
    return out


def local(
    x_in,
    cotangent,
    seq_lengths,
    in_gain,
    w_z,
    w_x,
    w_dt,
    w_bc,
    conv_wx,
    conv_bx,
    conv_wbc,
    conv_bbc,
    dt_bias,
    a_log,
    d_skip,
    gnorm_gain,
    w_out,
):
    rows, d = x_in.shape
    own_heads = dt_bias.shape[0]
    heads = 2 * own_heads
    half = own_heads * HD
    width = 2 * half
    cols = width + 2 * NS
    shard = w_z.shape[0]
    yl, x, core, z, yh = (lax.axis_index(a) for a in ("yl", "x", "core", "z", "yh"))
    dp = (yl * 4 + x) * 2 + core
    side = yh == 0

    lengths = seq_lengths[0]
    spans = (lengths + Q - 1) // Q * Q
    starts = jnp.cumsum(spans) - spans
    place = jnp.arange(9, dtype=jnp.int32)[:, None] * Q
    inside = (place >= starts) & (place < starts + spans)
    keep = jnp.sum((inside & (place > starts)).astype(jnp.int32), axis=1)
    live = jnp.sum(jnp.where(inside, jnp.clip(starts + lengths - place, 0, Q), 0), axis=1)
    ring = jnp.arange(4, dtype=jnp.int32)
    hops = jnp.array([0, 3, 1, 2], jnp.int32)
    from_y = (yh * 2 + yl + hops) % 4
    from_x = (x + hops) % 4
    shard_rows = (((from_y % 2)[None, :] * 4 + from_x[:, None]) * 2).reshape(16) * shard
    table = jnp.concatenate(
        [
            keep,
            yh[None],
            pick(live[:8].reshape(4, 2), yh, 1),
            (ring + 3 + yh) % 4,
            jnp.tile(from_y // 2, 4),
            shard_rows + core * shard,
            shard_rows + (1 - core) * shard,
        ]
    ).astype(jnp.int32)

    resid = x_in.astype(F32)
    inverse = lax.rsqrt(jnp.mean(resid * resid, axis=-1, keepdims=True) + EPS)
    normed = (resid * inverse * in_gain).astype(BF)
    ext = jnp.concatenate([normed, lax.ppermute(normed[rows - 16 :], "yh", SWAP)])

    blank = lambda k: jnp.zeros((shard, k), BF)
    gap = LOW - heads
    low_dt = jnp.concatenate([w_dt, blank(own_heads + gap), w_dt, blank(128 - LOW - own_heads)], axis=1)
    high_dt = jnp.concatenate([blank(own_heads), w_dt, blank(own_heads + gap), w_dt, blank(128 - LOW - heads)], axis=1)
    own_bc = lax.dynamic_slice_in_dim(w_bc, yh * NS, NS, 1)
    own_x = jnp.concatenate([w_x, own_bc, jnp.where(side, low_dt, high_dt)], axis=1)
    wzo = lax.all_gather(jnp.concatenate([w_z, w_out], axis=1), ("yh",) + DP, axis=0, tiled=True)
    wzo = wzo.reshape(2, d, width)
    mine, other = gather_shards(own_x)

    def per_head(v):
        return jnp.pad(v, (0, half - own_heads))

    params = jnp.stack(
        [conv_wx[0], conv_wx[1], conv_wx[2], conv_wx[3], conv_bx, jnp.repeat(d_skip, HD), gnorm_gain]
        + [jnp.concatenate([dt_bias, -jnp.exp(a_log), jnp.zeros((half - heads,), F32)])]
    )
    swapped = lax.ppermute(params, "yh", SWAP)
    params = jnp.where(side, params, swapped), jnp.where(side, swapped, params)
    chans = jnp.concatenate(params, axis=1)
    conv = jnp.concatenate([chans[:5], jnp.zeros((3, width), F32)])
    conv_bc = jnp.concatenate([conv_wbc, conv_bbc[None], jnp.zeros((3, 2 * NS), F32)])
    conv = jnp.concatenate([conv, conv_bc], axis=1)
    chan = jnp.concatenate([chans[5:7], jnp.zeros((6, width), F32)])

    def head_row(at):
        v = jnp.concatenate([p[7, at : at + own_heads] for p in params] + [jnp.zeros((gap,), F32)])
        return jnp.concatenate([v, v, jnp.zeros((128 - 2 * LOW,), F32)])

    head = jnp.concatenate([jnp.stack([head_row(0), head_row(own_heads)]), jnp.zeros((6, 128), F32)])
    ones = expander(heads)
    tri = lower_ones().astype(BF)

    def assemble(pieces, start, stop):
        out = jnp.zeros((4 * (stop - start), d), BF)
        for hop, piece in zip((0, 3, 1, 2), pieces):
            out = lax.dynamic_update_slice_in_dim(out, piece[start:stop], (z + hop) % 4 * (stop - start), 0)
        return out

    pieces = (ext,) + ring_gather(ext, "z", 144)
    tokens = assemble(pieces, 0, rows)
    tails = assemble(pieces, rows, rows + 16)
    late, _ = lax.optimization_barrier((cotangent, pieces[1]))
    cot = assemble((late,) + ring_gather(late, "z", 128), 0, rows)

    wx, pre, before, act, zs, cum, states = front(table, mine, other, tokens, tails, conv, head, ones, tri)
    pair = lax.ppermute(states, "yh", SWAP)
    mixed = within(table, act, zs, cum, chan, ones)
    gate, mixed, hg, sin, sums = through(table, tokens, cot, wzo, mixed, act, cum, states, pair, chan, ones)
    sums = total(sums, [("z", NEAR), ("z", FAR)])
    hidden, gate_low, dy, dstates, gain_sum = gate_back(
        table, hg, mixed, gate, sums, act, cum, chan, ones, 4 * width
    )
    pair_dstates = lax.ppermute(dstates, "yh", SWAP)

    branch = mm_nt(hidden[:, :half], wzo[0, :, half:]) + mm_nt(hidden[:, half:], wzo[1, :, half:])
    branch = branch.astype(BF).reshape(4, 2, Q // 2, d)
    block = lambda k: pick(branch, (z + k) % 4, 0)
    ahead, behind, finish = ring_sum(block(2), block(1), block(3), block(0), "z")
    early = jnp.stack(
        [
            jnp.concatenate(
                [mm_tn(tokens, gate_low[:, half * i : half * (i + 1)]), mm_tn(cot, hidden[:, half * i : half * (i + 1)])],
                axis=1,
            ).astype(BF)
            for i in range(2)
        ]
    )
    dy, ahead, behind, early = lax.optimization_barrier((dy, ahead, behind, early))
    early = lax.psum_scatter(early.reshape(2 * d, width), ("yh",) + DP, scatter_dimension=0, tiled=True)
    branch = finish(ahead, behind).reshape(rows, d)
    own_live = pick(live, 2 * z + yh, 0)
    live_rows = jnp.arange(rows, dtype=jnp.int32)[:, None] < own_live
    output = (resid + jnp.where(live_rows, branch, 0.0)).astype(BF)

    low, low_tail, first, conv_sum, head_sum, skip_sum = backward(
        table, act, pre, before, zs, cum, sin, dy, dstates, pair_dstates, pair, conv, head, chan, ones, tri, heads
    )
    later = lax.ppermute(first, "yh", SWAP).reshape(4, 8, cols)
    later = jnp.where(side, later, jnp.roll(later, -1, axis=0))
    keep_later = pick(keep[1:9].reshape(4, 2), yh, 1).astype(F32)
    later = later * keep_later[:, None, None]
    fixed = low_tail.reshape(4, 8, cols)
    for j in range(1, 4):
        fixed = fixed.at[:, 8 - j :].add(conv[3 - j] * later[:, :j])
    low = low.reshape(4, Q, cols + 128).at[:, Q - 8 :, :cols].set(fixed.astype(BF)).reshape(4 * Q, cols + 128)

    far, dots_far = normed_part((z[None] + 2) % 4, gate_low, low, tokens, wzo, wx)
    near, dots = normed_part((z + jnp.array([1, 3, 0])) % 4, gate_low, low, tokens, wzo, wx)
    far, near = far.reshape(2, Q // 2, d), near.reshape(3, 2, Q // 2, d)
    ahead, behind, finish = ring_sum(far, near[0], near[1], near[2], "z")
    normed_grad = finish(ahead, behind).reshape(rows, d)
    late = jnp.stack(
        [
            mm_tn(
                tokens,
                jnp.concatenate(
                    [low[:, half * i : half * (i + 1)], low[:, width + NS * i : width + NS * (i + 1)], low[:, cols:]],
                    axis=1,
                ),
            ).astype(BF)
            for i in range(2)
        ]
    )
    late = scatter_shards(late)

    projected = jnp.sum(normed_grad * in_gain * resid, axis=-1, keepdims=True) / d
    x_grad = inverse * in_gain * normed_grad - resid * inverse**3 * projected + cotangent.astype(F32)

    bc_grad = total(late[:, half : half + NS], [("z", NEAR), ("z", FAR)])
    bc_pair = lax.ppermute(bc_grad, "yh", SWAP)
    w_bc_grad = jnp.concatenate([jnp.where(side, bc_grad, bc_pair), jnp.where(side, bc_pair, bc_grad)], axis=1)
    w_dt_grad = lax.dynamic_slice_in_dim(late[:, half + NS :], yh * own_heads, own_heads, 1)

    small = jnp.concatenate(
        [
            conv_sum[:5],
            jnp.concatenate([gain_sum[:1], head_sum[:1], head_sum[1:2]], axis=1),
            jnp.pad(skip_sum[:1], ((0, 0), (0, 2 * NS))),
            jnp.zeros((1, cols), F32),
        ]
    )
    dots = (dots_far[:1] + dots[:1]).reshape(8, d // 8)
    small = jnp.concatenate([small, jnp.pad(dots, ((0, 0), (0, 256 - d // 8)))], axis=1)
    small = total(small, [("core", SWAP), ("x", NEAR), ("x", FAR), ("yl", SWAP), ("yh", SWAP)])
    shared = total(small[:, width:], [("z", NEAR), ("z", FAR)])
    each = d // 128
    at = dp * shard + (2 * z + yh) * each
    dots = shared[:, 2 * NS : 2 * NS + d // 8].reshape(d)
    in_gain_grad = lax.dynamic_slice_in_dim(dots, at, each, 0) / lax.dynamic_slice_in_dim(in_gain, at, each, 0)
    own = lax.dynamic_slice_in_dim(small[:, :width], yh * half, half, 1)
    head_at = lambda k: lax.dynamic_slice_in_dim(small[5], width + 128 * k + yh * own_heads, own_heads, 0)
    return (
        output,
        x_grad,
        in_gain_grad,
        early[:, :half].astype(F32),
        late[:, :half],
        w_dt_grad,
        w_bc_grad,
        own[:4],
        own[4],
        shared[:4, : 2 * NS],
        shared[4, : 2 * NS],
        head_at(0),
        head_at(1),
        jnp.sum(own[6].reshape(own_heads, HD), axis=1),
        own[5],
        early[:, half:].astype(F32),
    )


def solution(mesh):
    grid = Mesh(mesh.devices.reshape(2, 4, 2, 4, 2), DP + ("z", "yh"))
    tensor = ("z", "yh")
    tokens, weight, channels = P(DP + tensor, None), P(DP, tensor), P(tensor)
    return jax.shard_map(
        local,
        mesh=grid,
        in_specs=(
            tokens,
            tokens,
            P(DP, None),
            P(),
            weight,
            weight,
            weight,
            P(DP, None),
            P(None, tensor),
            channels,
            P(),
            P(),
            channels,
            channels,
            channels,
            channels,
            weight,
        ),
        out_specs=(
            tokens,
            tokens,
            P(DP + tensor),
            weight,
            weight,
            weight,
            P(DP, None),
            P(None, tensor),
            channels,
            P(),
            P(),
            channels,
            channels,
            channels,
            channels,
            weight,
        ),
        check_vma=False,
    )
```

```python
import functools

import jax
import jax.numpy as jnp
import numpy as np
from jax import lax
from jax.experimental import pallas as pl
from jax.experimental.pallas import tpu as pltpu
from jax.sharding import Mesh
from jax.sharding import PartitionSpec as P

Q = 256
HD = 64
NS = 128
EPS = 1e-05
F32 = jnp.float32
BF = jnp.bfloat16
VMEM_LIMIT = 56 * 1024 * 1024


def mm(a, b):
    return lax.dot_general(a, b, (((1,), (0,)), ((), ())), preferred_element_type=F32)


def mm_nt(a, b):
    return lax.dot_general(a, b, (((1,), (1,)), ((), ())), preferred_element_type=F32)


def mm_tn(a, b):
    return lax.dot_general(a, b, (((0,), (0,)), ((), ())), preferred_element_type=F32)


def split3(v):
    hi = v.astype(BF)
    rest = v - hi.astype(F32)
    mid = rest.astype(BF)
    low = (rest - mid.astype(F32)).astype(BF)
    return hi, mid, low


def split2(v):
    hi = v.astype(BF)
    return hi, (v - hi.astype(F32)).astype(BF)


def lanes(shape):
    return lax.broadcasted_iota(jnp.int32, shape, len(shape) - 1)


def lower_ones():
    rows = lax.broadcasted_iota(jnp.int32, (Q, Q), 0)
    return rows >= lanes((Q, Q))


def expander(heads):
    row = np.arange(128)[:, None]
    head = np.arange(heads * HD)[None, :] // HD
    return jnp.asarray(((row == head) | (row == head + LOW)).astype(np.float32), BF)


LOW = 16


def spread(v, ones):
    hi, low = split2(v)
    return mm(jnp.where(lanes(v.shape) < LOW, hi.astype(F32), low.astype(F32)).astype(BF), ones)


def gather_heads(v, ones):
    hi, low = split2(v)
    return mm_nt(hi, ones) + mm_nt(low, ones)


def softplus(z):
    return jnp.maximum(z, 0.0) + jnp.log1p(jnp.exp(-jnp.abs(z)))


def sigmoid(v):
    return 1.0 / (1.0 + jnp.exp(-v))


def running_sum(tri, v):
    hi, mid, low = split3(v)
    return mm(tri, hi) + mm(tri, mid) + mm(tri, low)


def suffix_sum(tri, v):
    hi, mid, low = split3(v)
    return mm_tn(tri, hi) + mm_tn(tri, mid) + mm_tn(tri, low)


KEEP = 0
SIDE = 9
LIVE = 10
PREV = 14
HALF = 18
ROWS = 34
CORE = 66
ZED, EXE, WYE = 67, 68, 69
STATE_ROWS = NS + 16


CHEAP = pl.CostEstimate(flops=1000, bytes_accessed=1000, transcendentals=0)


def call(kernel, name, grid, table, ins, outs, scratch=()):
    def spec(block, index):
        if block is None:
            return pl.BlockSpec(memory_space=pl.ANY)
        return pl.BlockSpec(block, index)

    return pl.pallas_call(
        kernel,
        grid_spec=pltpu.PrefetchScalarGridSpec(
            num_scalar_prefetch=1,
            grid=(grid,),
            in_specs=[spec(block, index) for _, block, index in ins],
            out_specs=[spec(block, index) for _, _, block, index in outs],
            scratch_shapes=list(scratch),
        ),
        out_shape=[jax.ShapeDtypeStruct(shape, dtype) for shape, dtype, _, _ in outs],
        compiler_params=pltpu.CompilerParams(dimension_semantics=("arbitrary",), vmem_limit_bytes=VMEM_LIMIT),
        cost_estimate=CHEAP,
        name=name,
    )(table, *[array for array, _, _ in ins])


def rows_of(array, size=Q):
    return array, (size, array.shape[1]), lambda k, table: (k, 0)


def all_of(array):
    return array, array.shape, lambda k, table: (0,) * array.ndim


def out_rows(count, width, dtype, size=Q):
    return (count * size, width), dtype, (size, width), lambda k, table: (k, 0)


def out_all(shape, dtype):
    return shape, dtype, shape, lambda k, table: (0,) * len(shape)


def decays(cum, ones):
    grow = spread(jnp.exp(cum), ones)
    fade = spread(jnp.exp(cum[Q - 1 :, :] - cum), ones)
    return grow, fade


def conv_run(conv_ref, buf):
    run = conv_ref[4:5, :] + conv_ref[3:4, :] * buf[8 : 8 + Q, :]
    for j in range(1, 4):
        run = run + conv_ref[3 - j : 4 - j, :] * buf[8 - j : 8 - j + Q, :]
    return run


def pack_kernel(table, x_ref, bc_ref, dt_ref, z_ref, w_ref, out_ref):
    half = x_ref.shape[1]
    heads = dt_ref.shape[1]
    row = lax.broadcasted_iota(jnp.int32, (heads, 128), 0) + heads * table[0]
    lane = lanes((heads, 128))
    out_ref[:, :half] = x_ref[...]
    out_ref[:, half : half + NS] = jnp.where(table[0] == 0, up(bc_ref[:, :NS]), up(bc_ref[:, NS:])).astype(BF)
    place = ((lane == row) | (lane == row + LOW)).astype(F32).astype(BF)
    out_ref[:, half + NS : BLOCK] = mm(dt_ref[...], place).astype(BF)
    out_ref[:, BLOCK : BLOCK + half] = z_ref[...]
    out_ref[:, BLOCK + half :] = w_ref[...]


def pack(side, w_x, w_bc, w_dt, w_z, w_out):
    shape = (w_x.shape[0], 3 * w_x.shape[1] + NS + 128)
    return call(
        pack_kernel, "pack_shard", 1, side,
        [all_of(w_x), all_of(w_bc), all_of(w_dt), all_of(w_z), all_of(w_out)], [out_all(shape, BF)],
    )[0]


def prep_kernel(table, own_ref, pair_ref, wbc_ref, bbc_ref, conv_ref, chan_ref, head_ref):
    half = own_ref.shape[1]
    width = 2 * half
    own, pair = own_ref[...], pair_ref[...]
    first = table[SIDE] == 0
    for i in range(2):
        both = jnp.where(first, own, pair) if i == 0 else jnp.where(first, pair, own)
        span = slice(half * i, half * (i + 1))
        conv_ref[:, span] = both
        chan_ref[0:1, span] = both[5:6, :]
        chan_ref[1:2, span] = both[6:7, :]
    sub = lax.broadcasted_iota(jnp.int32, (8, 2 * NS), 0)
    rows = jnp.where(sub == 4, bbc_ref[...], 0.0)
    for j in range(4):
        rows = jnp.where(sub == j, wbc_ref[j : j + 1, :], rows)
    conv_ref[:, width:] = rows
    for i in range(2):
        at = slice(128 * i, 128 * (i + 1))
        head_ref[i : i + 1, :] = own[7:8, at] + pair[7:8, at]


def prep(table, own, pair, conv_wbc, conv_bbc):
    half = own.shape[1]
    out = lambda w: out_all((8, w), F32)
    return call(
        prep_kernel, "prep", 1, table,
        [all_of(own), all_of(pair), all_of(conv_wbc), all_of(conv_bbc)],
        [out(2 * half + 2 * NS), out(2 * half), out(128)],
    )


def shard_copies(table, shards, place, cols, sems):
    part = shards[0].shape[1]
    n = len(shards) // 2
    copies = []
    for c in range(2):
        refs = [(ref, i) for ref in shards[n * c : n * c + n] for i in range(ref.shape[0])]
        for i, (ref, at) in enumerate(refs):
            to = place(table[HALF + i], pl.ds(pl.multiple_of(table[ROWS + 16 * c + i], part), part))
            copies.append(
                pltpu.make_async_copy(ref.at[at, :, pl.ds(cols.start, cols.stop - cols.start)], to, sems.at[16 * c + i])
            )
    return copies


def piece_copies(table, pieces, to_ref, sems):
    copies = []
    own, on, back, far1, far2 = pieces
    cut, rows = far1.shape[0], own.shape[0]
    parts = (own, 0, 0, rows), (on, 1, 0, rows), (back, 3, 0, rows), (far1, 2, 0, cut), (far2, 2, cut, rows - cut)
    for i, (piece, hop, at, size) in enumerate(parts):
        to = to_ref.at[lax.rem(table[ZED] + hop, 4), pl.ds(at, size)]
        copies.append(pltpu.make_async_copy(piece, to, sems.at[i]))
    return copies


def front_kernel(
    table, *refs,
):
    shards, pieces, refs = refs[:10], refs[10:15], refs[15:]
    conv_ref, head_ref, ones_ref, tri_ref, w_ref, tok_ref, pre_ref, before_ref, act_ref, z_ref, *refs = refs
    cum_ref, state_ref, around, ext, buf, sems, piece_sems = refs
    k = pl.program_id(0)
    width = ones_ref.shape[1]
    half = width // 2

    @pl.when(k == 0)
    def _():
        place = lambda side, rows: w_ref.at[rows, pl.ds(pl.multiple_of(side * BLOCK, 128), BLOCK)]
        copies = shard_copies(table, shards, place, slice(0, BLOCK), sems)
        copies += piece_copies(table, pieces, around, piece_sems)
        for copy in copies:
            copy.start()
        for copy in copies:
            copy.wait()

    keep = table[KEEP + 2 * k + table[SIDE]].astype(F32)
    tok_ref[...] = around[k, 0:Q, :]
    ext[0:16, :] = around[table[PREV + k], Q:, :]
    ext[16:, :] = around[k, 0:Q, :]
    tok = ext[...]
    dt = jnp.zeros((Q, 128), F32)
    for i in range(2):
        proj = mm(tok, w_ref[:, BLOCK * i : BLOCK * (i + 1)])
        for to, size, at in ((half * i, half, 0), (width + NS * i, NS, half)):
            buf[0:8, to : to + size] = proj[8:16, at : at + size] * keep
            buf[8:, to : to + size] = proj[16:, at : at + size]
        dt = dt + proj[16:, half + NS :]
    pre_ref[...] = buf[8:, :]
    before_ref[...] = buf[0:8, :]
    run = conv_run(conv_ref, buf)
    act = (run * sigmoid(run)).astype(BF)
    act_ref[...] = act
    z = dt + head_ref[0:1, :]
    z_ref[...] = z
    step = softplus(z)
    cum = running_sum(tri_ref[...], step * head_ref[1:2, :])
    cum_ref[...] = cum
    ones = ones_ref[...]
    weigh = spread(step * jnp.exp(cum[Q - 1 :, :] - cum), ones)
    grown = (act[:, :width].astype(F32) * weigh).astype(BF)
    state_ref[0:NS, :] = mm_tn(act[:, width : width + NS], grown).astype(BF)
    last = spread(jnp.broadcast_to(jnp.exp(cum[Q - 1 :, :]), (16, 128)), ones)
    hi, low = split2(last)
    sub = lax.broadcasted_iota(jnp.int32, last.shape, 0)
    state_ref[NS:, :] = jnp.where(sub == 0, hi.astype(F32), low.astype(F32)).astype(BF)


BLOCK = 640


def front(table, shards, pieces, conv, head, ones, tri):
    rows, d = pieces[0].shape
    width = ones.shape[1]
    cols = width + 2 * NS
    return call(
        front_kernel, "conv_and_states", 4, table,
        [
            *[(a, None, None) for a in (*shards, *pieces)],
            all_of(conv), all_of(head), all_of(ones), all_of(tri),
        ],
        [
            out_all((d, 2 * BLOCK), BF), out_rows(4, d, BF),
            out_rows(4, cols, F32), out_rows(4, cols, F32, 8), out_rows(4, cols, BF),
            out_rows(4, 128, F32), out_rows(4, 128, F32), out_rows(4, width, BF, STATE_ROWS),
        ],
        [
            pltpu.VMEM((4, rows, d), BF), pltpu.VMEM((rows, d), BF), pltpu.VMEM((8 + Q, cols), F32),
            pltpu.SemaphoreType.DMA((32,)), pltpu.SemaphoreType.DMA((5,)),
        ],
    )


def within_kernel(table, act_ref, z_ref, cum_ref, chan_ref, ones_ref, mixed_ref):
    width = ones_ref.shape[1]
    act = act_ref[...]
    cum = cum_ref[...]
    x = act[:, :width].astype(F32)
    xs = x * spread(softplus(z_ref[...]), ones_ref[...])
    scores = mm_nt(act[:, width + NS :], act[:, width : width + NS])
    cum_row = cum.T
    lower = lower_ones()
    half = lanes((Q, 128)) < HD
    for p in range(width // 128):
        span = slice(128 * p, 128 * (p + 1))
        xp = xs[:, span]
        total = chan_ref[0:1, span] * x[:, span]
        for i in range(2):
            h = 2 * p + i
            diff = cum[:, h : h + 1] - cum_row[h : h + 1, :]
            mix = (scores * jnp.exp(jnp.where(lower, diff, -1e30))).astype(BF)
            total = total + mm(mix, jnp.where(half if i == 0 else ~half, xp, 0.0).astype(BF))
        mixed_ref[:, span] = total


def project_kernel(table, *refs):
    shards, pieces, refs = refs[:10], refs[10:15], refs[15:]
    tok_ref, wz_ref, wout_ref, cot_ref, gate_ref, hg_ref, around, sems, sems2, piece_sems = refs
    k = pl.program_id(0)
    width = gate_ref.shape[1]
    half = width // 2

    def copies(to_ref, at, sems):
        place = lambda side, rows: to_ref.at[rows, pl.ds(pl.multiple_of(side * half, 128), half)]
        return shard_copies(table, shards, place, slice(at, at + half), sems)

    @pl.when(k == 0)
    def _():
        all_copies = copies(wz_ref, BLOCK, sems) + copies(wout_ref, BLOCK + half, sems2)
        all_copies += piece_copies(table, pieces, around, piece_sems)
        for copy in all_copies:
            copy.start()
        for copy in all_copies:
            copy.wait()

    gate_ref[...] = mm(tok_ref[...], wz_ref[...])
    cot = around[k]
    cot_ref[...] = cot
    live = lax.broadcasted_iota(jnp.int32, (Q, width), 0) < table[LIVE + k]
    hg_ref[...] = jnp.where(live, mm(cot, wout_ref[...]), 0.0)


def project(table, shards, pieces, tokens):
    rows, d = pieces[0].shape
    width = shards[0].shape[2] - BLOCK
    return call(
        project_kernel, "project", 4, table,
        [*[(a, None, None) for a in (*shards, *pieces)], rows_of(tokens)],
        [
            out_all((d, width), BF), out_all((d, width), BF), out_rows(4, d, BF),
            out_rows(4, width, F32), out_rows(4, width, F32),
        ],
        [
            pltpu.VMEM((4, rows, d), BF), pltpu.SemaphoreType.DMA((32,)), pltpu.SemaphoreType.DMA((32,)),
            pltpu.SemaphoreType.DMA((5,)),
        ],
    )


def within(table, act, z, cum, chan, ones):
    return call(
        within_kernel, "ssd_within", 4, table,
        [rows_of(act), rows_of(z), rows_of(cum), all_of(chan), all_of(ones)],
        [out_rows(4, ones.shape[1], F32)],
    )[0]


def decay_of(state_ref):
    rows = state_ref[NS : NS + 8, :].astype(F32)
    return rows[0:1, :] + rows[1:2, :]


def through_kernel(
    table, within_ref, gate_ref, hg_ref, act_ref, cum_ref, own_ref, pair_ref, chan_ref, ones_ref,
    mixed_ref, sin_ref, sums_ref,
    state,
):
    k = pl.program_id(0)
    width = ones_ref.shape[1]
    first = table[SIDE] == 0

    @pl.when(k == 0)
    def _():
        state[...] = jnp.zeros_like(state)

    own, pair = own_ref[0:NS, :].astype(F32), pair_ref[0:NS, :].astype(F32)
    own_decay, pair_decay = decay_of(own_ref), decay_of(pair_ref)
    at_a = table[KEEP + 2 * k].astype(F32) * state[...]
    after_a = jnp.where(first, own_decay, pair_decay) * at_a + jnp.where(first, own, pair)
    at_b = table[KEEP + 2 * k + 1].astype(F32) * after_a
    state[...] = jnp.where(first, pair_decay, own_decay) * at_b + jnp.where(first, pair, own)
    carried = jnp.where(first, at_a, at_b).astype(BF)
    sin_ref[...] = carried

    grow = spread(jnp.exp(cum_ref[...]), ones_ref[...])
    mixed = within_ref[...] + mm(act_ref[...], carried) * grow
    mixed_ref[...] = mixed
    gate = gate_ref[...]
    gated = mixed * (gate * sigmoid(gate))
    one = jnp.ones((8, width), BF)
    square = sum(mm_nt(one, part) for part in split2(gated * gated))
    inner = sum(mm_nt(one, part) for part in split2(hg_ref[...] * chan_ref[1:2, :] * gated))
    sub = lax.broadcasted_iota(jnp.int32, (8, Q), 0)
    sums_ref[...] = jnp.where(sub == 0, square, inner)


def c_rows(act):
    return act, (Q, NS), lambda k, table: (k, act.shape[1] // NS - 1)


def through(table, mixed, gate, hg, act, cum, own, pair, chan, ones):
    width = ones.shape[1]
    return call(
        through_kernel, "ssd_through", 4, table,
        [
            rows_of(mixed), rows_of(gate), rows_of(hg), c_rows(act), rows_of(cum),
            rows_of(own, STATE_ROWS), rows_of(pair, STATE_ROWS), all_of(chan), all_of(ones),
        ],
        [
            out_rows(4, width, F32), out_rows(4, width, BF, NS),
            ((8, 4 * Q), F32, (8, Q), lambda k, table: (0, k)),
        ],
        [pltpu.VMEM((NS, width), F32)],
    )


def gate_back_kernel(
    table, hg_ref, mixed_ref, gate_ref, sums_ref, sums1, sums2, sums3, act_ref, cum_ref, chan_ref, ones_ref,
    hidden_ref, glow_ref, dy_ref, dstate_ref, ngg_ref, *, inner,
):
    k = pl.program_id(0)
    width = ones_ref.shape[1]

    @pl.when(k == 0)
    def _():
        ngg_ref[...] = jnp.zeros_like(ngg_ref)

    sums = (sums_ref[...] + sums1[...]) + (sums2[...] + sums3[...])
    scale_row = lax.rsqrt(sums[0:1, :] / inner + EPS)
    pull_row = scale_row * scale_row * scale_row * (sums[1:2, :] / inner)
    sub = lax.broadcasted_iota(jnp.int32, (128, Q), 0)
    cols = jnp.where(sub == 0, scale_row, jnp.where(sub == 1, pull_row, 0.0)).T
    scale = cols[:, 0:1]
    pull = cols[:, 1:2]
    hg = hg_ref[...]
    mixed = mixed_ref[...]
    gate = gate_ref[...]
    sg = sigmoid(gate)
    silu = gate * sg
    gated = mixed * silu
    normal = gated * scale
    gain = chan_ref[1:2, :]
    row = lax.broadcasted_iota(jnp.int32, (Q, width), 0)
    hidden_ref[...] = jnp.where(row < table[LIVE + k], normal * gain, 0.0).astype(BF)
    ngg_ref[0:1, :] += jnp.sum(hg * normal, axis=0, keepdims=True)
    gg = scale * gain * hg - gated * pull
    dy = gg * silu
    dy_ref[...] = dy
    glow_ref[...] = (gg * mixed * sg * (1.0 + gate * (1.0 - sg))).astype(BF)
    grow = spread(jnp.exp(cum_ref[...]), ones_ref[...])
    dstate_ref[...] = mm_tn(act_ref[...], (dy * grow).astype(BF)).astype(BF)


def gate_back(table, hg, mixed, gate, sums, act, cum, chan, ones, inner):
    width = ones.shape[1]
    return call(
        functools.partial(gate_back_kernel, inner=inner), "gate_back", 4, table,
        [
            rows_of(hg), rows_of(mixed), rows_of(gate), *[(a, (8, Q), lambda k, table: (0, k)) for a in sums],
            c_rows(act), rows_of(cum), all_of(chan), all_of(ones),
        ],
        [
            out_rows(4, width, BF), out_rows(4, width, BF), out_rows(4, width, F32), out_rows(4, width, BF, NS),
            out_all((8, width), F32),
        ],
    )


def backward_kernel(
    table, act_ref, pre_ref, before_ref, z_ref, cum_ref, sin_ref, dy_ref, mine_ref, theirs_ref, decay_ref,
    conv_ref, head_ref, chan_ref, ones_ref, tri_ref,
    low_ref, tail_ref, first_ref, convsum_ref, headsum_ref, skipsum_ref,
    carry, buf, *, heads,
):
    k = 3 - pl.program_id(0)
    width = heads * HD
    cols = width + 2 * NS
    side = table[SIDE]

    @pl.when(pl.program_id(0) == 0)
    def _():
        carry[...] = jnp.zeros_like(carry)
        convsum_ref[...] = jnp.zeros_like(convsum_ref)
        headsum_ref[...] = jnp.zeros_like(headsum_ref)
        skipsum_ref[...] = jnp.zeros_like(skipsum_ref)

    act = act_ref[...]
    x = act[:, :width].astype(F32)
    bmat = act[:, width : width + NS]
    cmat = act[:, width + NS :]
    z = z_ref[...]
    step = softplus(z)
    cum = cum_ref[...]
    ones = ones_ref[...]
    tri = tri_ref[...]
    step_x = spread(step, ones)
    grow_x, fade_x = decays(cum, ones)
    last_x = grow_x[Q - 1 :, :]
    xs = x * step_x
    xsb = xs.astype(BF)
    dy = dy_ref[...]

    mine = mine_ref[...].astype(F32)
    theirs = theirs_ref[...].astype(F32)
    pair_decay = decay_of(decay_ref)
    keep_a = table[KEEP + 2 * k].astype(F32)
    keep_b = table[KEEP + 2 * k + 1].astype(F32)
    after_b = carry[...]
    first = side == 0
    after_a = keep_b * (jnp.where(first, pair_decay, last_x) * after_b + jnp.where(first, theirs, mine))
    carry[...] = keep_a * (jnp.where(first, last_x, pair_decay) * after_a + jnp.where(first, mine, theirs))
    dstate = jnp.where(first, after_a, after_b)
    dstate_low = dstate.astype(BF)

    scores = mm_nt(cmat, bmat)
    cum_row = cum.T
    lower = lower_ones()
    lane = lanes((Q, 128))
    even = lane < HD
    sub = lax.broadcasted_iota(jnp.int32, (128, Q), 0)
    dscores = jnp.zeros((Q, Q), F32)
    rowsum = jnp.zeros((Q, 128), F32)
    colsum = jnp.zeros((128, Q), F32)
    parts = []
    for p in range(heads // 2):
        span = slice(128 * p, 128 * (p + 1))
        dyp = dy[:, span]
        part = jnp.zeros((Q, 128), F32)
        for i in range(2):
            h = 2 * p + i
            diff = cum[:, h : h + 1] - cum_row[h : h + 1, :]
            decay = jnp.exp(jnp.where(lower, diff, -1e30))
            mix = (scores * decay).astype(BF)
            dym = jnp.where(even if i == 0 else ~even, dyp, 0.0).astype(BF)
            grad = mm_nt(dym, xsb[:, span]) * decay
            dscores = dscores + grad
            grad = grad * scores
            rowsum = jnp.where(lane == h, jnp.sum(grad, axis=1, keepdims=True), rowsum)
            colsum = jnp.where(sub == h, jnp.sum(grad, axis=0, keepdims=True), colsum)
            part = part + mm_tn(mix, dym)
        parts.append(part)
    inside = jnp.concatenate(parts, axis=1)
    carried = sin_ref[...]
    dyg = (dy * grow_x).astype(BF)
    dsl = dscores.astype(BF)
    dc = mm(dsl, bmat) + mm_nt(dyg, carried)
    db = mm_tn(dsl, cmat) + mm_nt((xs * fade_x).astype(BF), dstate_low)
    passed = mm(cmat, carried) * grow_x
    later = mm(bmat, dstate_low) * fade_x
    q_passed = gather_heads(dy * passed, ones)
    q_later = gather_heads(x * later, ones)
    q_inside = gather_heads(x * inside, ones)
    hold = jnp.sum(dstate * carried.astype(F32), axis=0, keepdims=True) * last_x
    q_hold = gather_heads(jnp.broadcast_to(hold, (8, width)), ones)[0:1, :]
    dx = step_x * (inside + later) + chan_ref[0:1, :] * dy
    net = jnp.where(lane < LOW, q_passed + rowsum - colsum.T, 0.0)
    push = step * q_later
    drate = suffix_sum(tri, net) + running_sum(tri, push) - push + q_hold
    rate_of = head_ref[1:2, :]
    dstep = q_inside + q_later + drate * rate_of
    dz = jnp.where(lane < heads, dstep * sigmoid(z), 0.0)
    headsum_ref[0:1, :] += jnp.sum(dz, axis=0, keepdims=True)
    headsum_ref[1:2, :] += jnp.sum(drate * step * rate_of, axis=0, keepdims=True)
    skipsum_ref[0:1, :] += jnp.sum(dy * x, axis=0, keepdims=True)

    grad = jnp.concatenate([dx, db, dc], axis=1)
    buf[0:8, :] = before_ref[...]
    buf[8 : 8 + Q, :] = pre_ref[...]
    run = conv_run(conv_ref, buf)
    sg = sigmoid(run)
    dact = grad * (sg * (1.0 + run * (1.0 - sg)))
    for j in range(4):
        convsum_ref[3 - j : 4 - j, :] += jnp.sum(dact * buf[8 - j : 8 - j + Q, :], axis=0, keepdims=True)
    convsum_ref[4:5, :] += jnp.sum(dact, axis=0, keepdims=True)
    first_ref[...] = dact[0:8, :]
    buf[0:Q, :] = dact
    buf[Q : Q + 8, :] = jnp.zeros((8, cols), F32)
    dpre = conv_ref[3:4, :] * dact
    for j in range(1, 4):
        dpre = dpre + conv_ref[3 - j : 4 - j, :] * buf[j : j + Q, :]
    tail_ref[...] = dpre[Q - 8 :, :]
    half = width // 2
    for i in range(2):
        at = BLOCK * i
        low_ref[:, at : at + half] = dpre[:, half * i : half * (i + 1)].astype(BF)
        low_ref[:, at + half : at + half + NS] = dpre[:, width + NS * i : width + NS * (i + 1)].astype(BF)
        low_ref[:, at + half + NS : at + BLOCK] = dz.astype(BF)


def backward(table, act, pre, before, z, cum, sin, dy, mine, theirs, pair, conv, head, chan, ones, tri, heads):
    cols = act.shape[1]
    width = heads * HD

    def back(array, size=Q):
        return array, (size, array.shape[1]), lambda i, table: (3 - i, 0)

    def out_back(w, dtype, size=Q):
        return (4 * size, w), dtype, (size, w), lambda i, table: (3 - i, 0)

    return call(
        functools.partial(backward_kernel, heads=heads), "ssd_backward", 4, table,
        [
            back(act), back(pre), back(before, 8), back(z), back(cum), back(sin, NS), back(dy),
            back(mine, NS), back(theirs, NS), back(pair, STATE_ROWS),
            all_of(conv), all_of(head), all_of(chan), all_of(ones), all_of(tri),
        ],
        [
            out_back(2 * BLOCK, BF), out_back(cols, F32, 8), out_back(cols, F32, 8),
            out_all((8, cols), F32), out_all((8, 128), F32), out_all((8, width), F32),
        ],
        [pltpu.VMEM((NS, width), F32), pltpu.VMEM((8 + Q, cols), F32)],
    )


def mend_kernel(table, low_ref, tail_ref, later_ref, conv_ref, out_ref):
    k = pl.program_id(0)
    width = conv_ref.shape[1] - 2 * NS
    half = width // 2
    later = later_ref[...] * table[KEEP + 2 * k + table[SIDE] + 1].astype(F32)
    fixed = tail_ref[...]
    sub = lax.broadcasted_iota(jnp.int32, fixed.shape, 0)
    for j in range(1, 4):
        moved = pltpu.roll(later, 8 - j, 0)
        fixed = fixed + jnp.where(sub >= 8 - j, conv_ref[3 - j : 4 - j, :] * moved, 0.0)
    rows = low_ref[...].astype(F32)
    for i in range(2):
        at = BLOCK * i
        new = fixed[:, half * i : half * (i + 1)], fixed[:, width + NS * i : width + NS * (i + 1)]
        new = jnp.concatenate([new[0], new[1], rows[8:, at + half + NS : at + BLOCK]], axis=1)
        out_ref[:, at : at + BLOCK] = jnp.concatenate([rows[:8, at : at + BLOCK], new], axis=0).astype(BF)


def mend(table, low, tail, later, conv):
    cols = conv.shape[1]
    edge = pl.BlockSpec((16, 2 * BLOCK), lambda k, table: (k * (Q // 16) + Q // 16 - 1, 0))
    return pl.pallas_call(
        mend_kernel,
        grid_spec=pltpu.PrefetchScalarGridSpec(
            num_scalar_prefetch=1,
            grid=(4,),
            in_specs=[
                edge,
                pl.BlockSpec((8, cols), lambda k, table: (k, 0)),
                pl.BlockSpec((8, cols), lambda k, table: (jnp.minimum(k + table[SIDE], 3), 0)),
                pl.BlockSpec((8, cols), lambda k, table: (0, 0)),
            ],
            out_specs=[edge],
        ),
        out_shape=[jax.ShapeDtypeStruct(low.shape, BF)],
        input_output_aliases={1: 0},
        compiler_params=pltpu.CompilerParams(dimension_semantics=("arbitrary",), vmem_limit_bytes=VMEM_LIMIT),
        cost_estimate=CHEAP,
        name="mend_rows",
    )(table, low, tail, later, conv)[0]


def by_core(grad, first, i, mine_ref, other_ref, cols):
    part = mine_ref.shape[3]
    for p in range(2):
        a = grad[2 * p * part : (2 * p + 1) * part]
        b = grad[(2 * p + 1) * part : (2 * p + 2) * part]
        mine_ref[p, i, 0, :, cols] = jnp.where(first, a, b).astype(BF)
        other_ref[p, i, 0, :, cols] = jnp.where(first, b, a).astype(BF)


def row_dots(grad, w):
    prod = grad * up(w)
    prod = sum(prod[:, at : at + 128] for at in range(0, prod.shape[1], 128))
    one = jnp.ones((8, 128), BF)
    return sum(mm_nt(one, part) for part in split2(prod))


def early_kernel(table, tok_ref, cot_ref, w_ref, glow_ref, hidden_ref, mine_ref, other_ref, dots_ref):
    half = glow_ref.shape[1] // 2
    first = table[CORE] == 0
    for at, left, right in ((0, tok_ref, glow_ref), (half, cot_ref, hidden_ref)):
        grad = mm_tn(left[...], right[...])
        for i in range(2):
            by_core(grad[:, half * i : half * (i + 1)], first, i, mine_ref, other_ref, slice(at, at + half))
        if at == 0:
            dots_ref[...] = row_dots(grad, w_ref[...])


def late_kernel(
    table, tok_ref, w_ref, low_ref, dots_ref, convsum_ref, gain_ref, headsum_ref, skipsum_ref,
    mine_ref, other_ref, small_ref, dots,
):
    i = pl.program_id(0)
    grad = mm_tn(tok_ref[...], low_ref[...])
    for side in range(2):
        by_core(grad[:, BLOCK * side : BLOCK * (side + 1)], table[CORE] == 0, side, mine_ref, other_ref, slice(0, BLOCK))
    dots[i] = row_dots(grad, w_ref[...])

    @pl.when(i == 3)
    def _():
        width = gain_ref.shape[1]
        cols = convsum_ref.shape[1]
        sub = lax.broadcasted_iota(jnp.int32, (8, width), 0)
        other = jnp.where(sub == 5, gain_ref[0:1, :], jnp.where(sub == 6, skipsum_ref[0:1, :], 0.0))
        small_ref[:, :width] = jnp.where(sub < 5, convsum_ref[:, :width], other)
        sub = lax.broadcasted_iota(jnp.int32, (8, 128), 0)
        for h in range(2):
            at = slice(width + 128 * h, width + 128 * (h + 1))
            other = jnp.where(sub == 5, headsum_ref[h : h + 1, :], 0.0)
            small_ref[:, at] = jnp.where(sub < 5, convsum_ref[:, at], other)
        sub = lax.broadcasted_iota(jnp.int32, (8, 256), 0)
        size = dots.shape[2]
        flat = jnp.concatenate([dots[q] + dots_ref[:, size * q : size * (q + 1)] for q in range(4)], axis=1)
        rows = jnp.zeros((8, 256), F32)
        for r in range(flat.shape[1] // 256):
            rows = jnp.where(sub == r, flat[:, 256 * r : 256 * (r + 1)], rows)
        small_ref[:, cols:] = rows


def shard_outs(d, cols):
    part = d // 16
    out = ((4, 2, 2, part, cols), BF, (2, 2, 1, part, cols), lambda i, table: (i % 2, 0, i // 2, 0, 0))
    return [out, out]


def early_weights(table, tokens, cot, wz, glow, hidden):
    rows, d = tokens.shape
    width = glow.shape[1]
    columns = lambda a: (a, (rows, d // 4), lambda i, table: (0, i))
    return call(
        early_kernel, "early_weights", 4, table,
        [
            columns(tokens), columns(cot), (wz, (d // 4, width), lambda i, table: (i, 0)),
            all_of(glow), all_of(hidden),
        ],
        [*shard_outs(d, width), ((8, d), F32, (8, d // 4), lambda i, table: (0, i))],
    )


def late_weights(table, tokens, wx, low, dots, conv_sum, gain_sum, head_sum, skip_sum):
    rows, d = tokens.shape
    return call(
        late_kernel, "late_weights", 4, table,
        [
            (tokens, (rows, d // 4), lambda i, table: (0, i)),
            (wx, (d // 4, 2 * BLOCK), lambda i, table: (i, 0)),
            all_of(low), all_of(dots), all_of(conv_sum), all_of(gain_sum), all_of(head_sum), all_of(skip_sum),
        ],
        [*shard_outs(d, BLOCK), out_all((8, 2 * BLOCK), F32)],
        [pltpu.VMEM((4, 8, d // 4), F32)],
    )


def in_order(values, place):
    def at(i):
        hop = lax.rem(i + 4 - place, 4)
        return jnp.where(hop == 0, values[0], jnp.where(hop == 1, values[1], jnp.where(hop == 2, values[2], values[3])))

    return (at(0) + at(1)) + (at(2) + at(3))


def x_pack_kernel(table, mine_ref, other_ref, small_ref, small2_ref, far_ref, ahead_ref, behind_ref, own_ref, parts_ref):
    part = mine_ref.shape[3]
    total = small_ref[...] + small2_ref[...]
    parts = [jnp.concatenate([p[:, :BLOCK], p[:, BLOCK:]], axis=0) for p in (up(v) for v in split2(total))]
    parts = jnp.concatenate(parts, axis=0).astype(BF)
    parts_ref[...] = parts
    for hop, out in ((2, far_ref), (1, ahead_ref), (3, behind_ref), (0, own_ref)):
        i = lax.rem(table[EXE] + hop, 4)
        for y in range(4):
            v = up(mine_ref[i, y // 2, y % 2]) + up(other_ref[i, y // 2, y % 2])
            out[part * y : part * (y + 1), :] = v.astype(BF)
        if hop:
            out[4 * part :, :] = parts


def x_pack(table, mine, other, small, small2):
    part = mine.shape[3]
    rows = 4 * part
    return call(
        x_pack_kernel, "x_pack", 1, table,
        [all_of(mine), all_of(other), all_of(small), all_of(small2)],
        [
            *[out_all((rows + 32, BLOCK), BF) for _ in range(3)],
            out_all((rows, BLOCK), BF), out_all((32, BLOCK), BF),
        ],
    )


def y_pack_kernel(
    table, own_ref, far_ref, back_ref, on_ref, parts_ref, early_ref, efar_ref, eback_ref, eon_ref,
    one_ref, two_ref, three_ref, stay_ref, small_ref, late, early,
):
    part = stay_ref.shape[0]
    rows = 4 * part
    late[...] = up(own_ref[...]) + sum(up(v[0:rows, :]) for v in (far_ref, back_ref, on_ref))
    early[...] = sum(up(v[...]) for v in (early_ref, efar_ref, eback_ref, eon_ref))
    joined = lambda v, at: up(v[at : at + 16, :]) + up(v[at + 16 : at + 32, :])
    small = in_order(
        [joined(parts_ref, 0), joined(on_ref, rows), joined(far_ref, rows), joined(back_ref, rows)], table[EXE]
    )
    hi, low = split2(small)
    small_ref[:, :BLOCK] = hi
    small_ref[:, BLOCK:] = low
    half = BLOCK - NS - 128
    for hop, out in ((2, two_ref), (1, one_ref), (3, three_ref), (0, stay_ref)):
        to = pl.multiple_of(lax.rem(table[WYE] + hop, 4) * part, part)
        pair = pl.multiple_of(lax.rem(table[WYE] + hop + 2, 4) * part, part)
        out[0:part, :BLOCK] = late[pl.ds(to, part), :].astype(out.dtype)
        out[0:part, BLOCK : BLOCK + NS] = late[pl.ds(pair, part), half : half + NS].astype(out.dtype)
        out[0:part, BLOCK + NS :] = early[pl.ds(to, part), :].astype(out.dtype)
        if hop:
            out[part:, :BLOCK] = hi
            out[part:, BLOCK : 2 * BLOCK] = low
            out[part:, 2 * BLOCK :] = jnp.zeros((16, out.shape[1] - 2 * BLOCK), BF)


def y_pack(table, own, got, parts, early, early_got):
    rows = own.shape[0]
    part = rows // 4
    wide = BLOCK + NS + early.shape[1]
    return call(
        y_pack_kernel, "y_pack", 1, table,
        [all_of(a) for a in (own, *got, parts, early, *early_got)],
        [
            *[out_all((part + 16, wide), BF) for _ in range(3)],
            out_all((part, wide), F32), out_all((16, 2 * BLOCK), BF),
        ],
        [pltpu.VMEM((rows, BLOCK), F32), pltpu.VMEM(early.shape, F32)],
    )


def z_pack_kernel(
    table, stay_ref, one_ref, two_ref, three_ref, small_ref,
    x_ref, dt_ref, z_ref, out_ref, share_ref, chan_ref, head_ref,
):
    part = stay_ref.shape[0]
    half = x_ref.shape[1]
    got = one_ref, two_ref, three_ref
    total = stay_ref[...] + sum(up(v[0:part, :]) for v in got)
    x_ref[...] = total[:, :half]
    dt_ref[...] = total[:, half + NS : BLOCK]
    z_ref[...] = total[:, BLOCK + NS : BLOCK + NS + half]
    out_ref[...] = total[:, BLOCK + NS + half :]
    first = table[SIDE] == 0
    own, pair = total[:, half : half + NS], total[:, BLOCK : BLOCK + NS]
    share_ref[0:part, :NS] = jnp.where(first, own, pair)
    share_ref[0:part, NS:] = jnp.where(first, pair, own)
    joined = lambda v: up(v[:, :BLOCK]) + up(v[:, BLOCK : 2 * BLOCK])
    small = in_order([joined(small_ref[...])] + [joined(v[part:, :]) for v in got], table[WYE])
    rest = 2 * half - BLOCK
    width = jnp.concatenate([small[:8], small[8:, :rest]], axis=1)
    chan_ref[...] = jnp.where(first, width[:, :half], width[:, half:])
    head_ref[...] = small[8:, rest : rest + 256]
    share_ref[part : part + 8, :] = small[8:, rest : rest + 256]
    share_ref[part + 8 :, :] = small[8:, rest + 256 :]


def z_pack(table, stay, got, small):
    part = stay.shape[0]
    half = BLOCK - NS - 128
    out = lambda *shape: out_all(shape, F32)
    return call(
        z_pack_kernel, "z_pack", 1, table,
        [all_of(a) for a in (stay, *got, small)],
        [
            out(part, half), out(part, 128), out(part, half), out(part, half),
            out(part + 16, 256), out(8, half), out(8, 256),
        ],
    )


def finish_kernel(table, own_ref, on_ref, far_ref, back_ref, bc_ref, conv_ref, dots_ref):
    part = bc_ref.shape[0]
    total = in_order([v[...] for v in (own_ref, on_ref, far_ref, back_ref)], table[ZED])
    bc_ref[...] = total[:part]
    conv_ref[...] = total[part : part + 8]
    dots_ref[...] = total[part + 8 :]


def finish(table, own, on, far, back):
    out = lambda rows: out_all((rows, own.shape[1]), F32)
    return call(
        finish_kernel, "finish", 1, table, [all_of(a) for a in (own, on, far, back)],
        [out(own.shape[0] - 16), out(8), out(8)],
    )


def put_one(total, out_refs):
    for n, out_ref in enumerate(out_refs):

        @pl.when(pl.program_id(0) == n)
        def _(out_ref=out_ref):
            out_ref[...] = total.astype(BF)


def normed_kernel(order, glow_ref, low_ref, wz_ref, wx_ref, *out_refs):
    put_one(mm_nt(low_ref[...], wx_ref[...]) + mm_nt(glow_ref[...], wz_ref[...]), out_refs)


def branch_kernel(order, hidden_ref, wout_ref, *out_refs):
    put_one(mm_nt(hidden_ref[...], wout_ref[...]), out_refs)


def picked(a):
    return a, (Q, a.shape[1]), lambda i, order: (order[i], 0)


def normed_part(order, glow, low, wz, wx):
    n = order.shape[0]
    return call(
        normed_kernel, "normed_grad", n, order, [picked(glow), picked(low), all_of(wz), all_of(wx)],
        [out_all((Q, wx.shape[0]), BF)] * n,
    )


def branch_part(order, hidden, wout):
    n = order.shape[0]
    return call(
        branch_kernel, "branch", n, order, [picked(hidden), all_of(wout)], [out_all((Q, wout.shape[0]), BF)] * n
    )


DP = ("yl", "x", "core")
RIGHT = [(i, (i + 1) % 4) for i in range(4)]
LEFT = [(i, (i + 3) % 4) for i in range(4)]
NEAR = [(i, i ^ 1) for i in range(4)]
FAR = [(i, i ^ 2) for i in range(4)]
SWAP = [(0, 1), (1, 0)]


def around_y(step):
    place = lambda y: y % 2 * 2 + y // 2
    return [(place(y), place((y + step) % 4)) for y in range(4)]


def pick(array, index, axis):
    return lax.dynamic_index_in_dim(array, index, axis, keepdims=False)


def up(v):
    return v.astype(F32)


def ring_sends(far, ahead, behind, axis):
    return (
        lax.ppermute(far, axis, FAR),
        lax.ppermute(ahead, axis, RIGHT),
        lax.ppermute(behind, axis, LEFT),
    )


def y_sends(shard):
    send = lambda step: lax.ppermute(shard(step), ("yl", "yh"), around_y(step))
    two, one, three = send(2), send(1), send(3)
    return three, two, one


def ring_far(back, on, axis, cut):
    return lax.ppermute(back[:cut], axis, RIGHT), lax.ppermute(on[cut:], axis, LEFT)


def neighbours(v, axis):
    return lax.ppermute(v, axis, RIGHT), lax.ppermute(v, axis, LEFT)


def with_other_core(arrays):
    return (*arrays, *[lax.ppermute(a, "core", SWAP) for a in arrays])


def local(
    x_in,
    cotangent,
    seq_lengths,
    in_gain,
    w_z,
    w_x,
    w_dt,
    w_bc,
    conv_wx,
    conv_bx,
    conv_wbc,
    conv_bbc,
    dt_bias,
    a_log,
    d_skip,
    gnorm_gain,
    w_out,
):
    rows, d = x_in.shape
    own_heads = dt_bias.shape[0]
    heads = 2 * own_heads
    half = own_heads * HD
    width = 2 * half
    cols = width + 2 * NS
    shard = w_z.shape[0]
    yl, x, core, z, yh = (lax.axis_index(a) for a in ("yl", "x", "core", "z", "yh"))
    dp = (yl * 4 + x) * 2 + core
    side = yh == 0

    hops = (0, 3, 1, 2)
    x_tail = lax.ppermute(x_in[rows - 16 :], "yh", SWAP)
    resid = x_in.astype(F32)
    inverse = lax.rsqrt(jnp.mean(resid * resid, axis=-1, keepdims=True) + EPS)
    longer = up(jnp.concatenate([x_in, x_tail]))
    longer_inverse = lax.rsqrt(jnp.mean(longer * longer, axis=-1, keepdims=True) + EPS)
    ext = (longer * longer_inverse * in_gain).astype(BF)

    order = lax.optimization_barrier
    own_w, _ = order((pack(yh[None], w_x, w_bc, w_dt, w_z, w_out), x_tail))
    one, two, three = y_sends(lambda step: own_w)
    x_own = jnp.stack([own_w, three, one, two])
    x_near = neighbours(x_own, "x")
    t_near = neighbours(ext, "z")
    seq_lengths, conv_bx, dt_bias, _ = order((seq_lengths, conv_bx, dt_bias, t_near[0]))

    lane_gap = jnp.zeros((LOW - heads,), F32)
    apart = jnp.zeros((own_heads,), F32)

    def by_lane(v):
        v = jnp.where(side, jnp.concatenate([v, apart]), jnp.concatenate([apart, v]))
        return jnp.concatenate([v, lane_gap, v, jnp.zeros((128 - LOW - heads,), F32)])

    params = jnp.stack(
        [conv_wx[0], conv_wx[1], conv_wx[2], conv_wx[3], conv_bx, jnp.repeat(d_skip, HD), gnorm_gain]
        + [jnp.concatenate([by_lane(dt_bias), by_lane(-jnp.exp(a_log)), jnp.zeros((half - 256,), F32)])]
    )
    pair_params = lax.ppermute(params, "yh", SWAP)
    lengths = seq_lengths[0]
    spans = (lengths + Q - 1) // Q * Q
    starts = jnp.cumsum(spans) - spans

    def stretch(c):
        at = c * Q
        going, living = 0, 0
        for i in range(lengths.shape[0]):
            inside = (at >= starts[i]) & (at < starts[i] + spans[i])
            going = going + (inside & (at > starts[i])).astype(jnp.int32)
            living = living + jnp.where(inside, jnp.clip(starts[i] + lengths[i] - at, 0, Q), 0)
        return going, living

    slot = jnp.arange(WYE + 1, dtype=jnp.int32)
    i = (slot - HALF) % 16
    hop = lambda k: jnp.where(k == 1, 3, jnp.where(k == 2, 1, jnp.where(k == 3, 2, 0)))
    shard_y, shard_x = (yh * 2 + yl + hop(i % 4)) % 4, (x + hop(i // 4)) % 4
    shard_core = jnp.where(slot < ROWS + 16, core, 1 - core)
    table = jnp.where(slot < SIDE, stretch(slot)[0], yh)
    table = jnp.where(slot >= LIVE, stretch(2 * (slot - LIVE) + yh)[1], table)
    table = jnp.where(slot >= PREV, (slot - PREV + 3 + yh) % 4, table)
    table = jnp.where(slot >= HALF, shard_y // 2, table)
    table = jnp.where(slot >= ROWS, ((shard_y % 2 * 4 + shard_x) * 2 + shard_core) * shard, table)
    table = jnp.where(slot >= CORE, core, table)
    table = jnp.where(slot >= ZED, z, table)
    table = jnp.where(slot >= EXE, x, table)
    table = jnp.where(slot >= WYE, yh * 2 + yl, table)

    ones = expander(heads)
    tri = jnp.asarray(np.tril(np.ones((Q, Q), np.float32)), BF)

    x_near, t_near = order((x_near, t_near))
    x_far, t_far = ring_far(*x_near, "x", 2), ring_far(*t_near, "z", 144)
    conv, chan, head = prep(table, params, pair_params, conv_wbc, conv_bbc[None])
    t_far, cot = order((t_far, cotangent))
    c_near = neighbours(cot, "z")
    shards = with_other_core((x_own, *x_near, *x_far))

    wx, tokens, pre, before, act, zs, cum, states = front(
        table, shards, (ext, t_near[1], t_near[0], *t_far), conv, head, ones, tri
    )
    pair = lax.ppermute(states, "yh", SWAP)
    act, c_near = order((act, c_near))
    c_far = ring_far(*c_near, "z", 128)
    mixed = within(table, act, zs, cum, chan, ones)
    wz, wout, cot, gate, hg = project(table, shards, (cotangent, c_near[1], c_near[0], *c_far), tokens)
    mixed, sin, sums = through(table, mixed, gate, hg, act, cum, states, pair, chan, ones)
    sums = sums, *ring_sends(sums, sums, sums, "z")
    hidden, gate_low, dy, dstates, gain_sum = gate_back(
        table, hg, mixed, gate, sums, act, cum, chan, ones, 4 * width
    )
    pair_dstates = lax.ppermute(dstates, "yh", SWAP)

    early, early_other, early_dots = early_weights(table, tokens, cot, wz, gate_low, hidden)
    around_z = (z + jnp.array([2, 1, 3, 0], jnp.int32)) % 4
    branch = branch_part(around_z, hidden, wout)
    pair_dstates, early, early_other, branch = order((pair_dstates, early, early_other, branch))
    early_other = lax.ppermute(early_other, "core", SWAP)
    branch_got = ring_sends(*branch[:3], "z")
    early = [
        (up(pick(early, (x + k) % 4, 0)) + up(pick(early_other, (x + k) % 4, 0))).astype(BF).reshape(4 * shard, width)
        for k in (2, 1, 3, 0)
    ]
    dy, early = order((dy, early))
    early_near = lax.ppermute(early[1], "x", RIGHT), lax.ppermute(early[2], "x", LEFT)
    own_live = stretch(2 * z + yh)[1]
    live_rows = jnp.arange(rows, dtype=jnp.int32)[:, None] < own_live

    low, low_tail, first, conv_sum, head_sum, skip_sum = backward(
        table, act, pre, before, zs, cum, sin, dy, dstates, pair_dstates, pair,
        conv, head, chan, ones, tri, heads,
    )
    first, branch_got, early_near, early[0] = order((first, branch_got, early_near, early[0]))
    later, early_far = order((lax.ppermute(first, "yh", SWAP), early[0]))
    early_far = lax.ppermute(early_far, "x", FAR)
    low = mend(table, low, low_tail, later, conv)
    late, late_other, small = late_weights(
        table, tokens, wx, low, early_dots, conv_sum, gain_sum, head_sum, skip_sum
    )
    low, around_z, late_other, small, early_far = order((low, around_z, late_other, small, early_far))
    late_other, small_other = lax.ppermute(late_other, "core", SWAP), lax.ppermute(small, "core", SWAP)
    far = normed_part(around_z[:1], gate_low, low, wz, wx)[0]
    far, late_other, small_other = order((far, late_other, small_other))
    *sends, late, parts = x_pack(table, late, late_other, small, small_other)
    sends, around_z, far = order((sends, around_z, far))
    got = ring_sends(*sends, "x")
    from_far = lax.ppermute(far, "z", FAR)
    around_z, _ = order((around_z, got[1]))
    ahead, behind, own = normed_part(around_z[1:], gate_low, low, wz, wx)
    branch = up(branch[3]) + sum(up(v) for v in branch_got)
    output = (resid + jnp.where(live_rows, branch, 0.0)).astype(BF)
    got, from_far, ahead, behind, own, output = order((got, from_far, ahead, behind, own, output))
    one, two, three, stay, small = y_pack(table, late, got, parts, early[3], (early_far, *early_near))
    got = y_sends(lambda step: {1: one, 2: two, 3: three}[step])
    from_ahead, from_behind = lax.ppermute(ahead, "z", RIGHT), lax.ppermute(behind, "z", LEFT)
    normed_grad = up(own) + up(from_far) + up(from_ahead) + up(from_behind)

    projected = jnp.sum(normed_grad * in_gain * resid, axis=-1, keepdims=True) / d
    x_grad = inverse * in_gain * normed_grad - resid * inverse**3 * projected + up(cotangent)

    w_x_grad, w_dt_grad, w_z_grad, w_out_grad, shared, own, heads_own = z_pack(table, stay, got, small)
    head_at = lambda k: lax.dynamic_slice_in_dim(heads_own[5], 128 * k + yh * own_heads, own_heads, 0)
    w_dt_grad = lax.dynamic_slice_in_dim(w_dt_grad, yh * own_heads, own_heads, 1)
    skip_grad = jnp.sum(own[6].reshape(own_heads, HD), axis=1)
    far, back, on = ring_sends(shared, shared, shared, "z")
    far, back, on, x_grad, w_dt_grad, skip_grad = order((far, back, on, x_grad, w_dt_grad, skip_grad))
    w_bc_grad, conv_bc_grad, dots = finish(table, shared, on, far, back)
    dots = dots[: d // 256]
    each = d // 128
    at = dp * shard + (2 * z + yh) * each
    in_gain_grad = lax.dynamic_slice_in_dim(dots.reshape(d), at, each, 0) / lax.dynamic_slice_in_dim(in_gain, at, each, 0)
    return (
        output,
        x_grad,
        in_gain_grad,
        w_z_grad,
        w_x_grad,
        w_dt_grad,
        w_bc_grad,
        own[:4],
        own[4],
        conv_bc_grad[:4],
        conv_bc_grad[4],
        head_at(0),
        head_at(1),
        skip_grad,
        own[5],
        w_out_grad,
    )


def solution(mesh):
    grid = Mesh(mesh.devices.reshape(2, 4, 2, 4, 2), DP + ("z", "yh"))
    tensor = ("z", "yh")
    tokens, weight, channels = P(DP + tensor, None), P(DP, tensor), P(tensor)
    return jax.shard_map(
        local,
        mesh=grid,
        in_specs=(
            tokens,
            tokens,
            P(DP, None),
            P(),
            weight,
            weight,
            weight,
            P(DP, None),
            P(None, tensor),
            channels,
            P(),
            P(),
            channels,
            channels,
            channels,
            channels,
            weight,
        ),
        out_specs=(
            tokens,
            tokens,
            P(DP + tensor),
            weight,
            weight,
            weight,
            P(DP, None),
            P(None, tensor),
            channels,
            P(),
            P(),
            channels,
            channels,
            channels,
            channels,
            weight,
        ),
        check_vma=False,
    )
```

```python
import functools

import jax
import jax.numpy as jnp
import numpy as np
from jax import lax
from jax.experimental import pallas as pl
from jax.experimental.pallas import tpu as pltpu
from jax.sharding import Mesh
from jax.sharding import PartitionSpec as P

Q = 256
HD = 64
NS = 128
EPS = 1e-05
F32 = jnp.float32
BF = jnp.bfloat16
VMEM_LIMIT = 56 * 1024 * 1024


def mm(a, b):
    return lax.dot_general(a, b, (((1,), (0,)), ((), ())), preferred_element_type=F32)


def mm_nt(a, b):
    return lax.dot_general(a, b, (((1,), (1,)), ((), ())), preferred_element_type=F32)


def mm_tn(a, b):
    return lax.dot_general(a, b, (((0,), (0,)), ((), ())), preferred_element_type=F32)


def split3(v):
    hi = v.astype(BF)
    rest = v - hi.astype(F32)
    mid = rest.astype(BF)
    low = (rest - mid.astype(F32)).astype(BF)
    return hi, mid, low


def split2(v):
    hi = v.astype(BF)
    return hi, (v - hi.astype(F32)).astype(BF)


def lanes(shape):
    return lax.broadcasted_iota(jnp.int32, shape, len(shape) - 1)


def lower_ones():
    rows = lax.broadcasted_iota(jnp.int32, (Q, Q), 0)
    return rows >= lanes((Q, Q))


def expander(heads):
    row = np.arange(128)[:, None]
    head = np.arange(heads * HD)[None, :] // HD
    return jnp.asarray(((row == head) | (row == head + LOW)).astype(np.float32), BF)


LOW = 16


def spread(v, ones):
    hi, low = split2(v)
    return mm(jnp.where(lanes(v.shape) < LOW, hi.astype(F32), low.astype(F32)).astype(BF), ones)


def gather_heads(v, ones):
    hi, low = split2(v)
    return mm_nt(hi, ones) + mm_nt(low, ones)


def softplus(z):
    return jnp.maximum(z, 0.0) + jnp.log1p(jnp.exp(-jnp.abs(z)))


def sigmoid(v):
    return 1.0 / (1.0 + jnp.exp(-v))


def running_sum(tri, v):
    hi, mid, low = split3(v)
    return mm(tri, hi) + mm(tri, mid) + mm(tri, low)


def suffix_sum(tri, v):
    hi, mid, low = split3(v)
    return mm_tn(tri, hi) + mm_tn(tri, mid) + mm_tn(tri, low)


KEEP = 0
SIDE = 9
LIVE = 10
PREV = 14
HALF = 18
ROWS = 34
CORE = 66
ZED, EXE, WYE = 67, 68, 69
GAIN = 70
OWN = 71
STATE_ROWS = NS + 16


CHEAP = pl.CostEstimate(flops=1000, bytes_accessed=1000, transcendentals=0)


def call(kernel, name, grid, table, ins, outs, scratch=()):
    def spec(block, index):
        if block is None:
            return pl.BlockSpec(memory_space=pl.ANY)
        return pl.BlockSpec(block, index)

    return pl.pallas_call(
        kernel,
        grid_spec=pltpu.PrefetchScalarGridSpec(
            num_scalar_prefetch=1,
            grid=(grid,),
            in_specs=[spec(block, index) for _, block, index in ins],
            out_specs=[spec(block, index) for _, _, block, index in outs],
            scratch_shapes=list(scratch),
        ),
        out_shape=[jax.ShapeDtypeStruct(shape, dtype) for shape, dtype, _, _ in outs],
        compiler_params=pltpu.CompilerParams(dimension_semantics=("arbitrary",), vmem_limit_bytes=VMEM_LIMIT),
        cost_estimate=CHEAP,
        name=name,
    )(table, *[array for array, _, _ in ins])


def rows_of(array, size=Q):
    return array, (size, array.shape[1]), lambda k, table: (k, 0)


def all_of(array):
    return array, array.shape, lambda k, table: (0,) * array.ndim


def out_rows(count, width, dtype, size=Q):
    return (count * size, width), dtype, (size, width), lambda k, table: (k, 0)


def out_all(shape, dtype):
    return shape, dtype, shape, lambda k, table: (0,) * len(shape)


def decays(cum, ones):
    grow = spread(jnp.exp(cum), ones)
    fade = spread(jnp.exp(cum[Q - 1 :, :] - cum), ones)
    return grow, fade


def conv_run(conv_ref, buf):
    run = conv_ref[4:5, :] + conv_ref[3:4, :] * buf[8 : 8 + Q, :]
    for j in range(1, 4):
        run = run + conv_ref[3 - j : 4 - j, :] * buf[8 - j : 8 - j + Q, :]
    return run


def table_kernel(place, lengths_ref, out_ref):
    yl, x, core, z, yh, shard = (place[i] for i in range(6))
    starts, start = [], 0
    for i in range(lengths_ref.shape[1]):
        length = lengths_ref[0, i]
        span = lax.div(length + (Q - 1), Q) * Q
        starts.append((start, length, span))
        start = start + span

    def stretch(c):
        at = c * Q
        going, living = 0, 0
        for start, length, span in starts:
            inside = (at >= start) & (at < start + span)
            going = going + jnp.where(inside & (at > start), 1, 0)
            living = living + jnp.where(inside, jnp.clip(start + length - at, 0, Q), 0)
        return going, living

    for c in range(9):
        out_ref[KEEP + c] = stretch(c)[0]
    out_ref[SIDE] = yh
    for k in range(4):
        out_ref[LIVE + k] = stretch(2 * k + yh)[1]
        out_ref[PREV + k] = lax.rem(k + 3 + yh, 4)
    hops = (0, 3, 1, 2)
    for i in range(16):
        shard_y = lax.rem(yh * 2 + yl + hops[i % 4], 4)
        shard_x = lax.rem(x + hops[i // 4], 4)
        row = (lax.rem(shard_y, 2) * 4 + shard_x) * 2
        out_ref[HALF + i] = lax.div(shard_y, 2)
        out_ref[ROWS + i] = (row + core) * shard
        out_ref[ROWS + 16 + i] = (row + 1 - core) * shard
    for at, value in ((CORE, core), (ZED, z), (EXE, x), (WYE, yh * 2 + yl), (GAIN, ((yl * 4 + x) * 2 + core) * 8 + 2 * z + yh)):
        out_ref[at] = value
    out_ref[OWN] = stretch(2 * z + yh)[1]


def make_table(place, lengths):
    return pl.pallas_call(
        table_kernel,
        grid_spec=pltpu.PrefetchScalarGridSpec(
            num_scalar_prefetch=1,
            grid=(1,),
            in_specs=[pl.BlockSpec(memory_space=pltpu.SMEM)],
            out_specs=pl.BlockSpec(memory_space=pltpu.SMEM),
        ),
        out_shape=jax.ShapeDtypeStruct((OWN + 1,), jnp.int32),
        cost_estimate=CHEAP,
        name="table",
    )(place, lengths)


def pack_kernel(table, x_ref, bc_ref, dt_ref, z_ref, w_ref, out_ref):
    half = x_ref.shape[1]
    heads = dt_ref.shape[1]
    row = lax.broadcasted_iota(jnp.int32, (heads, 128), 0) + heads * table[0]
    lane = lanes((heads, 128))
    out_ref[:, :half] = x_ref[...]
    out_ref[:, half : half + NS] = jnp.where(table[0] == 0, up(bc_ref[:, :NS]), up(bc_ref[:, NS:])).astype(BF)
    place = ((lane == row) | (lane == row + LOW)).astype(F32).astype(BF)
    out_ref[:, half + NS : BLOCK] = mm(dt_ref[...], place).astype(BF)
    out_ref[:, BLOCK : BLOCK + half] = z_ref[...]
    out_ref[:, BLOCK + half :] = w_ref[...]


def pack(side, w_x, w_bc, w_dt, w_z, w_out):
    shape = (w_x.shape[0], 3 * w_x.shape[1] + NS + 128)
    return call(
        pack_kernel, "pack_shard", 1, side,
        [all_of(w_x), all_of(w_bc), all_of(w_dt), all_of(w_z), all_of(w_out)], [out_all(shape, BF)],
    )[0]


def prep_kernel(table, own_ref, pair_ref, wbc_ref, bbc_ref, conv_ref, chan_ref, head_ref):
    half = own_ref.shape[1]
    width = 2 * half
    own, pair = own_ref[...], pair_ref[...]
    first = table[SIDE] == 0
    for i in range(2):
        both = jnp.where(first, own, pair) if i == 0 else jnp.where(first, pair, own)
        span = slice(half * i, half * (i + 1))
        conv_ref[:, span] = both
        chan_ref[0:1, span] = both[5:6, :]
        chan_ref[1:2, span] = both[6:7, :]
    sub = lax.broadcasted_iota(jnp.int32, (8, 2 * NS), 0)
    rows = jnp.where(sub == 4, bbc_ref[...], 0.0)
    for j in range(4):
        rows = jnp.where(sub == j, wbc_ref[j : j + 1, :], rows)
    conv_ref[:, width:] = rows
    for i in range(2):
        at = slice(128 * i, 128 * (i + 1))
        head_ref[i : i + 1, :] = own[7:8, at] + pair[7:8, at]


def prep(table, own, pair, conv_wbc, conv_bbc):
    half = own.shape[1]
    out = lambda w: out_all((8, w), F32)
    return call(
        prep_kernel, "prep", 1, table,
        [all_of(own), all_of(pair), all_of(conv_wbc), all_of(conv_bbc)],
        [out(2 * half + 2 * NS), out(2 * half), out(128)],
    )


def shard_copies(table, shards, place, cols, sems):
    part = shards[0].shape[1]
    n = len(shards) // 2
    copies = []
    for c in range(2):
        refs = [(ref, i) for ref in shards[n * c : n * c + n] for i in range(ref.shape[0])]
        for i, (ref, at) in enumerate(refs):
            to = place(table[HALF + i], pl.ds(pl.multiple_of(table[ROWS + 16 * c + i], part), part))
            copies.append(
                pltpu.make_async_copy(ref.at[at, :, pl.ds(cols.start, cols.stop - cols.start)], to, sems.at[16 * c + i])
            )
    return copies


def piece_copies(table, pieces, to_ref, sems):
    copies, at = [], 0
    for i, piece in enumerate(pieces):
        hop = (0, 1, 3, 2)[min(i, 3)]
        at = at + pieces[i - 1].shape[0] if i > 3 else 0
        to = to_ref.at[lax.rem(table[ZED] + hop, 4), pl.ds(at, piece.shape[0])]
        copies.append(pltpu.make_async_copy(piece, to, sems.at[i]))
    return copies


def front_kernel(
    table, *refs,
):
    shards, pieces, refs = refs[:10], refs[10:14], refs[14:]
    conv_ref, head_ref, ones_ref, tri_ref, w_ref, tok_ref, tail_ref, pre_ref, before_ref, act_ref, *refs = refs
    z_ref, cum_ref, state_ref, around, ext, buf, sems, piece_sems = refs
    k = pl.program_id(0)
    width = ones_ref.shape[1]
    half = width // 2

    @pl.when(k == 0)
    def _():
        place = lambda side, rows: w_ref.at[rows, pl.ds(pl.multiple_of(side * BLOCK, 128), BLOCK)]
        copies = shard_copies(table, shards, place, slice(0, BLOCK), sems)
        copies += piece_copies(table, pieces, around, piece_sems)
        for copy in copies:
            copy.start()
        for copy in copies:
            copy.wait()

    keep = table[KEEP + 2 * k + table[SIDE]].astype(F32)
    tok_ref[...] = around[k, 0:Q, :]
    ext[0:16, :] = around[table[PREV + k], Q:, :]
    tail_ref[...] = ext[0:16, :]
    ext[16:, :] = around[k, 0:Q, :]
    tok = ext[...]
    dt = jnp.zeros((Q, 128), F32)
    for i in range(2):
        proj = mm(tok, w_ref[:, BLOCK * i : BLOCK * (i + 1)])
        for to, size, at in ((half * i, half, 0), (width + NS * i, NS, half)):
            buf[0:8, to : to + size] = proj[8:16, at : at + size] * keep
            buf[8:, to : to + size] = proj[16:, at : at + size]
        dt = dt + proj[16:, half + NS :]
    pre_ref[...] = buf[8:, :]
    before_ref[...] = buf[0:8, :]
    run = conv_run(conv_ref, buf)
    act = (run * sigmoid(run)).astype(BF)
    act_ref[...] = act
    z = dt + head_ref[0:1, :]
    z_ref[...] = z
    step = softplus(z)
    cum = running_sum(tri_ref[...], step * head_ref[1:2, :])
    cum_ref[...] = cum
    ones = ones_ref[...]
    weigh = spread(step * jnp.exp(cum[Q - 1 :, :] - cum), ones)
    grown = (act[:, :width].astype(F32) * weigh).astype(BF)
    state_ref[0:NS, :] = mm_tn(act[:, width : width + NS], grown).astype(BF)
    last = spread(jnp.broadcast_to(jnp.exp(cum[Q - 1 :, :]), (16, 128)), ones)
    hi, low = split2(last)
    sub = lax.broadcasted_iota(jnp.int32, last.shape, 0)
    state_ref[NS:, :] = jnp.where(sub == 0, hi.astype(F32), low.astype(F32)).astype(BF)


BLOCK = 640


def front(table, shards, pieces, conv, head, ones, tri):
    rows, d = pieces[0].shape
    width = ones.shape[1]
    cols = width + 2 * NS
    return call(
        front_kernel, "conv_and_states", 4, table,
        [
            *[(a, None, None) for a in (*shards, *pieces)],
            all_of(conv), all_of(head), all_of(ones), all_of(tri),
        ],
        [
            out_all((d, 2 * BLOCK), BF), out_rows(4, d, BF), out_rows(4, d, BF, 16),
            out_rows(4, cols, F32), out_rows(4, cols, F32, 8), out_rows(4, cols, BF),
            out_rows(4, 128, F32), out_rows(4, 128, F32), out_rows(4, width, BF, STATE_ROWS),
        ],
        [
            pltpu.VMEM((4, rows, d), BF), pltpu.VMEM((rows, d), BF), pltpu.VMEM((8 + Q, cols), F32),
            pltpu.SemaphoreType.DMA((32,)), pltpu.SemaphoreType.DMA((4,)),
        ],
    )


def within_kernel(table, act_ref, z_ref, cum_ref, chan_ref, ones_ref, mixed_ref):
    width = ones_ref.shape[1]
    act = act_ref[...]
    cum = cum_ref[...]
    x = act[:, :width].astype(F32)
    xs = x * spread(softplus(z_ref[...]), ones_ref[...])
    scores = mm_nt(act[:, width + NS :], act[:, width : width + NS])
    cum_row = cum.T
    lower = lower_ones()
    half = lanes((Q, 128)) < HD
    for p in range(width // 128):
        span = slice(128 * p, 128 * (p + 1))
        xp = xs[:, span]
        total = chan_ref[0:1, span] * x[:, span]
        for i in range(2):
            h = 2 * p + i
            diff = cum[:, h : h + 1] - cum_row[h : h + 1, :]
            mix = (scores * jnp.exp(jnp.where(lower, diff, -1e30))).astype(BF)
            total = total + mm(mix, jnp.where(half if i == 0 else ~half, xp, 0.0).astype(BF))
        mixed_ref[:, span] = total


def project_kernel(table, *refs):
    shards, pieces, refs = refs[:10], refs[10:15], refs[15:]
    tok_ref, wz_ref, wout_ref, cot_ref, gate_ref, hg_ref, around, sems, sems2, piece_sems = refs
    k = pl.program_id(0)
    width = gate_ref.shape[1]
    half = width // 2

    def copies(to_ref, at, sems):
        place = lambda side, rows: to_ref.at[rows, pl.ds(pl.multiple_of(side * half, 128), half)]
        return shard_copies(table, shards, place, slice(at, at + half), sems)

    def rest():
        return copies(wout_ref, BLOCK + half, sems2) + piece_copies(table, pieces, around, piece_sems)

    @pl.when(k == 0)
    def _():
        for copy in copies(wz_ref, BLOCK, sems) + rest():
            copy.start()
        for copy in copies(wz_ref, BLOCK, sems):
            copy.wait()

    gate_ref[...] = mm(tok_ref[...], wz_ref[...])

    @pl.when(k == 0)
    def _():
        for copy in rest():
            copy.wait()

    cot = around[k]
    cot_ref[...] = cot
    live = lax.broadcasted_iota(jnp.int32, (Q, width), 0) < table[LIVE + k]
    hg_ref[...] = jnp.where(live, mm(cot, wout_ref[...]), 0.0)


def project(table, shards, pieces, tokens):
    rows, d = pieces[0].shape
    width = shards[0].shape[2] - BLOCK
    return call(
        project_kernel, "project", 4, table,
        [*[(a, None, None) for a in (*shards, *pieces)], rows_of(tokens)],
        [
            out_all((d, width), BF), out_all((d, width), BF), out_rows(4, d, BF),
            out_rows(4, width, F32), out_rows(4, width, F32),
        ],
        [
            pltpu.VMEM((4, rows, d), BF), pltpu.SemaphoreType.DMA((32,)), pltpu.SemaphoreType.DMA((32,)),
            pltpu.SemaphoreType.DMA((5,)),
        ],
    )


def within(table, act, z, cum, chan, ones):
    return call(
        within_kernel, "ssd_within", 4, table,
        [rows_of(act), rows_of(z), rows_of(cum), all_of(chan), all_of(ones)],
        [out_rows(4, ones.shape[1], F32)],
    )[0]


def decay_of(state_ref):
    rows = state_ref[NS : NS + 8, :].astype(F32)
    return rows[0:1, :] + rows[1:2, :]


def through_kernel(
    table, within_ref, gate_ref, hg_ref, act_ref, cum_ref, own_ref, pair_ref, chan_ref, ones_ref,
    mixed_ref, sin_ref, sums_ref,
    state,
):
    k = pl.program_id(0)
    width = ones_ref.shape[1]
    first = table[SIDE] == 0

    @pl.when(k == 0)
    def _():
        state[...] = jnp.zeros_like(state)

    own, pair = own_ref[0:NS, :].astype(F32), pair_ref[0:NS, :].astype(F32)
    own_decay, pair_decay = decay_of(own_ref), decay_of(pair_ref)
    at_a = table[KEEP + 2 * k].astype(F32) * state[...]
    after_a = jnp.where(first, own_decay, pair_decay) * at_a + jnp.where(first, own, pair)
    at_b = table[KEEP + 2 * k + 1].astype(F32) * after_a
    state[...] = jnp.where(first, pair_decay, own_decay) * at_b + jnp.where(first, pair, own)
    carried = jnp.where(first, at_a, at_b).astype(BF)
    sin_ref[...] = carried

    grow = spread(jnp.exp(cum_ref[...]), ones_ref[...])
    mixed = within_ref[...] + mm(act_ref[...], carried) * grow
    mixed_ref[...] = mixed
    gate = gate_ref[...]
    gated = mixed * (gate * sigmoid(gate))
    one = jnp.ones((8, width), BF)
    square = sum(mm_nt(one, part) for part in split2(gated * gated))
    inner = sum(mm_nt(one, part) for part in split2(hg_ref[...] * chan_ref[1:2, :] * gated))
    sub = lax.broadcasted_iota(jnp.int32, (8, Q), 0)
    sums_ref[...] = jnp.where(sub == 0, square, inner)


def c_rows(act):
    return act, (Q, NS), lambda k, table: (k, act.shape[1] // NS - 1)


def through(table, mixed, gate, hg, act, cum, own, pair, chan, ones):
    width = ones.shape[1]
    return call(
        through_kernel, "ssd_through", 4, table,
        [
            rows_of(mixed), rows_of(gate), rows_of(hg), c_rows(act), rows_of(cum),
            rows_of(own, STATE_ROWS), rows_of(pair, STATE_ROWS), all_of(chan), all_of(ones),
        ],
        [
            out_rows(4, width, F32), out_rows(4, width, BF, NS),
            ((8, 4 * Q), F32, (8, Q), lambda k, table: (0, k)),
        ],
        [pltpu.VMEM((NS, width), F32)],
    )


def gate_back_kernel(
    table, hg_ref, mixed_ref, gate_ref, sums_ref, sums1, sums2, sums3, act_ref, cum_ref, chan_ref, ones_ref,
    hidden_ref, glow_ref, dy_ref, dstate_ref, ngg_ref, *, inner,
):
    k = pl.program_id(0)
    width = ones_ref.shape[1]

    @pl.when(k == 0)
    def _():
        ngg_ref[...] = jnp.zeros_like(ngg_ref)

    sums = (sums_ref[...] + sums1[...]) + (sums2[...] + sums3[...])
    scale_row = lax.rsqrt(sums[0:1, :] / inner + EPS)
    pull_row = scale_row * scale_row * scale_row * (sums[1:2, :] / inner)
    sub = lax.broadcasted_iota(jnp.int32, (128, Q), 0)
    cols = jnp.where(sub == 0, scale_row, jnp.where(sub == 1, pull_row, 0.0)).T
    scale = cols[:, 0:1]
    pull = cols[:, 1:2]
    hg = hg_ref[...]
    mixed = mixed_ref[...]
    gate = gate_ref[...]
    sg = sigmoid(gate)
    silu = gate * sg
    gated = mixed * silu
    normal = gated * scale
    gain = chan_ref[1:2, :]
    row = lax.broadcasted_iota(jnp.int32, (Q, width), 0)
    hidden_ref[...] = jnp.where(row < table[LIVE + k], normal * gain, 0.0).astype(BF)
    ngg_ref[0:1, :] += jnp.sum(hg * normal, axis=0, keepdims=True)
    gg = scale * gain * hg - gated * pull
    dy = gg * silu
    dy_ref[...] = dy
    glow_ref[...] = (gg * mixed * sg * (1.0 + gate * (1.0 - sg))).astype(BF)
    grow = spread(jnp.exp(cum_ref[...]), ones_ref[...])
    dstate_ref[...] = mm_tn(act_ref[...], (dy * grow).astype(BF)).astype(BF)


def gate_back(table, hg, mixed, gate, sums, act, cum, chan, ones, inner):
    width = ones.shape[1]
    return call(
        functools.partial(gate_back_kernel, inner=inner), "gate_back", 4, table,
        [
            rows_of(hg), rows_of(mixed), rows_of(gate), *[(a, (8, Q), lambda k, table: (0, k)) for a in sums],
            c_rows(act), rows_of(cum), all_of(chan), all_of(ones),
        ],
        [
            out_rows(4, width, BF), out_rows(4, width, BF), out_rows(4, width, F32), out_rows(4, width, BF, NS),
            out_all((8, width), F32),
        ],
    )


def backward_kernel(
    table, act_ref, pre_ref, before_ref, z_ref, cum_ref, sin_ref, dy_ref, mine_ref, theirs_ref, decay_ref,
    conv_ref, head_ref, chan_ref, ones_ref, tri_ref,
    low_ref, fix_ref, convsum_ref, headsum_ref, skipsum_ref,
    carry, buf, *, heads,
):
    k = 3 - pl.program_id(0)
    width = heads * HD
    cols = width + 2 * NS
    side = table[SIDE]

    @pl.when(pl.program_id(0) == 0)
    def _():
        carry[...] = jnp.zeros_like(carry)
        convsum_ref[...] = jnp.zeros_like(convsum_ref)
        headsum_ref[...] = jnp.zeros_like(headsum_ref)
        skipsum_ref[...] = jnp.zeros_like(skipsum_ref)

    act = act_ref[...]
    x = act[:, :width].astype(F32)
    bmat = act[:, width : width + NS]
    cmat = act[:, width + NS :]
    z = z_ref[...]
    step = softplus(z)
    cum = cum_ref[...]
    ones = ones_ref[...]
    tri = tri_ref[...]
    step_x = spread(step, ones)
    grow_x, fade_x = decays(cum, ones)
    last_x = grow_x[Q - 1 :, :]
    xs = x * step_x
    xsb = xs.astype(BF)
    dy = dy_ref[...]

    mine = mine_ref[...].astype(F32)
    theirs = theirs_ref[...].astype(F32)
    pair_decay = decay_of(decay_ref)
    keep_a = table[KEEP + 2 * k].astype(F32)
    keep_b = table[KEEP + 2 * k + 1].astype(F32)
    after_b = carry[...]
    first = side == 0
    after_a = keep_b * (jnp.where(first, pair_decay, last_x) * after_b + jnp.where(first, theirs, mine))
    carry[...] = keep_a * (jnp.where(first, last_x, pair_decay) * after_a + jnp.where(first, mine, theirs))
    dstate = jnp.where(first, after_a, after_b)
    dstate_low = dstate.astype(BF)

    scores = mm_nt(cmat, bmat)
    cum_row = cum.T
    lower = lower_ones()
    lane = lanes((Q, 128))
    even = lane < HD
    sub = lax.broadcasted_iota(jnp.int32, (128, Q), 0)
    dscores = jnp.zeros((Q, Q), F32)
    rowsum = jnp.zeros((Q, 128), F32)
    colsum = jnp.zeros((128, Q), F32)
    parts = []
    for p in range(heads // 2):
        span = slice(128 * p, 128 * (p + 1))
        dyp = dy[:, span]
        part = jnp.zeros((Q, 128), F32)
        for i in range(2):
            h = 2 * p + i
            diff = cum[:, h : h + 1] - cum_row[h : h + 1, :]
            decay = jnp.exp(jnp.where(lower, diff, -1e30))
            mix = (scores * decay).astype(BF)
            dym = jnp.where(even if i == 0 else ~even, dyp, 0.0).astype(BF)
            grad = mm_nt(dym, xsb[:, span]) * decay
            dscores = dscores + grad
            grad = grad * scores
            rowsum = jnp.where(lane == h, jnp.sum(grad, axis=1, keepdims=True), rowsum)
            colsum = jnp.where(sub == h, jnp.sum(grad, axis=0, keepdims=True), colsum)
            part = part + mm_tn(mix, dym)
        parts.append(part)
    inside = jnp.concatenate(parts, axis=1)
    carried = sin_ref[...]
    dyg = (dy * grow_x).astype(BF)
    dsl = dscores.astype(BF)
    dc = mm(dsl, bmat) + mm_nt(dyg, carried)
    db = mm_tn(dsl, cmat) + mm_nt((xs * fade_x).astype(BF), dstate_low)
    passed = mm(cmat, carried) * grow_x
    later = mm(bmat, dstate_low) * fade_x
    q_passed = gather_heads(dy * passed, ones)
    q_later = gather_heads(x * later, ones)
    q_inside = gather_heads(x * inside, ones)
    hold = jnp.sum(dstate * carried.astype(F32), axis=0, keepdims=True) * last_x
    q_hold = gather_heads(jnp.broadcast_to(hold, (8, width)), ones)[0:1, :]
    dx = step_x * (inside + later) + chan_ref[0:1, :] * dy
    net = jnp.where(lane < LOW, q_passed + rowsum - colsum.T, 0.0)
    push = step * q_later
    drate = suffix_sum(tri, net) + running_sum(tri, push) - push + q_hold
    rate_of = head_ref[1:2, :]
    dstep = q_inside + q_later + drate * rate_of
    dz = jnp.where(lane < heads, dstep * sigmoid(z), 0.0)
    headsum_ref[0:1, :] += jnp.sum(dz, axis=0, keepdims=True)
    headsum_ref[1:2, :] += jnp.sum(drate * step * rate_of, axis=0, keepdims=True)
    skipsum_ref[0:1, :] += jnp.sum(dy * x, axis=0, keepdims=True)

    grad = jnp.concatenate([dx, db, dc], axis=1)
    buf[0:8, :] = before_ref[...]
    buf[8 : 8 + Q, :] = pre_ref[...]
    run = conv_run(conv_ref, buf)
    sg = sigmoid(run)
    dact = grad * (sg * (1.0 + run * (1.0 - sg)))
    for j in range(4):
        convsum_ref[3 - j : 4 - j, :] += jnp.sum(dact * buf[8 - j : 8 - j + Q, :], axis=0, keepdims=True)
    convsum_ref[4:5, :] += jnp.sum(dact, axis=0, keepdims=True)
    buf[0:Q, :] = dact
    buf[Q : Q + 8, :] = jnp.zeros((8, cols), F32)
    dpre = conv_ref[3:4, :] * dact
    for j in range(1, 4):
        dpre = dpre + conv_ref[3 - j : 4 - j, :] * buf[j : j + Q, :]
    half = width // 2
    for i in range(2):
        at = BLOCK * i
        low_ref[:, at : at + half] = dpre[:, half * i : half * (i + 1)].astype(BF)
        low_ref[:, at + half : at + half + NS] = dpre[:, width + NS * i : width + NS * (i + 1)].astype(BF)
        low_ref[:, at + half + NS : at + BLOCK] = dz.astype(BF)
    begin = dact[0:8, :] * table[KEEP + 2 * k + side].astype(F32)
    sub = lax.broadcasted_iota(jnp.int32, begin.shape, 0)
    fix = jnp.zeros_like(begin)
    for j in range(1, 4):
        fix = fix + jnp.where(sub >= 8 - j, conv_ref[3 - j : 4 - j, :] * pltpu.roll(begin, 8 - j, 0), 0.0)
    fix = jnp.concatenate([jnp.zeros_like(fix), fix], axis=0)
    for i in range(2):
        at = BLOCK * i
        fix_ref[:, at : at + half] = fix[:, half * i : half * (i + 1)].astype(BF)
        fix_ref[:, at + half : at + half + NS] = fix[:, width + NS * i : width + NS * (i + 1)].astype(BF)
        fix_ref[:, at + half + NS : at + BLOCK] = jnp.zeros((16, 128), BF)


def backward(table, act, pre, before, z, cum, sin, dy, mine, theirs, pair, conv, head, chan, ones, tri, heads):
    cols = act.shape[1]
    width = heads * HD

    def back(array, size=Q):
        return array, (size, array.shape[1]), lambda i, table: (3 - i, 0)

    def out_back(w, dtype, size=Q):
        return (4 * size, w), dtype, (size, w), lambda i, table: (3 - i, 0)

    return call(
        functools.partial(backward_kernel, heads=heads), "ssd_backward", 4, table,
        [
            back(act), back(pre), back(before, 8), back(z), back(cum), back(sin, NS), back(dy),
            back(mine, NS), back(theirs, NS), back(pair, STATE_ROWS),
            all_of(conv), all_of(head), all_of(chan), all_of(ones), all_of(tri),
        ],
        [
            out_back(2 * BLOCK, BF), out_back(2 * BLOCK, BF, 16),
            out_all((8, cols), F32), out_all((8, 128), F32), out_all((8, width), F32),
        ],
        [pltpu.VMEM((NS, width), F32), pltpu.VMEM((8 + Q, cols), F32)],
    )


def by_core(grad, first, i, mine_ref, other_ref, cols):
    part = mine_ref.shape[3]
    for p in range(2):
        a = grad[2 * p * part : (2 * p + 1) * part]
        b = grad[(2 * p + 1) * part : (2 * p + 2) * part]
        mine_ref[p, i, 0, :, cols] = jnp.where(first, a, b).astype(BF)
        other_ref[p, i, 0, :, cols] = jnp.where(first, b, a).astype(BF)


def row_dots(grad, w):
    prod = grad * up(w)
    prod = sum(prod[:, at : at + 128] for at in range(0, prod.shape[1], 128))
    one = jnp.ones((8, 128), BF)
    return sum(mm_nt(one, part) for part in split2(prod))


def early_kernel(table, tok_ref, cot_ref, w_ref, glow_ref, hidden_ref, mine_ref, other_ref, dots_ref):
    half = glow_ref.shape[1] // 2
    first = table[CORE] == 0
    for at, left, right in ((0, tok_ref, glow_ref), (half, cot_ref, hidden_ref)):
        grad = mm_tn(left[...], right[...])
        for i in range(2):
            by_core(grad[:, half * i : half * (i + 1)], first, i, mine_ref, other_ref, slice(at, at + half))
        if at == 0:
            dots_ref[...] = row_dots(grad, w_ref[...])


def late_kernel(
    table, tok_ref, tail_ref, w_ref, low_ref, fix_ref, dots_ref, convsum_ref, gain_ref, headsum_ref, skipsum_ref,
    mine_ref, other_ref, small_ref, dots,
):
    i = pl.program_id(0)
    grad = mm_tn(tok_ref[...], low_ref[...]) + mm_tn(tail_ref[...], fix_ref[...])
    for side in range(2):
        by_core(grad[:, BLOCK * side : BLOCK * (side + 1)], table[CORE] == 0, side, mine_ref, other_ref, slice(0, BLOCK))
    dots[i] = row_dots(grad, w_ref[...])

    @pl.when(i == 3)
    def _():
        width = gain_ref.shape[1]
        cols = convsum_ref.shape[1]
        sub = lax.broadcasted_iota(jnp.int32, (8, width), 0)
        other = jnp.where(sub == 5, gain_ref[0:1, :], jnp.where(sub == 6, skipsum_ref[0:1, :], 0.0))
        small_ref[:, :width] = jnp.where(sub < 5, convsum_ref[:, :width], other)
        sub = lax.broadcasted_iota(jnp.int32, (8, 128), 0)
        for h in range(2):
            at = slice(width + 128 * h, width + 128 * (h + 1))
            other = jnp.where(sub == 5, headsum_ref[h : h + 1, :], 0.0)
            small_ref[:, at] = jnp.where(sub < 5, convsum_ref[:, at], other)
        sub = lax.broadcasted_iota(jnp.int32, (8, 256), 0)
        size = dots.shape[2]
        flat = jnp.concatenate([dots[q] + dots_ref[:, size * q : size * (q + 1)] for q in range(4)], axis=1)
        rows = jnp.zeros((8, 256), F32)
        for r in range(flat.shape[1] // 256):
            rows = jnp.where(sub == r, flat[:, 256 * r : 256 * (r + 1)], rows)
        small_ref[:, cols:] = rows


def shard_outs(d, cols):
    part = d // 16
    out = ((4, 2, 2, part, cols), BF, (2, 2, 1, part, cols), lambda i, table: (i % 2, 0, i // 2, 0, 0))
    return [out, out]


def early_weights(table, tokens, cot, wz, glow, hidden):
    rows, d = tokens.shape
    width = glow.shape[1]
    columns = lambda a: (a, (rows, d // 4), lambda i, table: (0, i))
    return call(
        early_kernel, "early_weights", 4, table,
        [
            columns(tokens), columns(cot), (wz, (d // 4, width), lambda i, table: (i, 0)),
            all_of(glow), all_of(hidden),
        ],
        [*shard_outs(d, width), ((8, d), F32, (8, d // 4), lambda i, table: (0, i))],
    )


def late_weights(table, tokens, tails, wx, low, fix, dots, conv_sum, gain_sum, head_sum, skip_sum):
    rows, d = tokens.shape
    return call(
        late_kernel, "late_weights", 4, table,
        [
            (tokens, (rows, d // 4), lambda i, table: (0, i)),
            (tails, (tails.shape[0], d // 4), lambda i, table: (0, i)),
            (wx, (d // 4, 2 * BLOCK), lambda i, table: (i, 0)),
            all_of(low), all_of(fix), all_of(dots), all_of(conv_sum), all_of(gain_sum), all_of(head_sum), all_of(skip_sum),
        ],
        [*shard_outs(d, BLOCK), out_all((8, 2 * BLOCK), F32)],
        [pltpu.VMEM((4, 8, d // 4), F32)],
    )


def in_order(values, place):
    def at(i):
        hop = lax.rem(i + 4 - place, 4)
        return jnp.where(hop == 0, values[0], jnp.where(hop == 1, values[1], jnp.where(hop == 2, values[2], values[3])))

    return (at(0) + at(1)) + (at(2) + at(3))


def x_pack_kernel(table, mine_ref, other_ref, small_ref, small2_ref, far_ref, ahead_ref, behind_ref, own_ref, parts_ref):
    part = mine_ref.shape[3]
    total = small_ref[...] + small2_ref[...]
    parts = [jnp.concatenate([p[:, :BLOCK], p[:, BLOCK:]], axis=0) for p in (up(v) for v in split2(total))]
    parts = jnp.concatenate(parts, axis=0).astype(BF)
    parts_ref[...] = parts
    for hop, out in ((2, far_ref), (1, ahead_ref), (3, behind_ref), (0, own_ref)):
        i = lax.rem(table[EXE] + hop, 4)
        for y in range(4):
            v = up(mine_ref[i, y // 2, y % 2]) + up(other_ref[i, y // 2, y % 2])
            out[part * y : part * (y + 1), :] = v.astype(BF)
        if hop:
            out[4 * part :, :] = parts


def x_pack(table, mine, other, small, small2):
    part = mine.shape[3]
    rows = 4 * part
    return call(
        x_pack_kernel, "x_pack", 1, table,
        [all_of(mine), all_of(other), all_of(small), all_of(small2)],
        [
            *[out_all((rows + 32, BLOCK), BF) for _ in range(3)],
            out_all((rows, BLOCK), BF), out_all((32, BLOCK), BF),
        ],
    )


def y_pack_kernel(
    table, own_ref, far_ref, back_ref, on_ref, parts_ref, early,
    one_ref, two_ref, three_ref, stay_ref, small_ref, late,
):
    part = stay_ref.shape[0]
    rows = 4 * part
    late[...] = up(own_ref[...]) + sum(up(v[0:rows, :]) for v in (far_ref, back_ref, on_ref))
    joined = lambda v, at: up(v[at : at + 16, :]) + up(v[at + 16 : at + 32, :])
    small = in_order(
        [joined(parts_ref, 0), joined(on_ref, rows), joined(far_ref, rows), joined(back_ref, rows)], table[EXE]
    )
    hi, low = split2(small)
    small_ref[:, :BLOCK] = hi
    small_ref[:, BLOCK:] = low
    half = BLOCK - NS - 128
    for hop, out in ((2, two_ref), (1, one_ref), (3, three_ref), (0, stay_ref)):
        to = pl.multiple_of(lax.rem(table[WYE] + hop, 4) * part, part)
        pair = pl.multiple_of(lax.rem(table[WYE] + hop + 2, 4) * part, part)
        out[0:part, :BLOCK] = late[pl.ds(to, part), :].astype(out.dtype)
        out[0:part, BLOCK : BLOCK + NS] = late[pl.ds(pair, part), half : half + NS].astype(out.dtype)
        out[0:part, BLOCK + NS :] = early[pl.ds(to, part), :].astype(out.dtype)
        if hop:
            out[part:, :BLOCK] = hi
            out[part:, BLOCK : 2 * BLOCK] = low
            out[part:, 2 * BLOCK :] = jnp.zeros((16, out.shape[1] - 2 * BLOCK), BF)


def y_pack(table, own, got, parts, early):
    rows = own.shape[0]
    part = rows // 4
    wide = BLOCK + NS + early.shape[1]
    return call(
        y_pack_kernel, "y_pack", 1, table,
        [all_of(a) for a in (own, *got, parts, early)],
        [
            *[out_all((part + 16, wide), BF) for _ in range(3)],
            out_all((part, wide), F32), out_all((16, 2 * BLOCK), BF),
        ],
        [pltpu.VMEM((rows, BLOCK), F32)],
    )


def z_pack_kernel(
    table, stay_ref, one_ref, two_ref, three_ref, small_ref,
    x_ref, dt_ref, z_ref, out_ref, share_ref, taps_ref, offset_ref, gain_ref, skip_ref, bias_ref, rate_ref,
):
    part = stay_ref.shape[0]
    half = x_ref.shape[1]
    got = one_ref, two_ref, three_ref
    total = stay_ref[...] + sum(up(v[0:part, :]) for v in got)
    x_ref[...] = total[:, :half]
    heads = dt_ref.shape[1]
    step = total[:, half + NS : BLOCK]
    dt_ref[...] = jnp.where(table[SIDE] == 0, step[:, :heads], step[:, heads : 2 * heads])
    z_ref[...] = total[:, BLOCK + NS : BLOCK + NS + half]
    out_ref[...] = total[:, BLOCK + NS + half :]
    first = table[SIDE] == 0
    own, pair = total[:, half : half + NS], total[:, BLOCK : BLOCK + NS]
    share_ref[0:part, :NS] = jnp.where(first, own, pair)
    share_ref[0:part, NS:] = jnp.where(first, pair, own)
    joined = lambda v: up(v[:, :BLOCK]) + up(v[:, BLOCK : 2 * BLOCK])
    small = in_order([joined(small_ref[...])] + [joined(v[part:, :]) for v in got], table[WYE])
    rest = 2 * half - BLOCK
    width = jnp.concatenate([small[:8], small[8:, :rest]], axis=1)
    chan = jnp.where(first, width[:, :half], width[:, half:])
    taps_ref[...] = chan[0:4]
    offset_ref[...] = chan[4:5]
    gain_ref[...] = chan[5:6]
    heads = bias_ref.shape[1]
    one = jnp.where(lax.broadcasted_iota(jnp.int32, (128, half), 0) == lanes((128, half)) // HD, 1.0, 0.0).astype(BF)
    skip_ref[...] = sum(mm_nt(part, one) for part in split3(chan))[6:7, :heads]
    for ref, at in ((bias_ref, rest), (rate_ref, rest + 128)):
        row = small[13:14, at : at + 128]
        ref[...] = jnp.where(first, row[:, :heads], row[:, heads : 2 * heads])
    share_ref[part : part + 8, :] = small[8:, rest : rest + 256]
    share_ref[part + 8 :, :] = small[8:, rest + 256 :]


def z_pack(table, stay, got, small):
    part = stay.shape[0]
    half = BLOCK - NS - 128
    out = lambda *shape: out_all(shape, F32)
    return call(
        z_pack_kernel, "z_pack", 1, table,
        [all_of(a) for a in (stay, *got, small)],
        [
            out(part, half), out(part, half // HD), out(part, half), out(part, half), out(part + 16, 256),
            out(4, half), out(1, half), out(1, half), out(1, half // HD), out(1, half // HD), out(1, half // HD),
        ],
    )


def finish_kernel(table, own_ref, on_ref, far_ref, back_ref, gain_ref, bc_ref, taps_ref, offset_ref, ingain_ref):
    part = bc_ref.shape[0]
    total = in_order([v[...] for v in (own_ref, on_ref, far_ref, back_ref)], table[ZED])
    bc_ref[...] = total[:part]
    taps_ref[...] = total[part : part + 4]
    offset_ref[...] = total[part + 4 : part + 5]
    d = gain_ref.shape[1]
    each = ingain_ref.shape[1]
    dots = jnp.concatenate([total[part + 8 + r : part + 9 + r] for r in range(d // 256)], axis=1)
    quotient = jnp.broadcast_to(dots / gain_ref[...], (8, d))
    ingain_ref[...] = pltpu.roll(quotient, lax.rem(d - table[GAIN] * each, d), 1)[0:1, :each]


def finish(table, own, on, far, back, gain):
    width = own.shape[1]
    d = gain.shape[1]
    out = lambda *shape: out_all(shape, F32)
    return call(
        finish_kernel, "finish", 1, table, [all_of(a) for a in (own, on, far, back, gain)],
        [out(own.shape[0] - 16, width), out(4, width), out(1, width), out(1, d // 128)],
    )


def put_one(total, out_refs):
    for n, out_ref in enumerate(out_refs):

        @pl.when(pl.program_id(0) == n)
        def _(out_ref=out_ref):
            out_ref[...] = total.astype(BF)


def normed_kernel(order, glow_ref, low_ref, fix_ref, wz_ref, wx_ref, *refs):
    *out_refs, ext = refs
    ext[0:Q, :] = low_ref[...]
    ext[Q:, :] = fix_ref[...]
    total = mm_nt(ext[...], wx_ref[...])
    put_one(jnp.concatenate([total[:Q] + mm_nt(glow_ref[...], wz_ref[...]), total[Q:]], axis=0), out_refs)


def branch_kernel(order, hidden_ref, wout_ref, *out_refs):
    put_one(mm_nt(hidden_ref[...], wout_ref[...]), out_refs)


def picked(a):
    return a, (Q, a.shape[1]), lambda i, order: (order[i], 0)


def normed_part(order, glow, low, fix, wz, wx):
    n = order.shape[0]
    return call(
        normed_kernel, "normed_grad", n, order,
        [picked(glow), picked(low), (fix, (16, fix.shape[1]), lambda i, order: (order[i], 0)), all_of(wz), all_of(wx)],
        [out_all((Q + 16, wx.shape[0]), BF)] * n,
        [pltpu.VMEM((Q + 16, low.shape[1]), BF)],
    )


def branch_part(order, hidden, wout):
    n = order.shape[0]
    return call(
        branch_kernel, "branch", n, order, [picked(hidden), all_of(wout)], [out_all((Q, wout.shape[0]), BF)] * n
    )


DP = ("yl", "x", "core")
RIGHT = [(i, (i + 1) % 4) for i in range(4)]
LEFT = [(i, (i + 3) % 4) for i in range(4)]
NEAR = [(i, i ^ 1) for i in range(4)]
FAR = [(i, i ^ 2) for i in range(4)]
SWAP = [(0, 1), (1, 0)]


def around_y(step):
    place = lambda y: y % 2 * 2 + y // 2
    return [(place(y), place((y + step) % 4)) for y in range(4)]


def pick(array, index, axis):
    return lax.dynamic_index_in_dim(array, index, axis, keepdims=False)


def up(v):
    return v.astype(F32)


def ring_sends(far, ahead, behind, axis):
    return (
        lax.ppermute(far, axis, FAR),
        lax.ppermute(ahead, axis, RIGHT),
        lax.ppermute(behind, axis, LEFT),
    )


def y_sends(shard):
    send = lambda step: lax.ppermute(shard(step), ("yl", "yh"), around_y(step))
    two, one, three = send(2), send(1), send(3)
    return three, two, one


def ring_far(back, on, axis, cut):
    return lax.ppermute(back[:cut], axis, RIGHT), lax.ppermute(on[cut:], axis, LEFT)


def neighbours(v, axis):
    return lax.ppermute(v, axis, RIGHT), lax.ppermute(v, axis, LEFT)


def with_other_core(arrays):
    return (*arrays, *[lax.ppermute(a, "core", SWAP) for a in arrays])


def local(
    x_in,
    cotangent,
    seq_lengths,
    in_gain,
    w_z,
    w_x,
    w_dt,
    w_bc,
    conv_wx,
    conv_bx,
    conv_wbc,
    conv_bbc,
    dt_bias,
    a_log,
    d_skip,
    gnorm_gain,
    w_out,
):
    rows, d = x_in.shape
    own_heads = dt_bias.shape[0]
    heads = 2 * own_heads
    half = own_heads * HD
    width = 2 * half
    cols = width + 2 * NS
    shard = w_z.shape[0]
    yl, x, core, z, yh = (lax.axis_index(a) for a in ("yl", "x", "core", "z", "yh"))
    dp = (yl * 4 + x) * 2 + core
    side = yh == 0

    hops = (0, 3, 1, 2)
    order = lax.optimization_barrier
    x_tail = lax.ppermute(x_in[rows - 16 :], "yh", SWAP)
    own_w, x_tail = order((pack(yh[None], w_x, w_bc, w_dt, w_z, w_out), x_tail))
    resid = x_in.astype(F32)
    inverse = lax.rsqrt(jnp.mean(resid * resid, axis=-1, keepdims=True) + EPS)
    longer = up(jnp.concatenate([x_in, x_tail]))
    longer_inverse = lax.rsqrt(jnp.mean(longer * longer, axis=-1, keepdims=True) + EPS)
    ext = (longer * longer_inverse * in_gain).astype(BF)

    one, two, three = y_sends(lambda step: own_w)
    x_own = jnp.stack([own_w, three, one, two])
    x_near = neighbours(x_own, "x")
    t_near = neighbours(ext, "z")
    x_near, t_near = order((x_near, t_near))
    x_far, t_far = ring_far(*x_near, "x", 2), lax.ppermute(t_near[0], "z", RIGHT)

    seq_lengths, conv_bx, dt_bias, _ = order((seq_lengths, conv_bx, dt_bias, t_near[0]))
    place = jnp.stack([yl, x, core, z, yh, jnp.full((), shard, yh.dtype)]).astype(jnp.int32)
    table = make_table(place, seq_lengths)
    lane_gap = jnp.zeros((LOW - heads,), F32)
    apart = jnp.zeros((own_heads,), F32)

    def by_lane(v):
        v = jnp.where(side, jnp.concatenate([v, apart]), jnp.concatenate([apart, v]))
        return jnp.concatenate([v, lane_gap, v, jnp.zeros((128 - LOW - heads,), F32)])

    params = jnp.stack(
        [conv_wx[0], conv_wx[1], conv_wx[2], conv_wx[3], conv_bx, jnp.repeat(d_skip, HD), gnorm_gain]
        + [jnp.concatenate([by_lane(dt_bias), by_lane(-jnp.exp(a_log)), jnp.zeros((half - 256,), F32)])]
    )
    pair_params = lax.ppermute(params, "yh", SWAP)
    conv, chan, head = prep(table, params, pair_params, conv_wbc, conv_bbc[None])
    ones = expander(heads)
    tri = jnp.asarray(np.tril(np.ones((Q, Q), np.float32)), BF)

    x_far, x_own, x_near, table, conv, chan, head = order((x_far, x_own, x_near, table, conv, chan, head))
    shards = with_other_core((x_own, *x_near, *x_far))
    cot, t_far = order((cotangent, t_far))
    c_near = neighbours(cot, "z")

    wx, tokens, tails, pre, before, act, zs, cum, states = front(
        table, shards, (ext, t_near[1], t_near[0], t_far), conv, head, ones, tri
    )
    pair = lax.ppermute(states, "yh", SWAP)
    act, c_near = order((act, c_near))
    c_far = ring_far(*c_near, "z", 128)
    mixed = within(table, act, zs, cum, chan, ones)
    wz, wout, cot, gate, hg = project(table, shards, (cotangent, c_near[1], c_near[0], *c_far), tokens)
    mixed, sin, sums = through(table, mixed, gate, hg, act, cum, states, pair, chan, ones)
    sums = sums, *ring_sends(sums, sums, sums, "z")
    hidden, gate_low, dy, dstates, gain_sum = gate_back(
        table, hg, mixed, gate, sums, act, cum, chan, ones, 4 * width
    )
    pair_dstates = lax.ppermute(dstates, "yh", SWAP)

    early, early_other, early_dots = early_weights(table, tokens, cot, wz, gate_low, hidden)
    around_z = (z + jnp.array([2, 1, 3, 0], jnp.int32)) % 4
    branch = branch_part(around_z, hidden, wout)
    pair_dstates, early, early_other, branch = order((pair_dstates, early, early_other, branch))
    early_other = lax.ppermute(early_other, "core", SWAP)
    branch_got = ring_sends(*branch[:3], "z")
    early = [
        (up(pick(early, (x + k) % 4, 0)) + up(pick(early_other, (x + k) % 4, 0))).astype(BF).reshape(4 * shard, width)
        for k in (2, 1, 3, 0)
    ]
    dy, early = order((dy, early))
    early_near = lax.ppermute(early[1], "x", RIGHT), lax.ppermute(early[2], "x", LEFT)
    own_live = table[OWN]
    live_rows = jnp.arange(rows, dtype=jnp.int32)[:, None] < own_live

    low, fix, conv_sum, head_sum, skip_sum = backward(
        table, act, pre, before, zs, cum, sin, dy, dstates, pair_dstates, pair,
        conv, head, chan, ones, tri, heads,
    )
    low, branch_got, early_near, early_far = order((low, branch_got, early_near, early[0]))
    early_far = lax.ppermute(early_far, "x", FAR)
    late, late_other, small = late_weights(
        table, tokens, tails, wx, low, fix, early_dots, conv_sum, gain_sum, head_sum, skip_sum
    )
    low, around_z, late_other, small, early_far = order((low, around_z, late_other, small, early_far))
    late_other, small_other = lax.ppermute(late_other, "core", SWAP), lax.ppermute(small, "core", SWAP)
    far = normed_part(around_z[:1], gate_low, low, fix, wz, wx)[0]
    far, late_other, small_other = order((far, late_other, small_other))
    *sends, late, parts = x_pack(table, late, late_other, small, small_other)
    sends, around_z, far = order((sends, around_z, far))
    got = ring_sends(*sends, "x")
    from_far = lax.ppermute(far, "z", FAR)
    around_z, parts = order((around_z, lax.ppermute(parts, "core", SWAP)))
    ahead, behind, own = normed_part(around_z[1:], gate_low, low, fix, wz, wx)
    early = up(early[3]) + up(early_far) + up(early_near[0]) + up(early_near[1])
    got, from_far, ahead, behind, own, early = order((got, from_far, ahead, behind, own, early))
    one, two, three, stay, small = y_pack(table, late, got, parts, early)
    got = y_sends(lambda step: {1: one, 2: two, 3: three}[step])
    from_ahead, from_behind = lax.ppermute(ahead, "z", RIGHT), lax.ppermute(behind, "z", LEFT)
    from_ahead, from_behind, got = order((from_ahead, from_behind, got))
    branch = up(branch[3]) + sum(up(v) for v in branch_got)
    output = (resid + jnp.where(live_rows, branch, 0.0)).astype(BF)
    normed_grad = up(own) + up(from_far) + up(from_ahead) + up(from_behind)
    before_it = [(t, (t + 7) % 8) for t in range(8)]
    last = lax.ppermute(normed_grad[rows:], ("z", "yh"), before_it)
    normed_grad = jnp.concatenate([normed_grad[: rows - 16], normed_grad[rows - 16 : rows] + last])

    got, output = order((got, output))
    w_x_grad, w_dt_grad, w_z_grad, w_out_grad, shared, taps, offset, gnorm_grad, skip_grad, bias_grad, rate_grad = z_pack(
        table, stay, got, small
    )
    far, back, on = ring_sends(shared, shared, shared, "z")
    normed_grad, _ = order((normed_grad, shared))
    projected = jnp.sum(normed_grad * in_gain * resid, axis=-1, keepdims=True) / d
    x_grad = inverse * in_gain * normed_grad - resid * inverse**3 * projected + up(cotangent)
    far, back, on, x_grad = order((far, back, on, x_grad))
    w_bc_grad, taps_bc, offset_bc, in_gain_grad = finish(table, shared, on, far, back, in_gain[None])
    return (
        output,
        x_grad,
        in_gain_grad.reshape(-1),
        w_z_grad,
        w_x_grad,
        w_dt_grad,
        w_bc_grad,
        taps,
        offset.reshape(-1),
        taps_bc,
        offset_bc.reshape(-1),
        bias_grad.reshape(-1),
        rate_grad.reshape(-1),
        skip_grad.reshape(-1),
        gnorm_grad.reshape(-1),
        w_out_grad,
    )


def solution(mesh):
    grid = Mesh(mesh.devices.reshape(2, 4, 2, 4, 2), DP + ("z", "yh"))
    tensor = ("z", "yh")
    tokens, weight, channels = P(DP + tensor, None), P(DP, tensor), P(tensor)
    return jax.shard_map(
        local,
        mesh=grid,
        in_specs=(
            tokens,
            tokens,
            P(DP, None),
            P(),
            weight,
            weight,
            weight,
            P(DP, None),
            P(None, tensor),
            channels,
            P(),
            P(),
            channels,
            channels,
            channels,
            channels,
            weight,
        ),
        out_specs=(
            tokens,
            tokens,
            P(DP + tensor),
            weight,
            weight,
            weight,
            P(DP, None),
            P(None, tensor),
            channels,
            P(),
            P(),
            channels,
            channels,
            channels,
            channels,
            weight,
        ),
        check_vma=False,
    )
```

```python
import functools

import jax
import jax.numpy as jnp
import numpy as np
from jax import lax
from jax.experimental import pallas as pl
from jax.experimental.pallas import tpu as pltpu
from jax.sharding import Mesh
from jax.sharding import PartitionSpec as P

Q = 256
HD = 64
NS = 128
EPS = 1e-05
F32 = jnp.float32
BF = jnp.bfloat16
VMEM_LIMIT = 56 * 1024 * 1024


def mm(a, b):
    return lax.dot_general(a, b, (((1,), (0,)), ((), ())), preferred_element_type=F32)


def mm_nt(a, b):
    return lax.dot_general(a, b, (((1,), (1,)), ((), ())), preferred_element_type=F32)


def mm_tn(a, b):
    return lax.dot_general(a, b, (((0,), (0,)), ((), ())), preferred_element_type=F32)


def split3(v):
    hi = v.astype(BF)
    rest = v - hi.astype(F32)
    mid = rest.astype(BF)
    low = (rest - mid.astype(F32)).astype(BF)
    return hi, mid, low


def split2(v):
    hi = v.astype(BF)
    return hi, (v - hi.astype(F32)).astype(BF)


def lanes(shape):
    return lax.broadcasted_iota(jnp.int32, shape, len(shape) - 1)


def lower_ones():
    rows = lax.broadcasted_iota(jnp.int32, (Q, Q), 0)
    return rows >= lanes((Q, Q))


def expander(heads):
    row = np.arange(128)[:, None]
    head = np.arange(heads * HD)[None, :] // HD
    return jnp.asarray(((row == head) | (row == head + LOW)).astype(np.float32), BF)


LOW = 16


def spread(v, ones):
    hi, low = split2(v)
    return mm(jnp.where(lanes(v.shape) < LOW, hi.astype(F32), low.astype(F32)).astype(BF), ones)


def gather_heads(v, ones):
    hi, low = split2(v)
    return mm_nt(hi, ones) + mm_nt(low, ones)


def softplus(z):
    return jnp.maximum(z, 0.0) + jnp.log1p(jnp.exp(-jnp.abs(z)))


def sigmoid(v):
    return 1.0 / (1.0 + jnp.exp(-v))


def running_sum(tri, v):
    hi, mid, low = split3(v)
    return mm(tri, hi) + mm(tri, mid) + mm(tri, low)


def suffix_sum(tri, v):
    hi, mid, low = split3(v)
    return mm_tn(tri, hi) + mm_tn(tri, mid) + mm_tn(tri, low)


KEEP = 0
SIDE = 9
LIVE = 10
PREV = 14
HALF = 18
ROWS = 34
CORE = 66
ZED, EXE, WYE = 67, 68, 69
GAIN = 70
OWN = 71
STATE_ROWS = NS + 16


CHEAP = pl.CostEstimate(flops=1000, bytes_accessed=1000, transcendentals=0)


def call(kernel, name, grid, table, ins, outs, scratch=()):
    def spec(block, index):
        if block is None:
            return pl.BlockSpec(memory_space=pl.ANY)
        return pl.BlockSpec(block, index)

    return pl.pallas_call(
        kernel,
        grid_spec=pltpu.PrefetchScalarGridSpec(
            num_scalar_prefetch=1,
            grid=(grid,),
            in_specs=[spec(block, index) for _, block, index in ins],
            out_specs=[spec(block, index) for _, _, block, index in outs],
            scratch_shapes=list(scratch),
        ),
        out_shape=[jax.ShapeDtypeStruct(shape, dtype) for shape, dtype, _, _ in outs],
        compiler_params=pltpu.CompilerParams(dimension_semantics=("arbitrary",), vmem_limit_bytes=VMEM_LIMIT),
        cost_estimate=CHEAP,
        name=name,
    )(table, *[array for array, _, _ in ins])


def rows_of(array, size=Q):
    return array, (size, array.shape[1]), lambda k, table: (k, 0)


def all_of(array):
    return array, array.shape, lambda k, table: (0,) * array.ndim


def out_rows(count, width, dtype, size=Q):
    return (count * size, width), dtype, (size, width), lambda k, table: (k, 0)


def out_all(shape, dtype):
    return shape, dtype, shape, lambda k, table: (0,) * len(shape)


def decays(cum, ones):
    grow = spread(jnp.exp(cum), ones)
    fade = spread(jnp.exp(cum[Q - 1 :, :] - cum), ones)
    return grow, fade


def conv_run(conv_ref, buf):
    run = conv_ref[4:5, :] + conv_ref[3:4, :] * buf[8 : 8 + Q, :]
    for j in range(1, 4):
        run = run + conv_ref[3 - j : 4 - j, :] * buf[8 - j : 8 - j + Q, :]
    return run


def table_kernel(place, lengths_ref, out_ref):
    yl, x, core, z, yh, shard = (place[i] for i in range(6))
    starts, start = [], 0
    for i in range(lengths_ref.shape[1]):
        length = lengths_ref[0, i]
        span = lax.div(length + (Q - 1), Q) * Q
        starts.append((start, length, span))
        start = start + span

    def stretch(c):
        at = c * Q
        going, living = 0, 0
        for start, length, span in starts:
            inside = (at >= start) & (at < start + span)
            going = going + jnp.where(inside & (at > start), 1, 0)
            living = living + jnp.where(inside, jnp.clip(start + length - at, 0, Q), 0)
        return going, living

    for c in range(9):
        out_ref[KEEP + c] = stretch(c)[0]
    out_ref[SIDE] = yh
    for k in range(4):
        out_ref[LIVE + k] = stretch(2 * k + yh)[1]
        out_ref[PREV + k] = lax.rem(k + 3 + yh, 4)
    hops = (0, 3, 1, 2)
    for i in range(16):
        shard_y = lax.rem(yh * 2 + yl + hops[i % 4], 4)
        shard_x = lax.rem(x + hops[i // 4], 4)
        row = (lax.rem(shard_y, 2) * 4 + shard_x) * 2
        out_ref[HALF + i] = lax.div(shard_y, 2)
        out_ref[ROWS + i] = (row + core) * shard
        out_ref[ROWS + 16 + i] = (row + 1 - core) * shard
    for at, value in ((CORE, core), (ZED, z), (EXE, x), (WYE, yh * 2 + yl), (GAIN, ((yl * 4 + x) * 2 + core) * 8 + 2 * z + yh)):
        out_ref[at] = value
    out_ref[OWN] = stretch(2 * z + yh)[1]


def make_table(place, lengths):
    return pl.pallas_call(
        table_kernel,
        grid_spec=pltpu.PrefetchScalarGridSpec(
            num_scalar_prefetch=1,
            grid=(1,),
            in_specs=[pl.BlockSpec(memory_space=pltpu.SMEM)],
            out_specs=pl.BlockSpec(memory_space=pltpu.SMEM),
        ),
        out_shape=jax.ShapeDtypeStruct((OWN + 1,), jnp.int32),
        cost_estimate=CHEAP,
        name="table",
    )(place, lengths)


def pack_kernel(table, x_ref, bc_ref, dt_ref, z_ref, w_ref, out_ref):
    half = x_ref.shape[1]
    heads = dt_ref.shape[1]
    row = lax.broadcasted_iota(jnp.int32, (heads, 128), 0) + heads * table[0]
    lane = lanes((heads, 128))
    out_ref[:, :half] = x_ref[...]
    out_ref[:, half : half + NS] = jnp.where(table[0] == 0, up(bc_ref[:, :NS]), up(bc_ref[:, NS:])).astype(BF)
    place = ((lane == row) | (lane == row + LOW)).astype(F32).astype(BF)
    out_ref[:, half + NS : BLOCK] = mm(dt_ref[...], place).astype(BF)
    out_ref[:, BLOCK : BLOCK + half] = z_ref[...]
    out_ref[:, BLOCK + half :] = w_ref[...]


def pack(side, w_x, w_bc, w_dt, w_z, w_out):
    shape = (w_x.shape[0], 3 * w_x.shape[1] + NS + 128)
    return call(
        pack_kernel, "pack_shard", 1, side,
        [all_of(w_x), all_of(w_bc), all_of(w_dt), all_of(w_z), all_of(w_out)], [out_all(shape, BF)],
    )[0]


def prep_kernel(table, own_ref, pair_ref, wbc_ref, bbc_ref, conv_ref, chan_ref, head_ref):
    half = own_ref.shape[1]
    width = 2 * half
    own, pair = own_ref[...], pair_ref[...]
    first = table[SIDE] == 0
    for i in range(2):
        both = jnp.where(first, own, pair) if i == 0 else jnp.where(first, pair, own)
        span = slice(half * i, half * (i + 1))
        conv_ref[:, span] = both
        chan_ref[0:1, span] = both[5:6, :]
        chan_ref[1:2, span] = both[6:7, :]
    sub = lax.broadcasted_iota(jnp.int32, (8, 2 * NS), 0)
    rows = jnp.where(sub == 4, bbc_ref[...], 0.0)
    for j in range(4):
        rows = jnp.where(sub == j, wbc_ref[j : j + 1, :], rows)
    conv_ref[:, width:] = rows
    for i in range(2):
        at = slice(128 * i, 128 * (i + 1))
        head_ref[i : i + 1, :] = own[7:8, at] + pair[7:8, at]


def prep(table, own, pair, conv_wbc, conv_bbc):
    half = own.shape[1]
    out = lambda w: out_all((8, w), F32)
    return call(
        prep_kernel, "prep", 1, table,
        [all_of(own), all_of(pair), all_of(conv_wbc), all_of(conv_bbc)],
        [out(2 * half + 2 * NS), out(2 * half), out(128)],
    )


def shard_copies(table, shards, place, cols, sems):
    part = shards[0].shape[1]
    n = len(shards) // 2
    copies = []
    for c in range(2):
        refs = [(ref, i) for ref in shards[n * c : n * c + n] for i in range(ref.shape[0])]
        for i, (ref, at) in enumerate(refs):
            to = place(table[HALF + i], pl.ds(pl.multiple_of(table[ROWS + 16 * c + i], part), part))
            copies.append(
                pltpu.make_async_copy(ref.at[at, :, pl.ds(cols.start, cols.stop - cols.start)], to, sems.at[16 * c + i])
            )
    return copies


def piece_copies(table, pieces, to_ref, sems):
    copies, at = [], 0
    for i, piece in enumerate(pieces):
        hop = (0, 1, 3, 2)[min(i, 3)]
        at = at + pieces[i - 1].shape[0] if i > 3 else 0
        to = to_ref.at[lax.rem(table[ZED] + hop, 4), pl.ds(at, piece.shape[0])]
        copies.append(pltpu.make_async_copy(piece, to, sems.at[i]))
    return copies


def front_kernel(
    table, *refs,
):
    shards, pieces, refs = refs[:10], refs[10:14], refs[14:]
    conv_ref, head_ref, ones_ref, tri_ref, w_ref, tok_ref, tail_ref, pre_ref, before_ref, slope_ref, act_ref, *refs = refs
    z_ref, cum_ref, state_ref, around, ext, buf, sems, piece_sems = refs
    k = pl.program_id(0)
    width = ones_ref.shape[1]
    half = width // 2

    @pl.when(k == 0)
    def _():
        place = lambda side, rows: w_ref.at[rows, pl.ds(pl.multiple_of(side * BLOCK, 128), BLOCK)]
        copies = shard_copies(table, shards, place, slice(0, BLOCK), sems)
        copies += piece_copies(table, pieces, around, piece_sems)
        for copy in copies:
            copy.start()
        for copy in copies:
            copy.wait()

    keep = table[KEEP + 2 * k + table[SIDE]].astype(F32)
    tok_ref[...] = around[k, 0:Q, :]
    ext[0:16, :] = around[table[PREV + k], Q:, :]
    tail_ref[...] = ext[0:16, :]
    ext[16:, :] = around[k, 0:Q, :]
    tok = ext[...]
    dt = jnp.zeros((Q, 128), F32)
    for i in range(2):
        proj = mm(tok, w_ref[:, BLOCK * i : BLOCK * (i + 1)])
        for to, size, at in ((half * i, half, 0), (width + NS * i, NS, half)):
            buf[0:8, to : to + size] = proj[8:16, at : at + size] * keep
            buf[8:, to : to + size] = proj[16:, at : at + size]
        dt = dt + proj[16:, half + NS :]
    pre_ref[...] = buf[8:, :].astype(BF)
    before_ref[...] = buf[0:8, :]
    run = conv_run(conv_ref, buf)
    sg = sigmoid(run)
    act = (run * sg).astype(BF)
    slope_ref[...] = (sg * (1.0 + run * (1.0 - sg))).astype(BF)
    act_ref[...] = act
    z = dt + head_ref[0:1, :]
    z_ref[...] = z
    step = softplus(z)
    cum = running_sum(tri_ref[...], step * head_ref[1:2, :])
    cum_ref[...] = cum
    ones = ones_ref[...]
    weigh = spread(step * jnp.exp(cum[Q - 1 :, :] - cum), ones)
    grown = (act[:, :width].astype(F32) * weigh).astype(BF)
    state_ref[0:NS, :] = mm_tn(act[:, width : width + NS], grown).astype(BF)
    last = spread(jnp.broadcast_to(jnp.exp(cum[Q - 1 :, :]), (16, 128)), ones)
    hi, low = split2(last)
    sub = lax.broadcasted_iota(jnp.int32, last.shape, 0)
    state_ref[NS:, :] = jnp.where(sub == 0, hi.astype(F32), low.astype(F32)).astype(BF)


BLOCK = 640


def front(table, shards, pieces, conv, head, ones, tri):
    rows, d = pieces[0].shape
    width = ones.shape[1]
    cols = width + 2 * NS
    return call(
        front_kernel, "conv_and_states", 4, table,
        [
            *[(a, None, None) for a in (*shards, *pieces)],
            all_of(conv), all_of(head), all_of(ones), all_of(tri),
        ],
        [
            out_all((d, 2 * BLOCK), BF), out_rows(4, d, BF), out_rows(4, d, BF, 16),
            out_rows(4, cols, BF), out_rows(4, cols, F32, 8), out_rows(4, cols, BF), out_rows(4, cols, BF),
            out_rows(4, 128, F32), out_rows(4, 128, F32), out_rows(4, width, BF, STATE_ROWS),
        ],
        [
            pltpu.VMEM((4, rows, d), BF), pltpu.VMEM((rows, d), BF), pltpu.VMEM((8 + Q, cols), F32),
            pltpu.SemaphoreType.DMA((32,)), pltpu.SemaphoreType.DMA((4,)),
        ],
    )


def within_kernel(table, act_ref, z_ref, cum_ref, chan_ref, ones_ref, mixed_ref):
    width = ones_ref.shape[1]
    act = act_ref[...]
    cum = cum_ref[...]
    x = act[:, :width].astype(F32)
    xs = x * spread(softplus(z_ref[...]), ones_ref[...])
    scores = mm_nt(act[:, width + NS :], act[:, width : width + NS])
    cum_row = cum.T
    lower = lower_ones()
    half = lanes((Q, 128)) < HD
    for p in range(width // 128):
        span = slice(128 * p, 128 * (p + 1))
        xp = xs[:, span]
        total = chan_ref[0:1, span] * x[:, span]
        for i in range(2):
            h = 2 * p + i
            diff = cum[:, h : h + 1] - cum_row[h : h + 1, :]
            mix = (scores * jnp.exp(jnp.where(lower, diff, -1e30))).astype(BF)
            total = total + mm(mix, jnp.where(half if i == 0 else ~half, xp, 0.0).astype(BF))
        mixed_ref[:, span] = total


def project_kernel(table, *refs):
    shards, pieces, refs = refs[:10], refs[10:15], refs[15:]
    tok_ref, wz_ref, wout_ref, cot_ref, gate_ref, hg_ref, around, sems, sems2, piece_sems = refs
    k = pl.program_id(0)
    width = gate_ref.shape[1]
    half = width // 2

    def copies(to_ref, at, sems):
        place = lambda side, rows: to_ref.at[rows, pl.ds(pl.multiple_of(side * half, 128), half)]
        return shard_copies(table, shards, place, slice(at, at + half), sems)

    @pl.when(k == 0)
    def _():
        all_copies = copies(wz_ref, BLOCK, sems) + copies(wout_ref, BLOCK + half, sems2)
        all_copies += piece_copies(table, pieces, around, piece_sems)
        for copy in all_copies:
            copy.start()
        for copy in all_copies:
            copy.wait()

    gate_ref[...] = mm(tok_ref[...], wz_ref[...]).astype(BF)
    cot = around[k]
    cot_ref[...] = cot
    live = lax.broadcasted_iota(jnp.int32, (Q, width), 0) < table[LIVE + k]
    hg_ref[...] = jnp.where(live, mm(cot, wout_ref[...]), 0.0).astype(BF)


def project(table, shards, pieces, tokens):
    rows, d = pieces[0].shape
    width = shards[0].shape[2] - BLOCK
    return call(
        project_kernel, "project", 4, table,
        [*[(a, None, None) for a in (*shards, *pieces)], rows_of(tokens)],
        [
            out_all((d, width), BF), out_all((d, width), BF), out_rows(4, d, BF),
            out_rows(4, width, BF), out_rows(4, width, BF),
        ],
        [
            pltpu.VMEM((4, rows, d), BF), pltpu.SemaphoreType.DMA((32,)), pltpu.SemaphoreType.DMA((32,)),
            pltpu.SemaphoreType.DMA((5,)),
        ],
    )


def within(table, act, z, cum, chan, ones):
    return call(
        within_kernel, "ssd_within", 4, table,
        [rows_of(act), rows_of(z), rows_of(cum), all_of(chan), all_of(ones)],
        [out_rows(4, ones.shape[1], F32)],
    )[0]


def decay_of(state_ref):
    rows = state_ref[NS : NS + 8, :].astype(F32)
    return rows[0:1, :] + rows[1:2, :]


def through_kernel(
    table, within_ref, gate_ref, hg_ref, act_ref, cum_ref, own_ref, pair_ref, chan_ref, ones_ref,
    mixed_ref, sin_ref, sums_ref,
    state,
):
    k = pl.program_id(0)
    width = ones_ref.shape[1]
    first = table[SIDE] == 0

    @pl.when(k == 0)
    def _():
        state[...] = jnp.zeros_like(state)

    own, pair = own_ref[0:NS, :].astype(F32), pair_ref[0:NS, :].astype(F32)
    own_decay, pair_decay = decay_of(own_ref), decay_of(pair_ref)
    at_a = table[KEEP + 2 * k].astype(F32) * state[...]
    after_a = jnp.where(first, own_decay, pair_decay) * at_a + jnp.where(first, own, pair)
    at_b = table[KEEP + 2 * k + 1].astype(F32) * after_a
    state[...] = jnp.where(first, pair_decay, own_decay) * at_b + jnp.where(first, pair, own)
    carried = jnp.where(first, at_a, at_b).astype(BF)
    sin_ref[...] = carried

    grow = spread(jnp.exp(cum_ref[...]), ones_ref[...])
    mixed = within_ref[...] + mm(act_ref[...], carried) * grow
    mixed_ref[...] = mixed.astype(BF)
    gate = up(gate_ref[...])
    gated = mixed * (gate * sigmoid(gate))
    one = jnp.ones((8, width), BF)
    square = sum(mm_nt(one, part) for part in split2(gated * gated))
    inner = sum(mm_nt(one, part) for part in split2(up(hg_ref[...]) * chan_ref[1:2, :] * gated))
    sub = lax.broadcasted_iota(jnp.int32, (8, Q), 0)
    sums_ref[...] = jnp.where(sub == 0, square, inner)


def c_rows(act):
    return act, (Q, NS), lambda k, table: (k, act.shape[1] // NS - 1)


def through(table, mixed, gate, hg, act, cum, own, pair, chan, ones):
    width = ones.shape[1]
    return call(
        through_kernel, "ssd_through", 4, table,
        [
            rows_of(mixed), rows_of(gate), rows_of(hg), c_rows(act), rows_of(cum),
            rows_of(own, STATE_ROWS), rows_of(pair, STATE_ROWS), all_of(chan), all_of(ones),
        ],
        [
            out_rows(4, width, BF), out_rows(4, width, BF, NS),
            ((8, 4 * Q), F32, (8, Q), lambda k, table: (0, k)),
        ],
        [pltpu.VMEM((NS, width), F32)],
    )


def gate_back_kernel(
    table, hg_ref, mixed_ref, gate_ref, sums_ref, sums1, sums2, sums3, act_ref, cum_ref, chan_ref, ones_ref,
    hidden_ref, glow_ref, dy_ref, dstate_ref, ngg_ref, *, inner,
):
    k = pl.program_id(0)
    width = ones_ref.shape[1]

    @pl.when(k == 0)
    def _():
        ngg_ref[...] = jnp.zeros_like(ngg_ref)

    sums = (sums_ref[...] + sums1[...]) + (sums2[...] + sums3[...])
    scale_row = lax.rsqrt(sums[0:1, :] / inner + EPS)
    pull_row = scale_row * scale_row * scale_row * (sums[1:2, :] / inner)
    sub = lax.broadcasted_iota(jnp.int32, (128, Q), 0)
    cols = jnp.where(sub == 0, scale_row, jnp.where(sub == 1, pull_row, 0.0)).T
    scale = cols[:, 0:1]
    pull = cols[:, 1:2]
    hg = up(hg_ref[...])
    mixed = up(mixed_ref[...])
    gate = up(gate_ref[...])
    sg = sigmoid(gate)
    silu = gate * sg
    gated = mixed * silu
    normal = gated * scale
    gain = chan_ref[1:2, :]
    row = lax.broadcasted_iota(jnp.int32, (Q, width), 0)
    hidden_ref[...] = jnp.where(row < table[LIVE + k], normal * gain, 0.0).astype(BF)
    ngg_ref[0:1, :] += jnp.sum(hg * normal, axis=0, keepdims=True)
    gg = scale * gain * hg - gated * pull
    dy = gg * silu
    dy_ref[...] = dy
    glow_ref[...] = (gg * mixed * sg * (1.0 + gate * (1.0 - sg))).astype(BF)
    grow = spread(jnp.exp(cum_ref[...]), ones_ref[...])
    dstate_ref[...] = mm_tn(act_ref[...], (dy * grow).astype(BF)).astype(BF)


def gate_back(table, hg, mixed, gate, sums, act, cum, chan, ones, inner):
    width = ones.shape[1]
    return call(
        functools.partial(gate_back_kernel, inner=inner), "gate_back", 4, table,
        [
            rows_of(hg), rows_of(mixed), rows_of(gate), *[(a, (8, Q), lambda k, table: (0, k)) for a in sums],
            c_rows(act), rows_of(cum), all_of(chan), all_of(ones),
        ],
        [
            out_rows(4, width, BF), out_rows(4, width, BF), out_rows(4, width, F32), out_rows(4, width, BF, NS),
            out_all((8, width), F32),
        ],
    )


def backward_kernel(
    table, act_ref, pre_ref, before_ref, slope_ref, z_ref, cum_ref, sin_ref, dy_ref, mine_ref, theirs_ref, decay_ref,
    conv_ref, head_ref, chan_ref, ones_ref, tri_ref,
    low_ref, fix_ref, convsum_ref, headsum_ref, skipsum_ref,
    carry, buf, *, heads,
):
    k = 3 - pl.program_id(0)
    width = heads * HD
    cols = width + 2 * NS
    side = table[SIDE]

    @pl.when(pl.program_id(0) == 0)
    def _():
        carry[...] = jnp.zeros_like(carry)
        convsum_ref[...] = jnp.zeros_like(convsum_ref)
        headsum_ref[...] = jnp.zeros_like(headsum_ref)
        skipsum_ref[...] = jnp.zeros_like(skipsum_ref)

    act = act_ref[...]
    x = act[:, :width].astype(F32)
    bmat = act[:, width : width + NS]
    cmat = act[:, width + NS :]
    z = z_ref[...]
    step = softplus(z)
    cum = cum_ref[...]
    ones = ones_ref[...]
    tri = tri_ref[...]
    step_x = spread(step, ones)
    grow_x, fade_x = decays(cum, ones)
    last_x = grow_x[Q - 1 :, :]
    xs = x * step_x
    xsb = xs.astype(BF)
    dy = dy_ref[...]

    mine = mine_ref[...].astype(F32)
    theirs = theirs_ref[...].astype(F32)
    pair_decay = decay_of(decay_ref)
    keep_a = table[KEEP + 2 * k].astype(F32)
    keep_b = table[KEEP + 2 * k + 1].astype(F32)
    after_b = carry[...]
    first = side == 0
    after_a = keep_b * (jnp.where(first, pair_decay, last_x) * after_b + jnp.where(first, theirs, mine))
    carry[...] = keep_a * (jnp.where(first, last_x, pair_decay) * after_a + jnp.where(first, mine, theirs))
    dstate = jnp.where(first, after_a, after_b)
    dstate_low = dstate.astype(BF)

    scores = mm_nt(bmat, cmat)
    cum_row = cum.T
    lane = lanes((Q, 128))
    even = lane < HD
    sub = lax.broadcasted_iota(jnp.int32, (128, Q), 0)
    later_ones = lanes((Q, Q)) >= lax.broadcasted_iota(jnp.int32, (Q, Q), 0)
    dscores = jnp.zeros((Q, Q), F32)
    rowsum = jnp.zeros((128, Q), F32)
    colsum = jnp.zeros((Q, 128), F32)
    parts = []
    for p in range(heads // 2):
        span = slice(128 * p, 128 * (p + 1))
        dyp = dy[:, span]
        part = jnp.zeros((Q, 128), F32)
        for i in range(2):
            h = 2 * p + i
            diff = cum_row[h : h + 1, :] - cum[:, h : h + 1]
            decay = jnp.exp(jnp.where(later_ones, diff, -1e30))
            mix = (scores * decay).astype(BF)
            dym = jnp.where(even if i == 0 else ~even, dyp, 0.0).astype(BF)
            grad = mm_nt(xsb[:, span], dym) * decay
            dscores = dscores + grad
            grad = grad * scores
            colsum = jnp.where(lane == h, jnp.sum(grad, axis=1, keepdims=True), colsum)
            rowsum = jnp.where(sub == h, jnp.sum(grad, axis=0, keepdims=True), rowsum)
            part = part + mm(mix, dym)
        parts.append(part)
    inside = jnp.concatenate(parts, axis=1)
    carried = sin_ref[...]
    dyg = (dy * grow_x).astype(BF)
    dsl = dscores.astype(BF)
    dc = mm_tn(dsl, bmat) + mm_nt(dyg, carried)
    db = mm(dsl, cmat) + mm_nt((xs * fade_x).astype(BF), dstate_low)
    passed = mm(cmat, carried) * grow_x
    later = mm(bmat, dstate_low) * fade_x
    q_passed = gather_heads(dy * passed, ones)
    q_later = gather_heads(x * later, ones)
    q_inside = gather_heads(x * inside, ones)
    hold = jnp.sum(dstate * carried.astype(F32), axis=0, keepdims=True) * last_x
    q_hold = gather_heads(jnp.broadcast_to(hold, (8, width)), ones)[0:1, :]
    dx = step_x * (inside + later) + chan_ref[0:1, :] * dy
    net = jnp.where(lane < LOW, q_passed + rowsum.T - colsum, 0.0)
    push = step * q_later
    drate = suffix_sum(tri, net) + running_sum(tri, push) - push + q_hold
    rate_of = head_ref[1:2, :]
    dstep = q_inside + q_later + drate * rate_of
    dz = jnp.where(lane < heads, dstep * sigmoid(z), 0.0)
    headsum_ref[0:1, :] += jnp.sum(dz, axis=0, keepdims=True)
    headsum_ref[1:2, :] += jnp.sum(drate * step * rate_of, axis=0, keepdims=True)
    skipsum_ref[0:1, :] += jnp.sum(dy * x, axis=0, keepdims=True)

    grad = jnp.concatenate([dx, db, dc], axis=1)
    dact = grad * up(slope_ref[...])
    pre = up(pre_ref[...])
    start = dact[0:8, :]
    ahead = before_ref[...]
    sub = lax.broadcasted_iota(jnp.int32, start.shape, 0)
    convsum_ref[4:5, :] += jnp.sum(dact, axis=0, keepdims=True)
    convsum_ref[3:4, :] += jnp.sum(dact * pre, axis=0, keepdims=True)
    buf[0:Q, :] = dact
    buf[Q : Q + 8, :] = jnp.zeros((8, cols), F32)
    dpre = conv_ref[3:4, :] * dact
    for j in range(1, 4):
        moved = buf[j : j + Q, :]
        dpre = dpre + conv_ref[3 - j : 4 - j, :] * moved
        first_rows = jnp.where(sub >= 8 - j, pltpu.roll(start, 8 - j, 0) * ahead, 0.0)
        convsum_ref[3 - j : 4 - j, :] += jnp.sum(moved * pre, axis=0, keepdims=True) + jnp.sum(
            first_rows, axis=0, keepdims=True
        )
    half = width // 2
    for i in range(2):
        at = BLOCK * i
        low_ref[:, at : at + half] = dpre[:, half * i : half * (i + 1)].astype(BF)
        low_ref[:, at + half : at + half + NS] = dpre[:, width + NS * i : width + NS * (i + 1)].astype(BF)
        low_ref[:, at + half + NS : at + BLOCK] = dz.astype(BF)
    begin = dact[0:8, :] * table[KEEP + 2 * k + side].astype(F32)
    sub = lax.broadcasted_iota(jnp.int32, begin.shape, 0)
    fix = jnp.zeros_like(begin)
    for j in range(1, 4):
        fix = fix + jnp.where(sub >= 8 - j, conv_ref[3 - j : 4 - j, :] * pltpu.roll(begin, 8 - j, 0), 0.0)
    fix = jnp.concatenate([jnp.zeros_like(fix), fix], axis=0)
    for i in range(2):
        at = BLOCK * i
        fix_ref[:, at : at + half] = fix[:, half * i : half * (i + 1)].astype(BF)
        fix_ref[:, at + half : at + half + NS] = fix[:, width + NS * i : width + NS * (i + 1)].astype(BF)
        fix_ref[:, at + half + NS : at + BLOCK] = jnp.zeros((16, 128), BF)


def backward(table, act, pre, before, slope, z, cum, sin, dy, mine, theirs, pair, conv, head, chan, ones, tri, heads):
    cols = act.shape[1]
    width = heads * HD

    def back(array, size=Q):
        return array, (size, array.shape[1]), lambda i, table: (3 - i, 0)

    def out_back(w, dtype, size=Q):
        return (4 * size, w), dtype, (size, w), lambda i, table: (3 - i, 0)

    return call(
        functools.partial(backward_kernel, heads=heads), "ssd_backward", 4, table,
        [
            back(act), back(pre), back(before, 8), back(slope), back(z), back(cum), back(sin, NS), back(dy),
            back(mine, NS), back(theirs, NS), back(pair, STATE_ROWS),
            all_of(conv), all_of(head), all_of(chan), all_of(ones), all_of(tri),
        ],
        [
            out_back(2 * BLOCK, BF), out_back(2 * BLOCK, BF, 16),
            out_all((8, cols), F32), out_all((8, 128), F32), out_all((8, width), F32),
        ],
        [pltpu.VMEM((NS, width), F32), pltpu.VMEM((8 + Q, cols), F32)],
    )


def by_core(grad, first, i, mine_ref, other_ref, cols):
    part = mine_ref.shape[3]
    for p in range(2):
        a = grad[2 * p * part : (2 * p + 1) * part]
        b = grad[(2 * p + 1) * part : (2 * p + 2) * part]
        mine_ref[p, i, 0, :, cols] = jnp.where(first, a, b).astype(BF)
        other_ref[p, i, 0, :, cols] = jnp.where(first, b, a).astype(BF)


def row_dots(grad, w):
    prod = grad * up(w)
    prod = sum(prod[:, at : at + 128] for at in range(0, prod.shape[1], 128))
    one = jnp.ones((8, 128), BF)
    return sum(mm_nt(one, part) for part in split2(prod))


def early_kernel(table, tok_ref, cot_ref, w_ref, glow_ref, hidden_ref, mine_ref, other_ref, dots_ref):
    half = glow_ref.shape[1] // 2
    first = table[CORE] == 0
    for at, left, right in ((0, tok_ref, glow_ref), (half, cot_ref, hidden_ref)):
        grad = mm_tn(left[...], right[...])
        for i in range(2):
            by_core(grad[:, half * i : half * (i + 1)], first, i, mine_ref, other_ref, slice(at, at + half))
        if at == 0:
            dots_ref[...] = row_dots(grad, w_ref[...])


def late_kernel(
    table, tok_ref, tail_ref, w_ref, low_ref, fix_ref, dots_ref, convsum_ref, gain_ref, headsum_ref, skipsum_ref,
    mine_ref, other_ref, small_ref, dots,
):
    i = pl.program_id(0)
    grad = mm_tn(tok_ref[...], low_ref[...]) + mm_tn(tail_ref[...], fix_ref[...])
    for side in range(2):
        by_core(grad[:, BLOCK * side : BLOCK * (side + 1)], table[CORE] == 0, side, mine_ref, other_ref, slice(0, BLOCK))
    dots[i] = row_dots(grad, w_ref[...])

    @pl.when(i == 3)
    def _():
        width = gain_ref.shape[1]
        cols = convsum_ref.shape[1]
        sub = lax.broadcasted_iota(jnp.int32, (8, width), 0)
        other = jnp.where(sub == 5, gain_ref[0:1, :], jnp.where(sub == 6, skipsum_ref[0:1, :], 0.0))
        small_ref[:, :width] = jnp.where(sub < 5, convsum_ref[:, :width], other)
        sub = lax.broadcasted_iota(jnp.int32, (8, 128), 0)
        for h in range(2):
            at = slice(width + 128 * h, width + 128 * (h + 1))
            other = jnp.where(sub == 5, headsum_ref[h : h + 1, :], 0.0)
            small_ref[:, at] = jnp.where(sub < 5, convsum_ref[:, at], other)
        sub = lax.broadcasted_iota(jnp.int32, (8, 256), 0)
        size = dots.shape[2]
        flat = jnp.concatenate([dots[q] + dots_ref[:, size * q : size * (q + 1)] for q in range(4)], axis=1)
        rows = jnp.zeros((8, 256), F32)
        for r in range(flat.shape[1] // 256):
            rows = jnp.where(sub == r, flat[:, 256 * r : 256 * (r + 1)], rows)
        small_ref[:, cols:] = rows


def shard_outs(d, cols):
    part = d // 16
    out = ((4, 2, 2, part, cols), BF, (2, 2, 1, part, cols), lambda i, table: (i % 2, 0, i // 2, 0, 0))
    return [out, out]


def early_weights(table, tokens, cot, wz, glow, hidden):
    rows, d = tokens.shape
    width = glow.shape[1]
    columns = lambda a: (a, (rows, d // 4), lambda i, table: (0, i))
    return call(
        early_kernel, "early_weights", 4, table,
        [
            columns(tokens), columns(cot), (wz, (d // 4, width), lambda i, table: (i, 0)),
            all_of(glow), all_of(hidden),
        ],
        [*shard_outs(d, width), ((8, d), F32, (8, d // 4), lambda i, table: (0, i))],
    )


def late_weights(table, tokens, tails, wx, low, fix, dots, conv_sum, gain_sum, head_sum, skip_sum):
    rows, d = tokens.shape
    return call(
        late_kernel, "late_weights", 4, table,
        [
            (tokens, (rows, d // 4), lambda i, table: (0, i)),
            (tails, (tails.shape[0], d // 4), lambda i, table: (0, i)),
            (wx, (d // 4, 2 * BLOCK), lambda i, table: (i, 0)),
            all_of(low), all_of(fix), all_of(dots), all_of(conv_sum), all_of(gain_sum), all_of(head_sum), all_of(skip_sum),
        ],
        [*shard_outs(d, BLOCK), out_all((8, 2 * BLOCK), F32)],
        [pltpu.VMEM((4, 8, d // 4), F32)],
    )


def in_order(values, place):
    def at(i):
        hop = lax.rem(i + 4 - place, 4)
        return jnp.where(hop == 0, values[0], jnp.where(hop == 1, values[1], jnp.where(hop == 2, values[2], values[3])))

    return (at(0) + at(1)) + (at(2) + at(3))


def x_pack_kernel(table, mine_ref, other_ref, small_ref, small2_ref, far_ref, ahead_ref, behind_ref, own_ref, parts_ref):
    part = mine_ref.shape[3]
    total = small_ref[...] + small2_ref[...]
    parts = [jnp.concatenate([p[:, :BLOCK], p[:, BLOCK:]], axis=0) for p in (up(v) for v in split2(total))]
    parts = jnp.concatenate(parts, axis=0).astype(BF)
    parts_ref[...] = parts
    for hop, out in ((2, far_ref), (1, ahead_ref), (3, behind_ref), (0, own_ref)):
        i = lax.rem(table[EXE] + hop, 4)
        for y in range(4):
            v = up(mine_ref[i, y // 2, y % 2]) + up(other_ref[i, y // 2, y % 2])
            out[part * y : part * (y + 1), :] = v.astype(BF)
        if hop:
            out[4 * part :, :] = parts


def x_pack(table, mine, other, small, small2):
    part = mine.shape[3]
    rows = 4 * part
    return call(
        x_pack_kernel, "x_pack", 1, table,
        [all_of(mine), all_of(other), all_of(small), all_of(small2)],
        [
            *[out_all((rows + 32, BLOCK), BF) for _ in range(3)],
            out_all((rows, BLOCK), BF), out_all((32, BLOCK), BF),
        ],
    )


def y_pack_kernel(
    table, own_ref, far_ref, back_ref, on_ref, parts_ref, early,
    one_ref, two_ref, three_ref, stay_ref, small_ref, late,
):
    part = stay_ref.shape[0]
    rows = 4 * part
    late[...] = up(own_ref[...]) + sum(up(v[0:rows, :]) for v in (far_ref, back_ref, on_ref))
    joined = lambda v, at: up(v[at : at + 16, :]) + up(v[at + 16 : at + 32, :])
    small = in_order(
        [joined(parts_ref, 0), joined(on_ref, rows), joined(far_ref, rows), joined(back_ref, rows)], table[EXE]
    )
    hi, low = split2(small)
    small_ref[:, :BLOCK] = hi
    small_ref[:, BLOCK:] = low
    half = BLOCK - NS - 128
    for hop, out in ((2, two_ref), (1, one_ref), (3, three_ref), (0, stay_ref)):
        to = pl.multiple_of(lax.rem(table[WYE] + hop, 4) * part, part)
        pair = pl.multiple_of(lax.rem(table[WYE] + hop + 2, 4) * part, part)
        out[0:part, :BLOCK] = late[pl.ds(to, part), :].astype(out.dtype)
        out[0:part, BLOCK : BLOCK + NS] = late[pl.ds(pair, part), half : half + NS].astype(out.dtype)
        out[0:part, BLOCK + NS :] = early[pl.ds(to, part), :].astype(out.dtype)
        if hop:
            out[part:, :BLOCK] = hi
            out[part:, BLOCK : 2 * BLOCK] = low
            out[part:, 2 * BLOCK :] = jnp.zeros((16, out.shape[1] - 2 * BLOCK), BF)


def y_pack(table, own, got, parts, early):
    rows = own.shape[0]
    part = rows // 4
    wide = BLOCK + NS + early.shape[1]
    return call(
        y_pack_kernel, "y_pack", 1, table,
        [all_of(a) for a in (own, *got, parts, early)],
        [
            *[out_all((part + 16, wide), BF) for _ in range(3)],
            out_all((part, wide), F32), out_all((16, 2 * BLOCK), BF),
        ],
        [pltpu.VMEM((rows, BLOCK), F32)],
    )


def z_pack_kernel(
    table, stay_ref, one_ref, two_ref, three_ref, small_ref,
    x_ref, dt_ref, z_ref, out_ref, share_ref, taps_ref, offset_ref, gain_ref, skip_ref, bias_ref, rate_ref,
):
    part = stay_ref.shape[0]
    half = x_ref.shape[1]
    got = one_ref, two_ref, three_ref
    total = stay_ref[...] + sum(up(v[0:part, :]) for v in got)
    x_ref[...] = total[:, :half]
    heads = dt_ref.shape[1]
    step = total[:, half + NS : BLOCK]
    dt_ref[...] = jnp.where(table[SIDE] == 0, step[:, :heads], step[:, heads : 2 * heads])
    z_ref[...] = total[:, BLOCK + NS : BLOCK + NS + half]
    out_ref[...] = total[:, BLOCK + NS + half :]
    first = table[SIDE] == 0
    own, pair = total[:, half : half + NS], total[:, BLOCK : BLOCK + NS]
    share_ref[0:part, :NS] = jnp.where(first, own, pair)
    share_ref[0:part, NS:] = jnp.where(first, pair, own)
    joined = lambda v: up(v[:, :BLOCK]) + up(v[:, BLOCK : 2 * BLOCK])
    small = in_order([joined(small_ref[...])] + [joined(v[part:, :]) for v in got], table[WYE])
    rest = 2 * half - BLOCK
    width = jnp.concatenate([small[:8], small[8:, :rest]], axis=1)
    chan = jnp.where(first, width[:, :half], width[:, half:])
    taps_ref[...] = chan[0:4]
    offset_ref[...] = chan[4:5]
    gain_ref[...] = chan[5:6]
    heads = bias_ref.shape[1]
    one = jnp.where(lax.broadcasted_iota(jnp.int32, (128, half), 0) == lanes((128, half)) // HD, 1.0, 0.0).astype(BF)
    skip_ref[...] = sum(mm_nt(part, one) for part in split3(chan))[6:7, :heads]
    for ref, at in ((bias_ref, rest), (rate_ref, rest + 128)):
        row = small[13:14, at : at + 128]
        ref[...] = jnp.where(first, row[:, :heads], row[:, heads : 2 * heads])
    share_ref[part : part + 8, :] = small[8:, rest : rest + 256]
    share_ref[part + 8 :, :] = small[8:, rest + 256 :]


def z_pack(table, stay, got, small):
    part = stay.shape[0]
    half = BLOCK - NS - 128
    out = lambda *shape: out_all(shape, F32)
    return call(
        z_pack_kernel, "z_pack", 1, table,
        [all_of(a) for a in (stay, *got, small)],
        [
            out(part, half), out(part, half // HD), out(part, half), out(part, half), out(part + 16, 256),
            out(4, half), out(1, half), out(1, half), out(1, half // HD), out(1, half // HD), out(1, half // HD),
        ],
    )


def finish_kernel(table, own_ref, on_ref, far_ref, back_ref, gain_ref, bc_ref, taps_ref, offset_ref, ingain_ref):
    part = bc_ref.shape[0]
    total = in_order([v[...] for v in (own_ref, on_ref, far_ref, back_ref)], table[ZED])
    bc_ref[...] = total[:part]
    taps_ref[...] = total[part : part + 4]
    offset_ref[...] = total[part + 4 : part + 5]
    d = gain_ref.shape[1]
    each = ingain_ref.shape[1]
    dots = jnp.concatenate([total[part + 8 + r : part + 9 + r] for r in range(d // 256)], axis=1)
    quotient = jnp.broadcast_to(dots / gain_ref[...], (8, d))
    ingain_ref[...] = pltpu.roll(quotient, lax.rem(d - table[GAIN] * each, d), 1)[0:1, :each]


def finish(table, own, on, far, back, gain):
    width = own.shape[1]
    d = gain.shape[1]
    out = lambda *shape: out_all(shape, F32)
    return call(
        finish_kernel, "finish", 1, table, [all_of(a) for a in (own, on, far, back, gain)],
        [out(own.shape[0] - 16, width), out(4, width), out(1, width), out(1, d // 128)],
    )


def put_one(total, out_refs):
    for n, out_ref in enumerate(out_refs):

        @pl.when(pl.program_id(0) == n)
        def _(out_ref=out_ref):
            out_ref[...] = total.astype(BF)


def normed_kernel(order, glow_ref, low_ref, fix_ref, wz_ref, wx_ref, *refs):
    *out_refs, ext = refs
    ext[0:Q, :] = low_ref[...]
    ext[Q:, :] = fix_ref[...]
    total = mm_nt(ext[...], wx_ref[...])
    put_one(jnp.concatenate([total[:Q] + mm_nt(glow_ref[...], wz_ref[...]), total[Q:]], axis=0), out_refs)


def branch_kernel(order, hidden_ref, wout_ref, *out_refs):
    put_one(mm_nt(hidden_ref[...], wout_ref[...]), out_refs)


def picked(a):
    return a, (Q, a.shape[1]), lambda i, order: (order[i], 0)


def normed_part(order, glow, low, fix, wz, wx):
    n = order.shape[0]
    return call(
        normed_kernel, "normed_grad", n, order,
        [picked(glow), picked(low), (fix, (16, fix.shape[1]), lambda i, order: (order[i], 0)), all_of(wz), all_of(wx)],
        [out_all((Q + 16, wx.shape[0]), BF)] * n,
        [pltpu.VMEM((Q + 16, low.shape[1]), BF)],
    )


def branch_part(order, hidden, wout):
    n = order.shape[0]
    return call(
        branch_kernel, "branch", n, order, [picked(hidden), all_of(wout)], [out_all((Q, wout.shape[0]), BF)] * n
    )


DP = ("yl", "x", "core")
RIGHT = [(i, (i + 1) % 4) for i in range(4)]
LEFT = [(i, (i + 3) % 4) for i in range(4)]
NEAR = [(i, i ^ 1) for i in range(4)]
FAR = [(i, i ^ 2) for i in range(4)]
SWAP = [(0, 1), (1, 0)]


def around_y(step):
    place = lambda y: y % 2 * 2 + y // 2
    return [(place(y), place((y + step) % 4)) for y in range(4)]


def pick(array, index, axis):
    return lax.dynamic_index_in_dim(array, index, axis, keepdims=False)


def up(v):
    return v.astype(F32)


def ring_sends(far, ahead, behind, axis):
    return (
        lax.ppermute(far, axis, FAR),
        lax.ppermute(ahead, axis, RIGHT),
        lax.ppermute(behind, axis, LEFT),
    )


def y_sends(shard):
    send = lambda step: lax.ppermute(shard(step), ("yl", "yh"), around_y(step))
    two, one, three = send(2), send(1), send(3)
    return three, two, one


def ring_far(back, on, axis, cut):
    return lax.ppermute(back[:cut], axis, RIGHT), lax.ppermute(on[cut:], axis, LEFT)


def neighbours(v, axis):
    return lax.ppermute(v, axis, RIGHT), lax.ppermute(v, axis, LEFT)


def with_other_core(arrays):
    return (*arrays, *[lax.ppermute(a, "core", SWAP) for a in arrays])


def local(
    x_in,
    cotangent,
    seq_lengths,
    in_gain,
    w_z,
    w_x,
    w_dt,
    w_bc,
    conv_wx,
    conv_bx,
    conv_wbc,
    conv_bbc,
    dt_bias,
    a_log,
    d_skip,
    gnorm_gain,
    w_out,
):
    rows, d = x_in.shape
    own_heads = dt_bias.shape[0]
    heads = 2 * own_heads
    half = own_heads * HD
    width = 2 * half
    cols = width + 2 * NS
    shard = w_z.shape[0]
    yl, x, core, z, yh = (lax.axis_index(a) for a in ("yl", "x", "core", "z", "yh"))
    dp = (yl * 4 + x) * 2 + core
    side = yh == 0

    hops = (0, 3, 1, 2)
    order = lax.optimization_barrier
    x_tail = lax.ppermute(x_in[rows - 16 :], "yh", SWAP)
    own_w, x_tail = order((pack(yh[None], w_x, w_bc, w_dt, w_z, w_out), x_tail))
    resid = x_in.astype(F32)
    inverse = lax.rsqrt(jnp.mean(resid * resid, axis=-1, keepdims=True) + EPS)
    longer = up(jnp.concatenate([x_in, x_tail]))
    longer_inverse = lax.rsqrt(jnp.mean(longer * longer, axis=-1, keepdims=True) + EPS)
    ext = (longer * longer_inverse * in_gain).astype(BF)

    one, two, three = y_sends(lambda step: own_w)
    x_own = jnp.stack([own_w, three, one, two])
    x_near = neighbours(x_own, "x")
    t_near = neighbours(ext, "z")
    x_near, t_near = order((x_near, t_near))
    x_far, t_far = ring_far(*x_near, "x", 2), lax.ppermute(t_near[0], "z", RIGHT)

    seq_lengths, conv_bx, dt_bias, _ = order((seq_lengths, conv_bx, dt_bias, t_near[0]))
    place = jnp.stack([yl, x, core, z, yh, jnp.full((), shard, yh.dtype)]).astype(jnp.int32)
    table = make_table(place, seq_lengths)
    lane_gap = jnp.zeros((LOW - heads,), F32)
    apart = jnp.zeros((own_heads,), F32)

    def by_lane(v):
        v = jnp.where(side, jnp.concatenate([v, apart]), jnp.concatenate([apart, v]))
        return jnp.concatenate([v, lane_gap, v, jnp.zeros((128 - LOW - heads,), F32)])

    params = jnp.stack(
        [conv_wx[0], conv_wx[1], conv_wx[2], conv_wx[3], conv_bx, jnp.repeat(d_skip, HD), gnorm_gain]
        + [jnp.concatenate([by_lane(dt_bias), by_lane(-jnp.exp(a_log)), jnp.zeros((half - 256,), F32)])]
    )
    pair_params = lax.ppermute(params, "yh", SWAP)
    conv, chan, head = prep(table, params, pair_params, conv_wbc, conv_bbc[None])
    ones = expander(heads)
    tri = jnp.asarray(np.tril(np.ones((Q, Q), np.float32)), BF)

    x_far, x_own, x_near, table, conv, chan, head = order((x_far, x_own, x_near, table, conv, chan, head))
    shards = with_other_core((x_own, *x_near, *x_far))
    cot, t_far = order((cotangent, t_far))
    c_near = neighbours(cot, "z")

    wx, tokens, tails, pre, before, slope, act, zs, cum, states = front(
        table, shards, (ext, t_near[1], t_near[0], t_far), conv, head, ones, tri
    )
    pair = lax.ppermute(states, "yh", SWAP)
    act, c_near = order((act, c_near))
    c_far = ring_far(*c_near, "z", 128)
    mixed = within(table, act, zs, cum, chan, ones)
    wz, wout, cot, gate, hg = project(table, shards, (cotangent, c_near[1], c_near[0], *c_far), tokens)
    mixed, sin, sums = through(table, mixed, gate, hg, act, cum, states, pair, chan, ones)
    sums = sums, *ring_sends(sums, sums, sums, "z")
    hidden, gate_low, dy, dstates, gain_sum = gate_back(
        table, hg, mixed, gate, sums, act, cum, chan, ones, 4 * width
    )
    pair_dstates = lax.ppermute(dstates, "yh", SWAP)

    early, early_other, early_dots = early_weights(table, tokens, cot, wz, gate_low, hidden)
    around_z = (z + jnp.array([2, 1, 3, 0], jnp.int32)) % 4
    branch = branch_part(around_z, hidden, wout)
    pair_dstates, early, early_other, branch = order((pair_dstates, early, early_other, branch))
    early_other = lax.ppermute(early_other, "core", SWAP)
    branch_got = ring_sends(*branch[:3], "z")
    early = [
        (up(pick(early, (x + k) % 4, 0)) + up(pick(early_other, (x + k) % 4, 0))).astype(BF).reshape(4 * shard, width)
        for k in (2, 1, 3, 0)
    ]
    dy, early = order((dy, early))
    early_near = lax.ppermute(early[1], "x", RIGHT), lax.ppermute(early[2], "x", LEFT)
    own_live = table[OWN]
    live_rows = jnp.arange(rows, dtype=jnp.int32)[:, None] < own_live

    low, fix, conv_sum, head_sum, skip_sum = backward(
        table, act, pre, before, slope, zs, cum, sin, dy, dstates, pair_dstates, pair,
        conv, head, chan, ones, tri, heads,
    )
    low, branch_got, early_near, early_far = order((low, branch_got, early_near, early[0]))
    early_far = lax.ppermute(early_far, "x", FAR)
    late, late_other, small = late_weights(
        table, tokens, tails, wx, low, fix, early_dots, conv_sum, gain_sum, head_sum, skip_sum
    )
    low, around_z, late_other, small, early_far = order((low, around_z, late_other, small, early_far))
    late_other, small_other = lax.ppermute(late_other, "core", SWAP), lax.ppermute(small, "core", SWAP)
    far = normed_part(around_z[:1], gate_low, low, fix, wz, wx)[0]
    far, late_other, small_other = order((far, late_other, small_other))
    *sends, late, parts = x_pack(table, late, late_other, small, small_other)
    sends, around_z, far = order((sends, around_z, far))
    got = ring_sends(*sends, "x")
    from_far = lax.ppermute(far, "z", FAR)
    around_z, parts = order((around_z, lax.ppermute(parts, "core", SWAP)))
    ahead, behind, own = normed_part(around_z[1:], gate_low, low, fix, wz, wx)
    early = up(early[3]) + up(early_far) + up(early_near[0]) + up(early_near[1])
    got, from_far, ahead, behind, own, early = order((got, from_far, ahead, behind, own, early))
    one, two, three, stay, small = y_pack(table, late, got, parts, early)
    got = y_sends(lambda step: {1: one, 2: two, 3: three}[step])
    from_ahead, from_behind = lax.ppermute(ahead, "z", RIGHT), lax.ppermute(behind, "z", LEFT)
    from_ahead, from_behind, got = order((from_ahead, from_behind, got))
    branch = up(branch[3]) + sum(up(v) for v in branch_got)
    output = (resid + jnp.where(live_rows, branch, 0.0)).astype(BF)
    normed_grad = up(own) + up(from_far) + up(from_ahead) + up(from_behind)
    before_it = [(t, (t + 7) % 8) for t in range(8)]
    last = lax.ppermute(normed_grad[rows:], ("z", "yh"), before_it)
    normed_grad = jnp.concatenate([normed_grad[: rows - 16], normed_grad[rows - 16 : rows] + last])

    got, output = order((got, output))
    w_x_grad, w_dt_grad, w_z_grad, w_out_grad, shared, taps, offset, gnorm_grad, skip_grad, bias_grad, rate_grad = z_pack(
        table, stay, got, small
    )
    far, back, on = ring_sends(shared, shared, shared, "z")
    normed_grad, _ = order((normed_grad, shared))
    projected = jnp.sum(normed_grad * in_gain * resid, axis=-1, keepdims=True) / d
    x_grad = inverse * in_gain * normed_grad - resid * inverse**3 * projected + up(cotangent)
    far, back, on, x_grad = order((far, back, on, x_grad))
    w_bc_grad, taps_bc, offset_bc, in_gain_grad = finish(table, shared, on, far, back, in_gain[None])
    return (
        output,
        x_grad,
        in_gain_grad.reshape(-1),
        w_z_grad,
        w_x_grad,
        w_dt_grad,
        w_bc_grad,
        taps,
        offset.reshape(-1),
        taps_bc,
        offset_bc.reshape(-1),
        bias_grad.reshape(-1),
        rate_grad.reshape(-1),
        skip_grad.reshape(-1),
        gnorm_grad.reshape(-1),
        w_out_grad,
    )


def solution(mesh):
    grid = Mesh(mesh.devices.reshape(2, 4, 2, 4, 2), DP + ("z", "yh"))
    tensor = ("z", "yh")
    tokens, weight, channels = P(DP + tensor, None), P(DP, tensor), P(tensor)
    return jax.shard_map(
        local,
        mesh=grid,
        in_specs=(
            tokens,
            tokens,
            P(DP, None),
            P(),
            weight,
            weight,
            weight,
            P(DP, None),
            P(None, tensor),
            channels,
            P(),
            P(),
            channels,
            channels,
            channels,
            channels,
            weight,
        ),
        out_specs=(
            tokens,
            tokens,
            P(DP + tensor),
            weight,
            weight,
            weight,
            P(DP, None),
            P(None, tensor),
            channels,
            P(),
            P(),
            channels,
            channels,
            channels,
            channels,
            weight,
        ),
        check_vma=False,
    )
```

```python
import functools

import jax
import jax.numpy as jnp
import numpy as np
from jax import lax
from jax.experimental import pallas as pl
from jax.experimental.pallas import tpu as pltpu
from jax.sharding import Mesh
from jax.sharding import PartitionSpec as P

Q = 256
HD = 64
NS = 128
EPS = 1e-05
F32 = jnp.float32
BF = jnp.bfloat16
VMEM_LIMIT = 56 * 1024 * 1024


def mm(a, b):
    return lax.dot_general(a, b, (((1,), (0,)), ((), ())), preferred_element_type=F32)


def mm_nt(a, b):
    return lax.dot_general(a, b, (((1,), (1,)), ((), ())), preferred_element_type=F32)


def mm_tn(a, b):
    return lax.dot_general(a, b, (((0,), (0,)), ((), ())), preferred_element_type=F32)


def split3(v):
    hi = v.astype(BF)
    rest = v - hi.astype(F32)
    mid = rest.astype(BF)
    low = (rest - mid.astype(F32)).astype(BF)
    return hi, mid, low


def split2(v):
    hi = v.astype(BF)
    return hi, (v - hi.astype(F32)).astype(BF)


def lanes(shape):
    return lax.broadcasted_iota(jnp.int32, shape, len(shape) - 1)


def lower_ones():
    rows = lax.broadcasted_iota(jnp.int32, (Q, Q), 0)
    return rows >= lanes((Q, Q))


def expander(heads):
    row = np.arange(128)[:, None]
    head = np.arange(heads * HD)[None, :] // HD
    return jnp.asarray(((row == head) | (row == head + LOW)).astype(np.float32), BF)


LOW = 16


def spread(v, ones):
    hi, low = split2(v)
    return mm(jnp.where(lanes(v.shape) < LOW, hi.astype(F32), low.astype(F32)).astype(BF), ones)


def gather_heads(v, ones):
    hi, low = split2(v)
    return mm_nt(hi, ones) + mm_nt(low, ones)


def softplus(z):
    return jnp.maximum(z, 0.0) + jnp.log1p(jnp.exp(-jnp.abs(z)))


def sigmoid(v):
    return 1.0 / (1.0 + jnp.exp(-v))


def running_sum(tri, v):
    hi, mid, low = split3(v)
    return mm(tri, hi) + mm(tri, mid) + mm(tri, low)


def suffix_sum(tri, v):
    hi, mid, low = split3(v)
    return mm_tn(tri, hi) + mm_tn(tri, mid) + mm_tn(tri, low)


KEEP = 0
SIDE = 9
LIVE = 10
PREV = 14
HALF = 18
ROWS = 34
CORE = 66
ZED, EXE, WYE = 67, 68, 69
GAIN = 70
OWN = 71
STATE_ROWS = NS + 16


CHEAP = pl.CostEstimate(flops=1000, bytes_accessed=1000, transcendentals=0)


def call(kernel, name, grid, table, ins, outs, scratch=()):
    def spec(block, index):
        if block is None:
            return pl.BlockSpec(memory_space=pl.ANY)
        return pl.BlockSpec(block, index)

    return pl.pallas_call(
        kernel,
        grid_spec=pltpu.PrefetchScalarGridSpec(
            num_scalar_prefetch=1,
            grid=(grid,),
            in_specs=[spec(block, index) for _, block, index in ins],
            out_specs=[spec(block, index) for _, _, block, index in outs],
            scratch_shapes=list(scratch),
        ),
        out_shape=[jax.ShapeDtypeStruct(shape, dtype) for shape, dtype, _, _ in outs],
        compiler_params=pltpu.CompilerParams(dimension_semantics=("arbitrary",), vmem_limit_bytes=VMEM_LIMIT),
        cost_estimate=CHEAP,
        name=name,
    )(table, *[array for array, _, _ in ins])


def rows_of(array, size=Q):
    return array, (size, array.shape[1]), lambda k, table: (k, 0)


def all_of(array):
    return array, array.shape, lambda k, table: (0,) * array.ndim


def out_rows(count, width, dtype, size=Q):
    return (count * size, width), dtype, (size, width), lambda k, table: (k, 0)


def out_all(shape, dtype):
    return shape, dtype, shape, lambda k, table: (0,) * len(shape)


def decays(cum, ones):
    grow = spread(jnp.exp(cum), ones)
    fade = spread(jnp.exp(cum[Q - 1 :, :] - cum), ones)
    return grow, fade


def conv_run(conv_ref, buf):
    run = conv_ref[4:5, :] + conv_ref[3:4, :] * buf[8 : 8 + Q, :]
    for j in range(1, 4):
        run = run + conv_ref[3 - j : 4 - j, :] * buf[8 - j : 8 - j + Q, :]
    return run


def table_kernel(place, lengths_ref, out_ref):
    yl, x, core, z, yh, shard = (place[i] for i in range(6))
    starts, start = [], 0
    for i in range(lengths_ref.shape[1]):
        length = lengths_ref[0, i]
        span = lax.div(length + (Q - 1), Q) * Q
        starts.append((start, length, span))
        start = start + span

    def stretch(c):
        at = c * Q
        going, living = 0, 0
        for start, length, span in starts:
            inside = (at >= start) & (at < start + span)
            going = going + jnp.where(inside & (at > start), 1, 0)
            living = living + jnp.where(inside, jnp.clip(start + length - at, 0, Q), 0)
        return going, living

    for c in range(9):
        out_ref[KEEP + c] = stretch(c)[0]
    out_ref[SIDE] = yh
    for k in range(4):
        out_ref[LIVE + k] = stretch(2 * k + yh)[1]
        out_ref[PREV + k] = lax.rem(k + 3 + yh, 4)
    hops = (0, 3, 1, 2)
    for i in range(16):
        shard_y = lax.rem(yh * 2 + yl + hops[i % 4], 4)
        shard_x = lax.rem(x + hops[i // 4], 4)
        row = (lax.rem(shard_y, 2) * 4 + shard_x) * 2
        out_ref[HALF + i] = lax.div(shard_y, 2)
        out_ref[ROWS + i] = (row + core) * shard
        out_ref[ROWS + 16 + i] = (row + 1 - core) * shard
    for at, value in ((CORE, core), (ZED, z), (EXE, x), (WYE, yh * 2 + yl), (GAIN, ((yl * 4 + x) * 2 + core) * 8 + 2 * z + yh)):
        out_ref[at] = value
    out_ref[OWN] = stretch(2 * z + yh)[1]


def make_table(place, lengths):
    return pl.pallas_call(
        table_kernel,
        grid_spec=pltpu.PrefetchScalarGridSpec(
            num_scalar_prefetch=1,
            grid=(1,),
            in_specs=[pl.BlockSpec(memory_space=pltpu.SMEM)],
            out_specs=pl.BlockSpec(memory_space=pltpu.SMEM),
        ),
        out_shape=jax.ShapeDtypeStruct((OWN + 1,), jnp.int32),
        cost_estimate=CHEAP,
        name="table",
    )(place, lengths)


def pack_kernel(table, x_ref, bc_ref, dt_ref, z_ref, w_ref, out_ref):
    half = x_ref.shape[1]
    heads = dt_ref.shape[1]
    row = lax.broadcasted_iota(jnp.int32, (heads, 128), 0) + heads * table[0]
    lane = lanes((heads, 128))
    out_ref[:, :half] = x_ref[...]
    out_ref[:, half : half + NS] = jnp.where(table[0] == 0, up(bc_ref[:, :NS]), up(bc_ref[:, NS:])).astype(BF)
    place = ((lane == row) | (lane == row + LOW)).astype(F32).astype(BF)
    out_ref[:, half + NS : BLOCK] = mm(dt_ref[...], place).astype(BF)
    out_ref[:, BLOCK : BLOCK + half] = z_ref[...]
    out_ref[:, BLOCK + half :] = w_ref[...]


def pack(side, w_x, w_bc, w_dt, w_z, w_out):
    shape = (w_x.shape[0], 3 * w_x.shape[1] + NS + 128)
    return call(
        pack_kernel, "pack_shard", 1, side,
        [all_of(w_x), all_of(w_bc), all_of(w_dt), all_of(w_z), all_of(w_out)], [out_all(shape, BF)],
    )[0]


def prep_kernel(table, own_ref, pair_ref, wbc_ref, bbc_ref, conv_ref, chan_ref, head_ref):
    half = own_ref.shape[1]
    width = 2 * half
    own, pair = own_ref[...], pair_ref[...]
    first = table[SIDE] == 0
    for i in range(2):
        both = jnp.where(first, own, pair) if i == 0 else jnp.where(first, pair, own)
        span = slice(half * i, half * (i + 1))
        conv_ref[:, span] = both
        chan_ref[0:1, span] = both[5:6, :]
        chan_ref[1:2, span] = both[6:7, :]
    sub = lax.broadcasted_iota(jnp.int32, (8, 2 * NS), 0)
    rows = jnp.where(sub == 4, bbc_ref[...], 0.0)
    for j in range(4):
        rows = jnp.where(sub == j, wbc_ref[j : j + 1, :], rows)
    conv_ref[:, width:] = rows
    for i in range(2):
        at = slice(128 * i, 128 * (i + 1))
        head_ref[i : i + 1, :] = own[7:8, at] + pair[7:8, at]


def prep(table, own, pair, conv_wbc, conv_bbc):
    half = own.shape[1]
    out = lambda w: out_all((8, w), F32)
    return call(
        prep_kernel, "prep", 1, table,
        [all_of(own), all_of(pair), all_of(conv_wbc), all_of(conv_bbc)],
        [out(2 * half + 2 * NS), out(2 * half), out(128)],
    )


def shard_copies(table, shards, place, cols, sems):
    part = shards[0].shape[1]
    n = len(shards) // 2
    copies = []
    for c in range(2):
        refs = [(ref, i) for ref in shards[n * c : n * c + n] for i in range(ref.shape[0])]
        for i, (ref, at) in enumerate(refs):
            to = place(table[HALF + i], pl.ds(pl.multiple_of(table[ROWS + 16 * c + i], part), part))
            copies.append(
                pltpu.make_async_copy(ref.at[at, :, pl.ds(cols.start, cols.stop - cols.start)], to, sems.at[16 * c + i])
            )
    return copies


def piece_copies(table, pieces, to_ref, sems):
    copies, at = [], 0
    for i, piece in enumerate(pieces):
        hop = (0, 1, 3, 2)[min(i, 3)]
        at = at + pieces[i - 1].shape[0] if i > 3 else 0
        to = to_ref.at[lax.rem(table[ZED] + hop, 4), pl.ds(at, piece.shape[0])]
        copies.append(pltpu.make_async_copy(piece, to, sems.at[i]))
    return copies


def front_kernel(
    table, *refs,
):
    shards, pieces, refs = refs[:10], refs[10:14], refs[14:]
    conv_ref, head_ref, ones_ref, tri_ref, w_ref, tok_ref, tail_ref, pre_ref, before_ref, slope_ref, act_ref, *refs = refs
    z_ref, cum_ref, state_ref, around, ext, buf, sems, piece_sems = refs
    k = pl.program_id(0)
    width = ones_ref.shape[1]
    half = width // 2

    @pl.when(k == 0)
    def _():
        place = lambda side, rows: w_ref.at[rows, pl.ds(pl.multiple_of(side * BLOCK, 128), BLOCK)]
        copies = shard_copies(table, shards, place, slice(0, BLOCK), sems)
        copies += piece_copies(table, pieces, around, piece_sems)
        for copy in copies:
            copy.start()
        for copy in copies:
            copy.wait()

    keep = table[KEEP + 2 * k + table[SIDE]].astype(F32)
    tok_ref[...] = around[k, 0:Q, :]
    ext[0:16, :] = around[table[PREV + k], Q:, :]
    tail_ref[...] = ext[0:16, :]
    ext[16:, :] = around[k, 0:Q, :]
    tok = ext[...]
    dt = jnp.zeros((Q, 128), F32)
    for i in range(2):
        proj = mm(tok, w_ref[:, BLOCK * i : BLOCK * (i + 1)])
        for to, size, at in ((half * i, half, 0), (width + NS * i, NS, half)):
            buf[0:8, to : to + size] = proj[8:16, at : at + size] * keep
            buf[8:, to : to + size] = proj[16:, at : at + size]
        dt = dt + proj[16:, half + NS :]
    pre_ref[...] = buf[8:, :].astype(BF)
    before_ref[...] = buf[0:8, :]
    run = conv_run(conv_ref, buf)
    sg = sigmoid(run)
    act = (run * sg).astype(BF)
    slope_ref[...] = (sg * (1.0 + run * (1.0 - sg))).astype(BF)
    act_ref[...] = act
    z = dt + head_ref[0:1, :]
    z_ref[...] = z
    step = softplus(z)
    cum = running_sum(tri_ref[...], step * head_ref[1:2, :])
    cum_ref[...] = cum
    ones = ones_ref[...]
    weigh = spread(step * jnp.exp(cum[Q - 1 :, :] - cum), ones)
    grown = (act[:, :width].astype(F32) * weigh).astype(BF)
    state_ref[0:NS, :] = mm_tn(act[:, width : width + NS], grown).astype(BF)
    last = spread(jnp.broadcast_to(jnp.exp(cum[Q - 1 :, :]), (16, 128)), ones)
    hi, low = split2(last)
    sub = lax.broadcasted_iota(jnp.int32, last.shape, 0)
    state_ref[NS:, :] = jnp.where(sub == 0, hi.astype(F32), low.astype(F32)).astype(BF)


BLOCK = 640


def front(table, shards, pieces, conv, head, ones, tri):
    rows, d = pieces[0].shape
    width = ones.shape[1]
    cols = width + 2 * NS
    return call(
        front_kernel, "conv_and_states", 4, table,
        [
            *[(a, None, None) for a in (*shards, *pieces)],
            all_of(conv), all_of(head), all_of(ones), all_of(tri),
        ],
        [
            out_all((d, 2 * BLOCK), BF), out_rows(4, d, BF), out_rows(4, d, BF, 16),
            out_rows(4, cols, BF), out_rows(4, cols, F32, 8), out_rows(4, cols, BF), out_rows(4, cols, BF),
            out_rows(4, 128, F32), out_rows(4, 128, F32), out_rows(4, width, BF, STATE_ROWS),
        ],
        [
            pltpu.VMEM((4, rows, d), BF), pltpu.VMEM((rows, d), BF), pltpu.VMEM((8 + Q, cols), F32),
            pltpu.SemaphoreType.DMA((32,)), pltpu.SemaphoreType.DMA((4,)),
        ],
    )


def within_kernel(table, act_ref, z_ref, cum_ref, chan_ref, ones_ref, mixed_ref):
    width = ones_ref.shape[1]
    act = act_ref[...]
    cum = cum_ref[...]
    x = act[:, :width].astype(F32)
    xs = x * spread(softplus(z_ref[...]), ones_ref[...])
    scores = mm_nt(act[:, width + NS :], act[:, width : width + NS])
    cum_row = cum.T
    lower = lower_ones()
    half = lanes((Q, 128)) < HD
    for p in range(width // 128):
        span = slice(128 * p, 128 * (p + 1))
        xp = xs[:, span]
        total = chan_ref[0:1, span] * x[:, span]
        for i in range(2):
            h = 2 * p + i
            diff = cum[:, h : h + 1] - cum_row[h : h + 1, :]
            mix = (scores * jnp.exp(jnp.where(lower, diff, -1e30))).astype(BF)
            total = total + mm(mix, jnp.where(half if i == 0 else ~half, xp, 0.0).astype(BF))
        mixed_ref[:, span] = total


def project_kernel(table, *refs):
    shards, pieces, refs = refs[:10], refs[10:15], refs[15:]
    tok_ref, wz_ref, wout_ref, cot_ref, gate_ref, hg_ref, around, sems, sems2, piece_sems = refs
    k = pl.program_id(0)
    width = gate_ref.shape[1]
    half = width // 2

    def copies(to_ref, at, sems):
        place = lambda side, rows: to_ref.at[rows, pl.ds(pl.multiple_of(side * half, 128), half)]
        return shard_copies(table, shards, place, slice(at, at + half), sems)

    @pl.when(k == 0)
    def _():
        all_copies = copies(wz_ref, BLOCK, sems) + copies(wout_ref, BLOCK + half, sems2)
        all_copies += piece_copies(table, pieces, around, piece_sems)
        for copy in all_copies:
            copy.start()
        for copy in all_copies:
            copy.wait()

    gate_ref[...] = mm(tok_ref[...], wz_ref[...]).astype(BF)
    cot = around[k]
    cot_ref[...] = cot
    live = lax.broadcasted_iota(jnp.int32, (Q, width), 0) < table[LIVE + k]
    hg_ref[...] = jnp.where(live, mm(cot, wout_ref[...]), 0.0).astype(BF)


def project(table, shards, pieces, tokens):
    rows, d = pieces[0].shape
    width = shards[0].shape[2] - BLOCK
    return call(
        project_kernel, "project", 4, table,
        [*[(a, None, None) for a in (*shards, *pieces)], rows_of(tokens)],
        [
            out_all((d, width), BF), out_all((d, width), BF), out_rows(4, d, BF),
            out_rows(4, width, BF), out_rows(4, width, BF),
        ],
        [
            pltpu.VMEM((4, rows, d), BF), pltpu.SemaphoreType.DMA((32,)), pltpu.SemaphoreType.DMA((32,)),
            pltpu.SemaphoreType.DMA((5,)),
        ],
    )


def within(table, act, z, cum, chan, ones):
    return call(
        within_kernel, "ssd_within", 4, table,
        [rows_of(act), rows_of(z), rows_of(cum), all_of(chan), all_of(ones)],
        [out_rows(4, ones.shape[1], F32)],
    )[0]


def decay_of(state_ref):
    rows = state_ref[NS : NS + 8, :].astype(F32)
    return rows[0:1, :] + rows[1:2, :]


def through_kernel(
    table, within_ref, gate_ref, hg_ref, act_ref, cum_ref, own_ref, pair_ref, chan_ref, ones_ref,
    mixed_ref, sin_ref, sums_ref,
    state,
):
    k = pl.program_id(0)
    width = ones_ref.shape[1]
    first = table[SIDE] == 0

    @pl.when(k == 0)
    def _():
        state[...] = jnp.zeros_like(state)

    own, pair = own_ref[0:NS, :].astype(F32), pair_ref[0:NS, :].astype(F32)
    own_decay, pair_decay = decay_of(own_ref), decay_of(pair_ref)
    at_a = table[KEEP + 2 * k].astype(F32) * state[...]
    after_a = jnp.where(first, own_decay, pair_decay) * at_a + jnp.where(first, own, pair)
    at_b = table[KEEP + 2 * k + 1].astype(F32) * after_a
    state[...] = jnp.where(first, pair_decay, own_decay) * at_b + jnp.where(first, pair, own)
    carried = jnp.where(first, at_a, at_b).astype(BF)
    sin_ref[...] = carried

    grow = spread(jnp.exp(cum_ref[...]), ones_ref[...])
    mixed = within_ref[...] + mm(act_ref[...], carried) * grow
    mixed_ref[...] = mixed.astype(BF)
    gate = up(gate_ref[...])
    gated = mixed * (gate * sigmoid(gate))
    one = jnp.ones((8, width), BF)
    square = sum(mm_nt(one, part) for part in split2(gated * gated))
    inner = sum(mm_nt(one, part) for part in split2(up(hg_ref[...]) * chan_ref[1:2, :] * gated))
    sub = lax.broadcasted_iota(jnp.int32, (8, Q), 0)
    sums_ref[...] = jnp.where(sub == 0, square, inner)


def c_rows(act):
    return act, (Q, NS), lambda k, table: (k, act.shape[1] // NS - 1)


def through(table, mixed, gate, hg, act, cum, own, pair, chan, ones):
    width = ones.shape[1]
    return call(
        through_kernel, "ssd_through", 4, table,
        [
            rows_of(mixed), rows_of(gate), rows_of(hg), c_rows(act), rows_of(cum),
            rows_of(own, STATE_ROWS), rows_of(pair, STATE_ROWS), all_of(chan), all_of(ones),
        ],
        [
            out_rows(4, width, BF), out_rows(4, width, BF, NS),
            ((8, 4 * Q), F32, (8, Q), lambda k, table: (0, k)),
        ],
        [pltpu.VMEM((NS, width), F32)],
    )


def gate_back_kernel(
    table, hg_ref, mixed_ref, gate_ref, sums_ref, sums1, sums2, sums3, act_ref, cum_ref, chan_ref, ones_ref,
    hidden_ref, glow_ref, dy_ref, dstate_ref, ngg_ref, *, inner,
):
    k = pl.program_id(0)
    width = ones_ref.shape[1]

    @pl.when(k == 0)
    def _():
        ngg_ref[...] = jnp.zeros_like(ngg_ref)

    sums = (sums_ref[...] + sums1[...]) + (sums2[...] + sums3[...])
    scale_row = lax.rsqrt(sums[0:1, :] / inner + EPS)
    pull_row = scale_row * scale_row * scale_row * (sums[1:2, :] / inner)
    sub = lax.broadcasted_iota(jnp.int32, (128, Q), 0)
    cols = jnp.where(sub == 0, scale_row, jnp.where(sub == 1, pull_row, 0.0)).T
    scale = cols[:, 0:1]
    pull = cols[:, 1:2]
    hg = up(hg_ref[...])
    mixed = up(mixed_ref[...])
    gate = up(gate_ref[...])
    sg = sigmoid(gate)
    silu = gate * sg
    gated = mixed * silu
    normal = gated * scale
    gain = chan_ref[1:2, :]
    row = lax.broadcasted_iota(jnp.int32, (Q, width), 0)
    hidden_ref[...] = jnp.where(row < table[LIVE + k], normal * gain, 0.0).astype(BF)
    ngg_ref[0:1, :] += jnp.sum(hg * normal, axis=0, keepdims=True)
    gg = scale * gain * hg - gated * pull
    dy = gg * silu
    dy_ref[...] = dy
    glow_ref[...] = (gg * mixed * sg * (1.0 + gate * (1.0 - sg))).astype(BF)
    grow = spread(jnp.exp(cum_ref[...]), ones_ref[...])
    dstate_ref[...] = mm_tn(act_ref[...], (dy * grow).astype(BF)).astype(BF)


def gate_back(table, hg, mixed, gate, sums, act, cum, chan, ones, inner):
    width = ones.shape[1]
    return call(
        functools.partial(gate_back_kernel, inner=inner), "gate_back", 4, table,
        [
            rows_of(hg), rows_of(mixed), rows_of(gate), *[(a, (8, Q), lambda k, table: (0, k)) for a in sums],
            c_rows(act), rows_of(cum), all_of(chan), all_of(ones),
        ],
        [
            out_rows(4, width, BF), out_rows(4, width, BF), out_rows(4, width, F32), out_rows(4, width, BF, NS),
            out_all((8, width), F32),
        ],
    )


def backward_kernel(
    table, act_ref, pre_ref, before_ref, slope_ref, z_ref, cum_ref, sin_ref, dy_ref, mine_ref, theirs_ref, decay_ref,
    conv_ref, head_ref, chan_ref, ones_ref, tri_ref,
    low_ref, fix_ref, convsum_ref, headsum_ref, skipsum_ref,
    carry, buf, *, heads,
):
    k = 3 - pl.program_id(0)
    width = heads * HD
    cols = width + 2 * NS
    side = table[SIDE]

    @pl.when(pl.program_id(0) == 0)
    def _():
        carry[...] = jnp.zeros_like(carry)
        convsum_ref[...] = jnp.zeros_like(convsum_ref)
        headsum_ref[...] = jnp.zeros_like(headsum_ref)
        skipsum_ref[...] = jnp.zeros_like(skipsum_ref)

    act = act_ref[...]
    x = act[:, :width].astype(F32)
    bmat = act[:, width : width + NS]
    cmat = act[:, width + NS :]
    z = z_ref[...]
    step = softplus(z)
    cum = cum_ref[...]
    ones = ones_ref[...]
    tri = tri_ref[...]
    step_x = spread(step, ones)
    grow_x, fade_x = decays(cum, ones)
    last_x = grow_x[Q - 1 :, :]
    xs = x * step_x
    xsb = xs.astype(BF)
    dy = dy_ref[...]

    mine = mine_ref[...].astype(F32)
    theirs = theirs_ref[...].astype(F32)
    pair_decay = decay_of(decay_ref)
    keep_a = table[KEEP + 2 * k].astype(F32)
    keep_b = table[KEEP + 2 * k + 1].astype(F32)
    after_b = carry[...]
    first = side == 0
    after_a = keep_b * (jnp.where(first, pair_decay, last_x) * after_b + jnp.where(first, theirs, mine))
    carry[...] = keep_a * (jnp.where(first, last_x, pair_decay) * after_a + jnp.where(first, mine, theirs))
    dstate = jnp.where(first, after_a, after_b)
    dstate_low = dstate.astype(BF)

    scores = mm_nt(bmat, cmat)
    cum_row = cum.T
    lane = lanes((Q, 128))
    even = lane < HD
    sub = lax.broadcasted_iota(jnp.int32, (128, Q), 0)
    later_ones = lanes((Q, Q)) >= lax.broadcasted_iota(jnp.int32, (Q, Q), 0)
    dscores = jnp.zeros((Q, Q), F32)
    rowsum = jnp.zeros((128, Q), F32)
    colsum = jnp.zeros((Q, 128), F32)
    parts = []
    for p in range(heads // 2):
        span = slice(128 * p, 128 * (p + 1))
        dyp = dy[:, span]
        part = jnp.zeros((Q, 128), F32)
        for i in range(2):
            h = 2 * p + i
            diff = cum_row[h : h + 1, :] - cum[:, h : h + 1]
            decay = jnp.exp(jnp.where(later_ones, diff, -1e30))
            mix = (scores * decay).astype(BF)
            dym = jnp.where(even if i == 0 else ~even, dyp, 0.0).astype(BF)
            grad = mm_nt(xsb[:, span], dym) * decay
            dscores = dscores + grad
            grad = grad * scores
            colsum = jnp.where(lane == h, jnp.sum(grad, axis=1, keepdims=True), colsum)
            rowsum = jnp.where(sub == h, jnp.sum(grad, axis=0, keepdims=True), rowsum)
            part = part + mm(mix, dym)
        parts.append(part)
    inside = jnp.concatenate(parts, axis=1)
    carried = sin_ref[...]
    dyg = (dy * grow_x).astype(BF)
    dsl = dscores.astype(BF)
    dc = mm_tn(dsl, bmat) + mm_nt(dyg, carried)
    db = mm(dsl, cmat) + mm_nt((xs * fade_x).astype(BF), dstate_low)
    passed = mm(cmat, carried) * grow_x
    later = mm(bmat, dstate_low) * fade_x
    q_passed = gather_heads(dy * passed, ones)
    q_later = gather_heads(x * later, ones)
    q_inside = gather_heads(x * inside, ones)
    hold = jnp.sum(dstate * carried.astype(F32), axis=0, keepdims=True) * last_x
    q_hold = gather_heads(jnp.broadcast_to(hold, (8, width)), ones)[0:1, :]
    dx = step_x * (inside + later) + chan_ref[0:1, :] * dy
    net = jnp.where(lane < LOW, q_passed + rowsum.T - colsum, 0.0)
    push = step * q_later
    drate = suffix_sum(tri, net) + running_sum(tri, push) - push + q_hold
    rate_of = head_ref[1:2, :]
    dstep = q_inside + q_later + drate * rate_of
    dz = jnp.where(lane < heads, dstep * sigmoid(z), 0.0)
    headsum_ref[0:1, :] += jnp.sum(dz, axis=0, keepdims=True)
    headsum_ref[1:2, :] += jnp.sum(drate * step * rate_of, axis=0, keepdims=True)
    skipsum_ref[0:1, :] += jnp.sum(dy * x, axis=0, keepdims=True)

    grad = jnp.concatenate([dx, db, dc], axis=1)
    dact = grad * up(slope_ref[...])
    pre = up(pre_ref[...])
    start = dact[0:8, :]
    ahead = before_ref[...]
    sub = lax.broadcasted_iota(jnp.int32, start.shape, 0)
    convsum_ref[4:5, :] += jnp.sum(dact, axis=0, keepdims=True)
    convsum_ref[3:4, :] += jnp.sum(dact * pre, axis=0, keepdims=True)
    buf[0:Q, :] = dact
    buf[Q : Q + 8, :] = jnp.zeros((8, cols), F32)
    dpre = conv_ref[3:4, :] * dact
    for j in range(1, 4):
        moved = buf[j : j + Q, :]
        dpre = dpre + conv_ref[3 - j : 4 - j, :] * moved
        first_rows = jnp.where(sub >= 8 - j, pltpu.roll(start, 8 - j, 0) * ahead, 0.0)
        convsum_ref[3 - j : 4 - j, :] += jnp.sum(moved * pre, axis=0, keepdims=True) + jnp.sum(
            first_rows, axis=0, keepdims=True
        )
    half = width // 2
    for i in range(2):
        at = BLOCK * i
        low_ref[:, at : at + half] = dpre[:, half * i : half * (i + 1)].astype(BF)
        low_ref[:, at + half : at + half + NS] = dpre[:, width + NS * i : width + NS * (i + 1)].astype(BF)
        low_ref[:, at + half + NS : at + BLOCK] = dz.astype(BF)
    begin = dact[0:8, :] * table[KEEP + 2 * k + side].astype(F32)
    sub = lax.broadcasted_iota(jnp.int32, begin.shape, 0)
    fix = jnp.zeros_like(begin)
    for j in range(1, 4):
        fix = fix + jnp.where(sub >= 8 - j, conv_ref[3 - j : 4 - j, :] * pltpu.roll(begin, 8 - j, 0), 0.0)
    fix = jnp.concatenate([jnp.zeros_like(fix), fix], axis=0)
    for i in range(2):
        at = BLOCK * i
        fix_ref[:, at : at + half] = fix[:, half * i : half * (i + 1)].astype(BF)
        fix_ref[:, at + half : at + half + NS] = fix[:, width + NS * i : width + NS * (i + 1)].astype(BF)
        fix_ref[:, at + half + NS : at + BLOCK] = jnp.zeros((16, 128), BF)


def backward(table, act, pre, before, slope, z, cum, sin, dy, mine, theirs, pair, conv, head, chan, ones, tri, heads):
    cols = act.shape[1]
    width = heads * HD

    def back(array, size=Q):
        return array, (size, array.shape[1]), lambda i, table: (3 - i, 0)

    def out_back(w, dtype, size=Q):
        return (4 * size, w), dtype, (size, w), lambda i, table: (3 - i, 0)

    return call(
        functools.partial(backward_kernel, heads=heads), "ssd_backward", 4, table,
        [
            back(act), back(pre), back(before, 8), back(slope), back(z), back(cum), back(sin, NS), back(dy),
            back(mine, NS), back(theirs, NS), back(pair, STATE_ROWS),
            all_of(conv), all_of(head), all_of(chan), all_of(ones), all_of(tri),
        ],
        [
            out_back(2 * BLOCK, BF), out_back(2 * BLOCK, BF, 16),
            out_all((8, cols), F32), out_all((8, 128), F32), out_all((8, width), F32),
        ],
        [pltpu.VMEM((NS, width), F32), pltpu.VMEM((8 + Q, cols), F32)],
    )


def by_core(grad, first, i, mine_ref, other_ref, cols):
    part = mine_ref.shape[3]
    for p in range(2):
        a = grad[2 * p * part : (2 * p + 1) * part]
        b = grad[(2 * p + 1) * part : (2 * p + 2) * part]
        mine_ref[p, i, 0, :, cols] = jnp.where(first, a, b).astype(BF)
        other_ref[p, i, 0, :, cols] = jnp.where(first, b, a).astype(BF)


def row_dots(grad, w):
    prod = grad * up(w)
    prod = sum(prod[:, at : at + 128] for at in range(0, prod.shape[1], 128))
    one = jnp.ones((8, 128), BF)
    return sum(mm_nt(one, part) for part in split2(prod))


def early_kernel(table, tok_ref, cot_ref, w_ref, glow_ref, hidden_ref, mine_ref, other_ref, dots_ref):
    half = glow_ref.shape[1] // 2
    first = table[CORE] == 0
    for at, left, right in ((0, tok_ref, glow_ref), (half, cot_ref, hidden_ref)):
        grad = mm_tn(left[...], right[...])
        for i in range(2):
            by_core(grad[:, half * i : half * (i + 1)], first, i, mine_ref, other_ref, slice(at, at + half))
        if at == 0:
            dots_ref[...] = row_dots(grad, w_ref[...])


def late_kernel(
    table, tok_ref, tail_ref, w_ref, low_ref, fix_ref, dots_ref, convsum_ref, gain_ref, headsum_ref, skipsum_ref,
    mine_ref, other_ref, small_ref, dots,
):
    i = pl.program_id(0)
    grad = mm_tn(tok_ref[...], low_ref[...]) + mm_tn(tail_ref[...], fix_ref[...])
    for side in range(2):
        by_core(grad[:, BLOCK * side : BLOCK * (side + 1)], table[CORE] == 0, side, mine_ref, other_ref, slice(0, BLOCK))
    dots[i] = row_dots(grad, w_ref[...])

    @pl.when(i == 3)
    def _():
        width = gain_ref.shape[1]
        cols = convsum_ref.shape[1]
        sub = lax.broadcasted_iota(jnp.int32, (8, width), 0)
        other = jnp.where(sub == 5, gain_ref[0:1, :], jnp.where(sub == 6, skipsum_ref[0:1, :], 0.0))
        small_ref[:, :width] = jnp.where(sub < 5, convsum_ref[:, :width], other)
        sub = lax.broadcasted_iota(jnp.int32, (8, 128), 0)
        for h in range(2):
            at = slice(width + 128 * h, width + 128 * (h + 1))
            other = jnp.where(sub == 5, headsum_ref[h : h + 1, :], 0.0)
            small_ref[:, at] = jnp.where(sub < 5, convsum_ref[:, at], other)
        sub = lax.broadcasted_iota(jnp.int32, (8, 256), 0)
        size = dots.shape[2]
        flat = jnp.concatenate([dots[q] + dots_ref[:, size * q : size * (q + 1)] for q in range(4)], axis=1)
        rows = jnp.zeros((8, 256), F32)
        for r in range(flat.shape[1] // 256):
            rows = jnp.where(sub == r, flat[:, 256 * r : 256 * (r + 1)], rows)
        small_ref[:, cols:] = rows


def shard_outs(d, cols):
    part = d // 16
    out = ((4, 2, 2, part, cols), BF, (2, 2, 1, part, cols), lambda i, table: (i % 2, 0, i // 2, 0, 0))
    return [out, out]


def early_weights(table, tokens, cot, wz, glow, hidden):
    rows, d = tokens.shape
    width = glow.shape[1]
    columns = lambda a: (a, (rows, d // 4), lambda i, table: (0, i))
    return call(
        early_kernel, "early_weights", 4, table,
        [
            columns(tokens), columns(cot), (wz, (d // 4, width), lambda i, table: (i, 0)),
            all_of(glow), all_of(hidden),
        ],
        [*shard_outs(d, width), ((8, d), F32, (8, d // 4), lambda i, table: (0, i))],
    )


def late_weights(table, tokens, tails, wx, low, fix, dots, conv_sum, gain_sum, head_sum, skip_sum):
    rows, d = tokens.shape
    return call(
        late_kernel, "late_weights", 4, table,
        [
            (tokens, (rows, d // 4), lambda i, table: (0, i)),
            (tails, (tails.shape[0], d // 4), lambda i, table: (0, i)),
            (wx, (d // 4, 2 * BLOCK), lambda i, table: (i, 0)),
            all_of(low), all_of(fix), all_of(dots), all_of(conv_sum), all_of(gain_sum), all_of(head_sum), all_of(skip_sum),
        ],
        [*shard_outs(d, BLOCK), out_all((8, 2 * BLOCK), F32)],
        [pltpu.VMEM((4, 8, d // 4), F32)],
    )


def in_order(values, place):
    def at(i):
        hop = lax.rem(i + 4 - place, 4)
        return jnp.where(hop == 0, values[0], jnp.where(hop == 1, values[1], jnp.where(hop == 2, values[2], values[3])))

    return (at(0) + at(1)) + (at(2) + at(3))


def x_pack_kernel(table, mine_ref, other_ref, small_ref, small2_ref, far_ref, ahead_ref, behind_ref, own_ref, parts_ref):
    part = mine_ref.shape[3]
    total = small_ref[...] + small2_ref[...]
    parts = [jnp.concatenate([p[:, :BLOCK], p[:, BLOCK:]], axis=0) for p in (up(v) for v in split2(total))]
    parts = jnp.concatenate(parts, axis=0).astype(BF)
    parts_ref[...] = parts
    for hop, out in ((2, far_ref), (1, ahead_ref), (3, behind_ref), (0, own_ref)):
        i = lax.rem(table[EXE] + hop, 4)
        for y in range(4):
            v = up(mine_ref[i, y // 2, y % 2]) + up(other_ref[i, y // 2, y % 2])
            out[part * y : part * (y + 1), :] = v.astype(BF)
        if hop:
            out[4 * part :, :] = parts


def x_pack(table, mine, other, small, small2):
    part = mine.shape[3]
    rows = 4 * part
    return call(
        x_pack_kernel, "x_pack", 1, table,
        [all_of(mine), all_of(other), all_of(small), all_of(small2)],
        [
            *[out_all((rows + 32, BLOCK), BF) for _ in range(3)],
            out_all((rows, BLOCK), BF), out_all((32, BLOCK), BF),
        ],
    )


def y_pack_kernel(
    table, own_ref, far_ref, back_ref, on_ref, parts_ref, early,
    one_ref, two_ref, three_ref, stay_ref, small_ref, late,
):
    part = stay_ref.shape[0]
    rows = 4 * part
    late[...] = up(own_ref[...]) + sum(up(v[0:rows, :]) for v in (far_ref, back_ref, on_ref))
    joined = lambda v, at: up(v[at : at + 16, :]) + up(v[at + 16 : at + 32, :])
    small = in_order(
        [joined(parts_ref, 0), joined(on_ref, rows), joined(far_ref, rows), joined(back_ref, rows)], table[EXE]
    )
    hi, low = split2(small)
    small_ref[:, :BLOCK] = hi
    small_ref[:, BLOCK:] = low
    half = BLOCK - NS - 128
    for hop, out in ((2, two_ref), (1, one_ref), (3, three_ref), (0, stay_ref)):
        to = pl.multiple_of(lax.rem(table[WYE] + hop, 4) * part, part)
        pair = pl.multiple_of(lax.rem(table[WYE] + hop + 2, 4) * part, part)
        out[0:part, :BLOCK] = late[pl.ds(to, part), :].astype(out.dtype)
        out[0:part, BLOCK : BLOCK + NS] = late[pl.ds(pair, part), half : half + NS].astype(out.dtype)
        out[0:part, BLOCK + NS :] = early[pl.ds(to, part), :].astype(out.dtype)
        if hop:
            out[part:, :BLOCK] = hi
            out[part:, BLOCK : 2 * BLOCK] = low
            out[part:, 2 * BLOCK :] = jnp.zeros((16, out.shape[1] - 2 * BLOCK), BF)


def y_pack(table, own, got, parts, early):
    rows = own.shape[0]
    part = rows // 4
    wide = BLOCK + NS + early.shape[1]
    return call(
        y_pack_kernel, "y_pack", 1, table,
        [all_of(a) for a in (own, *got, parts, early)],
        [
            *[out_all((part + 16, wide), BF) for _ in range(3)],
            out_all((part, wide), F32), out_all((16, 2 * BLOCK), BF),
        ],
        [pltpu.VMEM((rows, BLOCK), F32)],
    )


def z_pack_kernel(
    table, stay_ref, one_ref, two_ref, three_ref, small_ref,
    x_ref, dt_ref, z_ref, out_ref, share_ref, taps_ref, offset_ref, gain_ref, skip_ref, bias_ref, rate_ref,
):
    part = stay_ref.shape[0]
    half = x_ref.shape[1]
    got = one_ref, two_ref, three_ref
    total = stay_ref[...] + sum(up(v[0:part, :]) for v in got)
    x_ref[...] = total[:, :half]
    heads = dt_ref.shape[1]
    step = total[:, half + NS : BLOCK]
    dt_ref[...] = jnp.where(table[SIDE] == 0, step[:, :heads], step[:, heads : 2 * heads])
    z_ref[...] = total[:, BLOCK + NS : BLOCK + NS + half]
    out_ref[...] = total[:, BLOCK + NS + half :]
    first = table[SIDE] == 0
    own, pair = total[:, half : half + NS], total[:, BLOCK : BLOCK + NS]
    share_ref[0:part, :NS] = jnp.where(first, own, pair)
    share_ref[0:part, NS:] = jnp.where(first, pair, own)
    joined = lambda v: up(v[:, :BLOCK]) + up(v[:, BLOCK : 2 * BLOCK])
    small = in_order([joined(small_ref[...])] + [joined(v[part:, :]) for v in got], table[WYE])
    rest = 2 * half - BLOCK
    width = jnp.concatenate([small[:8], small[8:, :rest]], axis=1)
    chan = jnp.where(first, width[:, :half], width[:, half:])
    taps_ref[...] = chan[0:4]
    offset_ref[...] = chan[4:5]
    gain_ref[...] = chan[5:6]
    heads = bias_ref.shape[1]
    one = jnp.where(lax.broadcasted_iota(jnp.int32, (128, half), 0) == lanes((128, half)) // HD, 1.0, 0.0).astype(BF)
    skip_ref[...] = sum(mm_nt(part, one) for part in split3(chan))[6:7, :heads]
    for ref, at in ((bias_ref, rest), (rate_ref, rest + 128)):
        row = small[13:14, at : at + 128]
        ref[...] = jnp.where(first, row[:, :heads], row[:, heads : 2 * heads])
    share_ref[part : part + 8, :] = small[8:, rest : rest + 256]
    share_ref[part + 8 :, :] = small[8:, rest + 256 :]


def z_pack(table, stay, got, small):
    part = stay.shape[0]
    half = BLOCK - NS - 128
    out = lambda *shape: out_all(shape, F32)
    return call(
        z_pack_kernel, "z_pack", 1, table,
        [all_of(a) for a in (stay, *got, small)],
        [
            out(part, half), out(part, half // HD), out(part, half), out(part, half), out(part + 16, 256),
            out(4, half), out(1, half), out(1, half), out(1, half // HD), out(1, half // HD), out(1, half // HD),
        ],
    )


def finish_kernel(table, own_ref, on_ref, far_ref, back_ref, gain_ref, bc_ref, taps_ref, offset_ref, ingain_ref):
    part = bc_ref.shape[0]
    total = in_order([v[...] for v in (own_ref, on_ref, far_ref, back_ref)], table[ZED])
    bc_ref[...] = total[:part]
    taps_ref[...] = total[part : part + 4]
    offset_ref[...] = total[part + 4 : part + 5]
    d = gain_ref.shape[1]
    each = ingain_ref.shape[1]
    dots = jnp.concatenate([total[part + 8 + r : part + 9 + r] for r in range(d // 256)], axis=1)
    quotient = jnp.broadcast_to(dots / gain_ref[...], (8, d))
    ingain_ref[...] = pltpu.roll(quotient, lax.rem(d - table[GAIN] * each, d), 1)[0:1, :each]


def finish(table, own, on, far, back, gain):
    width = own.shape[1]
    d = gain.shape[1]
    out = lambda *shape: out_all(shape, F32)
    return call(
        finish_kernel, "finish", 1, table, [all_of(a) for a in (own, on, far, back, gain)],
        [out(own.shape[0] - 16, width), out(4, width), out(1, width), out(1, d // 128)],
    )


def put_one(total, out_refs):
    for n, out_ref in enumerate(out_refs):

        @pl.when(pl.program_id(0) == n)
        def _(out_ref=out_ref):
            out_ref[...] = total.astype(BF)


def normed_kernel(order, glow_ref, low_ref, fix_ref, wz_ref, wx_ref, *refs):
    *out_refs, ext = refs
    ext[0:Q, :] = low_ref[...]
    ext[Q:, :] = fix_ref[...]
    total = mm_nt(ext[...], wx_ref[...])
    put_one(jnp.concatenate([total[:Q] + mm_nt(glow_ref[...], wz_ref[...]), total[Q:]], axis=0), out_refs)


def branch_kernel(order, hidden_ref, wout_ref, *out_refs):
    put_one(mm_nt(hidden_ref[...], wout_ref[...]), out_refs)


def picked(a):
    return a, (Q, a.shape[1]), lambda i, order: (order[i], 0)


def normed_part(order, glow, low, fix, wz, wx):
    n = order.shape[0]
    return call(
        normed_kernel, "normed_grad", n, order,
        [picked(glow), picked(low), (fix, (16, fix.shape[1]), lambda i, order: (order[i], 0)), all_of(wz), all_of(wx)],
        [out_all((Q + 16, wx.shape[0]), BF)] * n,
        [pltpu.VMEM((Q + 16, low.shape[1]), BF)],
    )


def branch_part(order, hidden, wout):
    n = order.shape[0]
    return call(
        branch_kernel, "branch", n, order, [picked(hidden), all_of(wout)], [out_all((Q, wout.shape[0]), BF)] * n
    )


DP = ("yl", "x", "core")
RIGHT = [(i, (i + 1) % 4) for i in range(4)]
LEFT = [(i, (i + 3) % 4) for i in range(4)]
NEAR = [(i, i ^ 1) for i in range(4)]
FAR = [(i, i ^ 2) for i in range(4)]
SWAP = [(0, 1), (1, 0)]


def around_y(step):
    place = lambda y: y % 2 * 2 + y // 2
    return [(place(y), place((y + step) % 4)) for y in range(4)]


def pick(array, index, axis):
    return lax.dynamic_index_in_dim(array, index, axis, keepdims=False)


def up(v):
    return v.astype(F32)


def ring_sends(far, ahead, behind, axis):
    return (
        lax.ppermute(far, axis, FAR),
        lax.ppermute(ahead, axis, RIGHT),
        lax.ppermute(behind, axis, LEFT),
    )


def y_sends(shard):
    send = lambda step: lax.ppermute(shard(step), ("yl", "yh"), around_y(step))
    two, one, three = send(2), send(1), send(3)
    return three, two, one


def ring_far(back, on, axis, cut):
    return lax.ppermute(back[:cut], axis, RIGHT), lax.ppermute(on[cut:], axis, LEFT)


def neighbours(v, axis):
    return lax.ppermute(v, axis, RIGHT), lax.ppermute(v, axis, LEFT)


def with_other_core(arrays):
    return (*arrays, *[lax.ppermute(a, "core", SWAP) for a in arrays])


def local(
    x_in,
    cotangent,
    seq_lengths,
    in_gain,
    w_z,
    w_x,
    w_dt,
    w_bc,
    conv_wx,
    conv_bx,
    conv_wbc,
    conv_bbc,
    dt_bias,
    a_log,
    d_skip,
    gnorm_gain,
    w_out,
):
    rows, d = x_in.shape
    own_heads = dt_bias.shape[0]
    heads = 2 * own_heads
    half = own_heads * HD
    width = 2 * half
    cols = width + 2 * NS
    shard = w_z.shape[0]
    yl, x, core, z, yh = (lax.axis_index(a) for a in ("yl", "x", "core", "z", "yh"))
    dp = (yl * 4 + x) * 2 + core
    side = yh == 0

    hops = (0, 3, 1, 2)
    order = lax.optimization_barrier
    x_tail = lax.ppermute(x_in[rows - 16 :], "yh", SWAP)
    own_w, x_tail = order((pack(yh[None], w_x, w_bc, w_dt, w_z, w_out), x_tail))
    resid = x_in.astype(F32)
    inverse = lax.rsqrt(jnp.mean(resid * resid, axis=-1, keepdims=True) + EPS)
    longer = up(jnp.concatenate([x_in, x_tail]))
    longer_inverse = lax.rsqrt(jnp.mean(longer * longer, axis=-1, keepdims=True) + EPS)
    ext = (longer * longer_inverse * in_gain).astype(BF)

    one, two, three = y_sends(lambda step: own_w)
    x_own = jnp.stack([own_w, three, one, two])
    x_near = neighbours(x_own, "x")
    t_near = neighbours(ext, "z")
    x_near, t_near = order((x_near, t_near))
    x_far, t_far = ring_far(*x_near, "x", 2), lax.ppermute(t_near[0], "z", RIGHT)

    seq_lengths, conv_bx, dt_bias, _ = order((seq_lengths, conv_bx, dt_bias, t_near[0]))
    place = jnp.stack([yl, x, core, z, yh, jnp.full((), shard, yh.dtype)]).astype(jnp.int32)
    table = make_table(place, seq_lengths)
    lane_gap = jnp.zeros((LOW - heads,), F32)
    apart = jnp.zeros((own_heads,), F32)

    def by_lane(v):
        v = jnp.where(side, jnp.concatenate([v, apart]), jnp.concatenate([apart, v]))
        return jnp.concatenate([v, lane_gap, v, jnp.zeros((128 - LOW - heads,), F32)])

    params = jnp.stack(
        [conv_wx[0], conv_wx[1], conv_wx[2], conv_wx[3], conv_bx, jnp.repeat(d_skip, HD), gnorm_gain]
        + [jnp.concatenate([by_lane(dt_bias), by_lane(-jnp.exp(a_log)), jnp.zeros((half - 256,), F32)])]
    )
    pair_params = lax.ppermute(params, "yh", SWAP)
    conv, chan, head = prep(table, params, pair_params, conv_wbc, conv_bbc[None])
    ones = expander(heads)
    tri = jnp.asarray(np.tril(np.ones((Q, Q), np.float32)), BF)

    x_far, x_own, x_near, table, conv, chan, head = order((x_far, x_own, x_near, table, conv, chan, head))
    shards = with_other_core((x_own, *x_near, *x_far))
    cot, t_far = order((cotangent, t_far))
    c_near = neighbours(cot, "z")

    wx, tokens, tails, pre, before, slope, act, zs, cum, states = front(
        table, shards, (ext, t_near[1], t_near[0], t_far), conv, head, ones, tri
    )
    pair = lax.ppermute(states, "yh", SWAP)
    act, c_near = order((act, c_near))
    c_far = ring_far(*c_near, "z", 128)
    mixed = within(table, act, zs, cum, chan, ones)
    wz, wout, cot, gate, hg = project(table, shards, (cotangent, c_near[1], c_near[0], *c_far), tokens)
    mixed, sin, sums = through(table, mixed, gate, hg, act, cum, states, pair, chan, ones)
    sums = sums, *ring_sends(sums, sums, sums, "z")
    hidden, gate_low, dy, dstates, gain_sum = gate_back(
        table, hg, mixed, gate, sums, act, cum, chan, ones, 4 * width
    )
    pair_dstates = lax.ppermute(dstates, "yh", SWAP)

    early, early_other, early_dots = early_weights(table, tokens, cot, wz, gate_low, hidden)
    around_z = (z + jnp.array([2, 1, 3, 0], jnp.int32)) % 4
    branch = branch_part(around_z, hidden, wout)
    pair_dstates, early, early_other, branch = order((pair_dstates, early, early_other, branch))
    early_other = lax.ppermute(early_other, "core", SWAP)
    branch_got = ring_sends(*branch[:3], "z")
    early = [
        (up(pick(early, (x + k) % 4, 0)) + up(pick(early_other, (x + k) % 4, 0))).astype(BF).reshape(4 * shard, width)
        for k in (2, 1, 3, 0)
    ]
    dy, early = order((dy, early))
    early_near = lax.ppermute(early[1], "x", RIGHT), lax.ppermute(early[2], "x", LEFT)
    own_live = table[OWN]
    live_rows = jnp.arange(rows, dtype=jnp.int32)[:, None] < own_live

    low, fix, conv_sum, head_sum, skip_sum = backward(
        table, act, pre, before, slope, zs, cum, sin, dy, dstates, pair_dstates, pair,
        conv, head, chan, ones, tri, heads,
    )
    low, branch_got, early_near, early_far = order((low, branch_got, early_near, early[0]))
    early_far = lax.ppermute(early_far, "x", FAR)
    late, late_other, small = late_weights(
        table, tokens, tails, wx, low, fix, early_dots, conv_sum, gain_sum, head_sum, skip_sum
    )
    low, around_z, late_other, small, early_far = order((low, around_z, late_other, small, early_far))
    late_other, small_other = lax.ppermute(late_other, "core", SWAP), lax.ppermute(small, "core", SWAP)
    far = normed_part(around_z[:1], gate_low, low, fix, wz, wx)[0]
    far, late_other, small_other = order((far, late_other, small_other))
    *sends, late, parts = x_pack(table, late, late_other, small, small_other)
    sends, around_z, far = order((sends, around_z, far))
    got = ring_sends(*sends, "x")
    from_far = lax.ppermute(far, "z", FAR)
    around_z, parts = order((around_z, lax.ppermute(parts, "core", SWAP)))
    ahead, behind, own = normed_part(around_z[1:], gate_low, low, fix, wz, wx)
    early = up(early[3]) + up(early_far) + up(early_near[0]) + up(early_near[1])
    branch = up(branch[3]) + sum(up(v) for v in branch_got)
    output = (resid + jnp.where(live_rows, branch, 0.0)).astype(BF)
    got, from_far, ahead, behind, own, early, output = order((got, from_far, ahead, behind, own, early, output))
    one, two, three, stay, small = y_pack(table, late, got, parts, early)
    got = y_sends(lambda step: {1: one, 2: two, 3: three}[step])
    from_ahead, from_behind = lax.ppermute(ahead, "z", RIGHT), lax.ppermute(behind, "z", LEFT)
    from_ahead, from_behind, got = order((from_ahead, from_behind, got))
    normed_grad = up(own) + up(from_far) + up(from_ahead) + up(from_behind)
    before_it = [(t, (t + 7) % 8) for t in range(8)]
    last = lax.ppermute(normed_grad[rows:], ("z", "yh"), before_it)
    normed_grad = jnp.concatenate([normed_grad[: rows - 16], normed_grad[rows - 16 : rows] + last])

    w_x_grad, w_dt_grad, w_z_grad, w_out_grad, shared, taps, offset, gnorm_grad, skip_grad, bias_grad, rate_grad = z_pack(
        table, stay, got, small
    )
    far, back, on = ring_sends(shared, shared, shared, "z")
    normed_grad, _ = order((normed_grad, shared))
    projected = jnp.sum(normed_grad * in_gain * resid, axis=-1, keepdims=True) / d
    x_grad = inverse * in_gain * normed_grad - resid * inverse**3 * projected + up(cotangent)
    far, back, on, x_grad = order((far, back, on, x_grad))
    w_bc_grad, taps_bc, offset_bc, in_gain_grad = finish(table, shared, on, far, back, in_gain[None])
    return (
        output,
        x_grad,
        in_gain_grad.reshape(-1),
        w_z_grad,
        w_x_grad,
        w_dt_grad,
        w_bc_grad,
        taps,
        offset.reshape(-1),
        taps_bc,
        offset_bc.reshape(-1),
        bias_grad.reshape(-1),
        rate_grad.reshape(-1),
        skip_grad.reshape(-1),
        gnorm_grad.reshape(-1),
        w_out_grad,
    )


def solution(mesh):
    grid = Mesh(mesh.devices.reshape(2, 4, 2, 4, 2), DP + ("z", "yh"))
    tensor = ("z", "yh")
    tokens, weight, channels = P(DP + tensor, None), P(DP, tensor), P(tensor)
    return jax.shard_map(
        local,
        mesh=grid,
        in_specs=(
            tokens,
            tokens,
            P(DP, None),
            P(),
            weight,
            weight,
            weight,
            P(DP, None),
            P(None, tensor),
            channels,
            P(),
            P(),
            channels,
            channels,
            channels,
            channels,
            weight,
        ),
        out_specs=(
            tokens,
            tokens,
            P(DP + tensor),
            weight,
            weight,
            weight,
            P(DP, None),
            P(None, tensor),
            channels,
            P(),
            P(),
            channels,
            channels,
            channels,
            channels,
            weight,
        ),
        check_vma=False,
    )
```
